32 devices in a mesh: seq: 2 (over core), head: 4 (over z), dp: 4 (over y, x).
Axes of the slice: x: 2, y: 2, z: 4, core: 2. Of those that a mesh axis runs over, the one named last changes fastest.
Arguments:
- tokens: bfloat16 [4, 256, 4096], P('dp', 'seq', 'head'), may hold values from -6 to 6
- w_qkv: bfloat16 [4096, 3, 512], P(('seq', 'dp'), None, 'head'), may hold values from -0.09375 to 0.09375
- w_lr: bfloat16 [4096, 4], P(None, 'head'), may hold values from -0.1875 to 0.1875
- w_out: bfloat16 [4096, 512], P(('seq', 'dp'), 'head'), may hold values from -0.25 to 0.25
- w1_init: float32 [4, 128, 512], P('head'), may hold values from -0.5 to 0.5
- w2_init: float32 [4, 512, 128], P('head'), may hold values from -0.25 to 0.25
- d_out: bfloat16 [4, 256, 4096], P('dp', 'seq', 'head'), may hold values from -6 to 6
Outputs:
- out: bfloat16 [4, 256, 4096], P('dp', 'seq', 'head')
- d_tokens: bfloat16 [4, 256, 4096], P('dp', 'seq', 'head')
- d_w1_init: float32 [4, 128, 512], P('head', None, ('seq', 'dp'))
- d_w2_init: float32 [4, 512, 128], P('head', ('seq', 'dp'))
The draws below stay inside these ranges and needn't reach their ends.
All inputs are finite; a program needn't handle non-finite values.
Results may differ from the reference program's by a relative error of at most 0.018.
Values may be sent and summed in bfloat16 or wider, within the bound.
No kernel may reach another device: no remote copies, remote signals or barrier semaphores. Data moves between devices by JAX's collectives and lax.ppermute only.
A program may use at most 64 MiB of HBM per device.

```python
import jax
import jax.numpy as jnp
from jax import lax

D = 4096
HD = 128
INNER = 512
MB = 64
HEADS = 4
BATCH = 4
LENGTH = 256


def block_scale(rng, extent, split, least, high):
    def one(axis_at, shards_of):
        steps = jax.random.uniform(jax.random.fold_in(jax.random.fold_in(rng, 6), axis_at), (shards_of,), jnp.float32, least / len(split), high / len(split))
        return jnp.repeat(jnp.exp(steps), extent[axis_at] // shards_of).reshape((-1,) + (1,) * (len(extent) - axis_at - 1))

    factor_of = one(*split[0])
    for cut in split[1:]:
        factor_of = factor_of * one(*cut)
    return factor_of


def gaussian(own_key, shape, scale, bound, shards=(), kind=jnp.bfloat16):
    values = scale * jax.random.normal(own_key, shape, jnp.float32)
    if shards:
        values = values * block_scale(own_key, shape, shards, -0.22, 0.18)
    return jnp.clip(values, -bound, bound).astype(kind)


def setup_inputs(seed: int = 0) -> dict:
    seeds = jax.random.split(jax.random.key(seed), 8)
    tokens = gaussian(seeds[0], (BATCH, LENGTH, D), 1.0, 6.0, ((0, 4), (1, 2), (2, 4)))
    w_qkv = gaussian(seeds[1], (D, 3, HEADS * HD), D ** -0.5, 0.09375, ((0, 8), (2, 4)))
    w_lr = gaussian(seeds[2], (D, HEADS), (D // 4) ** -0.5, 0.1875, ((1, 4),))
    w_out = gaussian(seeds[3], (D, HEADS * HD), (HEADS * HD) ** -0.5, 0.25, ((0, 8), (1, 4)))
    w1_init = gaussian(seeds[4], (HEADS, HD, INNER), HD ** -0.5, 0.5, ((0, 4),), jnp.float32)
    w2_init = gaussian(seeds[5], (HEADS, INNER, HD), INNER ** -0.5, 0.25, ((0, 4),), jnp.float32)
    d_out = gaussian(seeds[6], (BATCH, LENGTH, D), 1.0, 6.0, ((0, 4), (1, 2), (2, 4)))
    return dict(tokens=tokens, w_qkv=w_qkv, w_lr=w_lr, w_out=w_out, w1_init=w1_init, w2_init=w2_init, d_out=d_out)


EPSILON = 1e-06
BASE_RATE = 0.1
GELU_SCALE = 0.7978845608028654
GELU_CUBIC = 0.044715
PRECISE = lax.Precision.HIGHEST
CONTRACT_LAST = (((1,), (1,)), ((), ()))
CONTRACT_FIRST = (((0,), (0,)), ((), ()))

def gelu_value(inputs):
    bend = jnp.tanh(GELU_SCALE * (inputs + GELU_CUBIC * inputs * inputs * inputs))
    return 0.5 * inputs * (1.0 + bend)

def gelu_slope(inputs):
    bend = jnp.tanh(GELU_SCALE * (inputs + GELU_CUBIC * inputs * inputs * inputs))
    return 0.5 * (1.0 + bend) + 0.5 * inputs * (1.0 - bend * bend) * GELU_SCALE * (1.0 + 3.0 * GELU_CUBIC * inputs * inputs)

def float_dot(left, right):
    return jnp.dot(left, right, precision=PRECISE)

def float_dims(left, right, dims):
    return lax.dot_general(left, right, dims, precision=PRECISE)

def norm_rows(inputs):
    centred = inputs - lax.optimization_barrier(jnp.mean(inputs, axis=-1, keepdims=True))
    inv_scale = lax.rsqrt(lax.optimization_barrier(jnp.mean(centred * centred, axis=-1, keepdims=True)) + EPSILON)
    return (centred * inv_scale, inv_scale)

def local_grads(w_first, w_second, key_rows, value_rows):
    pre_first = float_dot(key_rows, w_first)
    hidden = gelu_value(pre_first)
    normed, inv_scale = norm_rows(float_dot(hidden, w_second))
    residual = normed - (value_rows - key_rows)
    grad_second = inv_scale * (residual - lax.optimization_barrier(jnp.mean(residual, axis=-1, keepdims=True)) - normed * lax.optimization_barrier(jnp.mean(residual * normed, axis=-1, keepdims=True)))
    grad_first = float_dims(grad_second, w_second, CONTRACT_LAST) * gelu_slope(pre_first)
    return (hidden, grad_first, grad_second)

def inner_update(w_first, w_second, key_rows, hidden, grad_first, grad_second, rates):
    new_first = w_first - float_dims(key_rows, grad_first * rates[:, None], CONTRACT_FIRST)
    new_second = w_second - float_dims(hidden, grad_second * rates[:, None], CONTRACT_FIRST)
    return (new_first, new_second)

def inner_block(state_carry, block_rows):
    w_first, w_second = state_carry
    queries, key_rows, value_rows, rate_logit = block_rows
    rates = BASE_RATE * jax.nn.sigmoid(rate_logit) / key_rows.shape[1]
    hidden, grad_first, grad_second = local_grads(w_first, w_second, key_rows, value_rows)
    size_block = key_rows.shape[0]
    positions = lax.broadcasted_iota(jnp.int32, (size_block, size_block), 0)
    sources = lax.broadcasted_iota(jnp.int32, (size_block, size_block), 1)
    causal = jnp.where(sources <= positions, rates[None, :], jnp.float32(0.0))
    mix_first = float_dims(queries, key_rows, CONTRACT_LAST) * causal
    pre_query = float_dot(queries, w_first) - float_dot(mix_first, grad_first)
    hidden_query = gelu_value(pre_query)
    mix_second = float_dims(hidden_query, hidden, CONTRACT_LAST) * causal
    normed, unused = norm_rows(float_dot(hidden_query, w_second) - float_dot(mix_second, grad_second))
    new_state = inner_update(w_first, w_second, key_rows, hidden, grad_first, grad_second, rates)
    return (new_state, queries + normed)

def inner_run(w_first, w_second, queries, key_rows, value_rows, rate_logit):
    row_count = queries.shape[0]
    blocks = row_count // MB
    shaped = (queries.reshape(blocks, MB, -1), key_rows.reshape(blocks, MB, -1), value_rows.reshape(blocks, MB, -1), rate_logit.reshape(blocks, MB))
    final_state, outputs = lax.scan(inner_block, (w_first, w_second), shaped)
    return (final_state[0], final_state[1], outputs.reshape(row_count, -1))

def reference(tokens, w_qkv, w_lr, w_out, w1_init, w2_init, d_out):
    flat = tokens.reshape(BATCH * LENGTH, D)
    projected = jnp.dot(flat, w_qkv.reshape(D, 3 * HEADS * HD), preferred_element_type=jnp.float32)
    projected = projected.reshape(BATCH, LENGTH, 3, HEADS, HD)
    rate_logit = jnp.dot(flat, w_lr, preferred_element_type=jnp.float32).reshape(BATCH, LENGTH, HEADS)
    queries = projected[:, :, 0].transpose(0, 2, 1, 3)
    key_rows = projected[:, :, 1].transpose(0, 2, 1, 3)
    value_rows = projected[:, :, 2].transpose(0, 2, 1, 3)
    logits = rate_logit.transpose(0, 2, 1)

    def head_forward(w_first, w_second, query_h, key_h, value_h, logit_h):
        return inner_run(w_first, w_second, query_h, key_h, value_h, logit_h)[2]

    def seq_forward(inputs):
        return jax.vmap(head_forward)(w1_init, w2_init, inputs[0], inputs[1], inputs[2], inputs[3])
    ttt_heads = lax.map(seq_forward, (queries, key_rows, value_rows, logits))
    ttt_out = ttt_heads.astype(jnp.bfloat16)
    head_rows = ttt_out.transpose(1, 0, 2, 3).reshape(HEADS, BATCH * LENGTH, HD)
    out_columns = w_out.reshape(D, HEADS, HD).transpose(1, 0, 2)

    def add_out(running_sum, pieces):
        head_term = lax.dot_general(pieces[0], pieces[1], CONTRACT_LAST, preferred_element_type=jnp.float32)
        rounded = lax.optimization_barrier(head_term.astype(jnp.bfloat16))
        return (running_sum + rounded.astype(jnp.float32), None)
    out_sum, unused = lax.scan(add_out, jnp.zeros((BATCH * LENGTH, D), jnp.float32), (head_rows, out_columns))
    out = out_sum.astype(jnp.bfloat16).reshape(BATCH, LENGTH, D)
    d_flat = d_out.reshape(BATCH * LENGTH, D)
    d_ttt = jnp.dot(d_flat, w_out, preferred_element_type=jnp.float32)
    d_ttt = d_ttt.reshape(BATCH, LENGTH, HEADS, HD).transpose(0, 2, 1, 3)

    def head_backward(w_first, w_second, query_h, key_h, value_h, logit_h, cotangent_h):
        results, pull = jax.vjp(inner_run, w_first, w_second, query_h, key_h, value_h, logit_h)
        return pull((jnp.zeros_like(results[0]), jnp.zeros_like(results[1]), cotangent_h))

    def seq_backward(inputs):
        return jax.vmap(head_backward)(w1_init, w2_init, inputs[0], inputs[1], inputs[2], inputs[3], inputs[4])
    grads = lax.map(seq_backward, (queries, key_rows, value_rows, logits, d_ttt))
    d_w1_init = lax.optimization_barrier(jnp.sum(grads[0], axis=0))
    d_w2_init = lax.optimization_barrier(jnp.sum(grads[1], axis=0))
    d_proj = jnp.stack([grads[2], grads[3], grads[4]], axis=3)
    d_proj = d_proj.transpose(1, 0, 2, 3, 4).reshape(HEADS, BATCH * LENGTH, 3 * HD).astype(jnp.bfloat16)
    d_logit = grads[5].transpose(1, 0, 2).reshape(HEADS, BATCH * LENGTH)
    qkv_heads = w_qkv.reshape(D, 3, HEADS, HD).transpose(2, 0, 1, 3).reshape(HEADS, D, 3 * HD)
    rate_rows = w_lr.transpose(1, 0)

    def add_grad(running_sum, pieces):
        head_term = lax.dot_general(pieces[0], pieces[1], CONTRACT_LAST, preferred_element_type=jnp.float32)
        head_term = head_term + pieces[2][:, None] * pieces[3].astype(jnp.float32)[None, :]
        rounded = lax.optimization_barrier(head_term.astype(jnp.bfloat16))
        return (running_sum + rounded.astype(jnp.float32), None)
    grad_sum, unused = lax.scan(add_grad, jnp.zeros((BATCH * LENGTH, D), jnp.float32), (d_proj, qkv_heads, d_logit, rate_rows))
    d_tokens = grad_sum.astype(jnp.bfloat16).reshape(BATCH, LENGTH, D)
    return (out, d_tokens, d_w1_init, d_w2_init)
```

```python
import functools

import jax
import jax.numpy as jnp
from jax import lax
from jax.experimental import pallas as pl
from jax.experimental.pallas import tpu as pltpu
from jax.sharding import PartitionSpec as P

MB = 64
EPSILON = 1e-06
BASE_RATE = 0.1
GELU_SCALE = 0.7978845608028654
GELU_CUBIC = 0.044715
NN = ((1,), (0,))
NT = ((1,), (1,))
TN = ((0,), (0,))
EXTRA = 16
UNROLL_LIMIT = 8
F32 = jnp.float32
BF16 = jnp.bfloat16


def mm(left, right, dims):
    return lax.dot_general(
        left.astype(BF16), right.astype(BF16), (dims, ((), ())), preferred_element_type=F32
    )


def padded(lines):
    return jnp.concatenate([lines, jnp.zeros_like(lines)], axis=1)


def mean(rows):
    return jnp.mean(rows, axis=-1, keepdims=True)


def gelu_parts(v):
    square = v * v
    bend = jnp.tanh(v * (GELU_SCALE + (GELU_SCALE * GELU_CUBIC) * square))
    half = 0.5 + 0.5 * bend
    slope = GELU_SCALE + (3.0 * GELU_SCALE * GELU_CUBIC) * square
    bell = 0.5 - 0.5 * bend * bend
    lean = bell * slope
    second = 2.0 * lean * (1.0 - v * bend * slope) + (6.0 * GELU_SCALE * GELU_CUBIC) * square * bell
    return v * half, half + v * lean, second


def gelu_two(v):
    square = v * v
    bend = jnp.tanh(v * (GELU_SCALE + (GELU_SCALE * GELU_CUBIC) * square))
    half = 0.5 + 0.5 * bend
    slope = GELU_SCALE + (3.0 * GELU_SCALE * GELU_CUBIC) * square
    return v * half, half + v * ((0.5 - 0.5 * bend * bend) * slope)


def peers_of(array, axis):
    count = lax.axis_size(axis)
    found = [array]
    for step in range(1, count):
        pairs = [((i + step) % count, i) for i in range(count)]
        found.append(lax.ppermute(array, axis, pairs))
    return found


def gathered(array, axis):
    count = lax.axis_size(axis)
    return lax.all_to_all(jnp.broadcast_to(array[None], (count,) + array.shape), axis, 0, 0)


def project_kernel(seqs, dps, share, place_ref, tok_ref, dout_ref, rate_ref, *refs):
    w_refs, out_ref = refs[:seqs], refs[seqs]
    heads = rate_ref.shape[0]
    rows = tok_ref.shape[0]
    depth = tok_ref.shape[1] // share
    hd = w_refs[0].shape[2]
    tok = tok_ref[...]
    zeros = jnp.zeros((EXTRA, 2 * hd), BF16)
    for h in range(heads):
        logit = mm(rate_ref[h], tok, NT)
        high = logit.astype(BF16)
        out_ref[h, rows:, 0:rows] = high
        out_ref[h, rows:, rows : 2 * rows] = (logit - high.astype(F32)).astype(BF16)
        out_ref[h, rows:, 2 * hd :] = zeros
    for j in range(seqs):
        base = lax.rem(place_ref[0] + j, seqs) * (dps // share)
        for group in range(dps // share):
            inner = None
            outer = None
            for r in range(share):
                w = w_refs[j]
                d = group * share + r
                wide = jnp.concatenate(
                    [w[d, c * depth : (c + 1) * depth, :] for c in range(3)], axis=1
                )
                columns = slice(r * depth, (r + 1) * depth)
                part = mm(tok_ref[:, columns], wide, NN)
                back = mm(dout_ref[:, columns], w[d, 3 * depth : 4 * depth, :], NN)
                inner = part if inner is None else inner + part
                outer = back if outer is None else outer + back
            out_ref[base + group, 0:rows, 0 : 3 * hd] = inner.astype(BF16)
            out_ref[base + group, 0:rows, 3 * hd : 4 * hd] = outer.astype(BF16)


def inner_kernel(seqs, place_ref, *refs):
    x_refs = refs[:seqs]
    w1_ref, w2_ref, res_ref, dw_ref = refs[seqs : seqs + 4]
    (
        qs, ks, vs, ds, es, sg, os, lg,
        w1c, w2c, w1b, w2b,
        x2s, g1s, pgs, gfs, xqs, zqs, dx2s, dg1s,
        dys, ns, rs, ss, cs, g2s, dg2s, dks, des,
    ) = refs[seqs + 4 :]
    heads, chunk_rows, width = x_refs[0].shape
    hd = width // 4
    rows = chunk_rows - EXTRA
    blocks = seqs * rows // MB
    per = rows // MB
    place = place_ref[0]

    for j in range(seqs):
        owner = lax.rem(place + j, seqs)
        total = x_refs[j][0].astype(F32)
        for z in range(1, heads):
            total = total + x_refs[j][z].astype(F32)
        at = pl.ds(pl.multiple_of(owner * rows, rows), rows)
        qs[at, :] = total[0:rows, 0:hd]
        ks[at, :] = total[0:rows, hd : 2 * hd]
        vs[at, :] = total[0:rows, 2 * hd : 3 * hd]
        ds[at, :] = total[0:rows, 3 * hd : 4 * hd]
        logit = total[rows : rows + 8, 0:rows] + total[rows : rows + 8, rows : 2 * rows]
        gate = jax.nn.sigmoid(logit)
        scaled = (BASE_RATE / hd) * gate
        for b in range(per):
            es[owner * per + b] = padded(scaled[:, b * MB : (b + 1) * MB])
            sg[owner * per + b] = padded((scaled * (1.0 - gate))[:, b * MB : (b + 1) * MB])

    w1c[...] = w1_ref[...]
    start = w2_ref[...]
    w2c[...] = (start - mean(start)).T

    at_row = lax.broadcasted_iota(jnp.int32, (MB, MB), 0)
    at_col = lax.broadcasted_iota(jnp.int32, (MB, MB), 1)
    causal = at_col <= at_row
    diagonal = at_col == at_row

    def to_column(line):
        return jnp.sum(jnp.where(diagonal, line, 0.0), axis=1, keepdims=True)

    def to_line(column):
        return jnp.sum(jnp.where(diagonal, column, 0.0), axis=0, keepdims=True)

    def at_block(i):
        if isinstance(i, int):
            return slice(i * MB, (i + 1) * MB)
        return pl.ds(pl.multiple_of(i * MB, MB), MB)

    def forward(i):
        at = at_block(i)
        q, k, v, d_o = qs[at, :], ks[at, :], vs[at, :], ds[at, :]
        line = es[i][0:1, 0:MB]
        e = to_column(line)
        mask = jnp.where(causal, line, 0.0)
        w1 = w1c[...].astype(BF16)
        w2 = w2c[...].astype(BF16)
        w1b[i] = w1
        w2b[i] = w2
        kb, qb = k.astype(BF16), q.astype(BF16)
        gap = v - k
        gap = gap - mean(gap)
        both = mm(jnp.concatenate([kb, qb], axis=0), w1, NN)
        x2, g1, gg1 = gelu_parts(both[:MB])
        x2b = x2.astype(BF16)
        c = mm(x2b, w2, NT)
        var = mean(c * c)
        cross = mean(gap * c)
        s = lax.rsqrt(var + EPSILON)
        n = c * s
        cc = var * s * s - s * cross
        r = n - gap
        g2 = s * (r - n * cc)
        g2b = g2.astype(BF16)
        p = mm(g2b, w2, NN)
        g1f = p * g1
        w1c[...] = w1c[...] - mm(k, e * g1f, TN)
        w2c[...] = w2c[...] - mm(e * g2, x2b, TN)
        g1b = g1f.astype(BF16)
        b1 = mm(qb, kb, NT)
        a1 = (b1 * mask).astype(BF16)
        zq = both[MB:] - mm(a1, g1b, NN)
        xq, gq = gelu_two(zq)
        xqb = xq.astype(BF16)
        b2 = mm(xqb, x2b, NT)
        a2 = (b2 * mask).astype(BF16)
        y = mm(xqb, w2, NT) - mm(a2, g2b, NN)
        sq = lax.rsqrt(mean(y * y) + EPSILON)
        nq = y * sq
        os[at, 3 * hd : 4 * hd] = (q + nq).astype(BF16)
        dy = sq * (d_o - mean(d_o) - nq * mean(d_o * nq))
        dyb = dy.astype(BF16)
        da2 = -mm(dyb, g2b, NT)
        db2 = (da2 * mask).astype(BF16)
        dg2s[i] = -mm(a2, dyb, TN)
        dxq = mm(dyb, w2, NN) + mm(db2, x2b, NN)
        dx2s[i] = mm(db2, xqb, TN)
        dzq = (dxq * gq).astype(BF16)
        da1 = -mm(dzq, g1b, NT)
        db1 = (da1 * mask).astype(BF16)
        dg1s[i] = -mm(a1, dzq, TN)
        dq = d_o + mm(dzq, w1, NT) + mm(db1, kb, NN)
        os[at, 0:hd] = dq.astype(BF16)
        dks[i] = mm(db1, qb, TN)
        de = jnp.sum(jnp.where(causal, da2 * b2 + da1 * b1, 0.0), axis=0, keepdims=True)
        des[i] = padded(jnp.broadcast_to(de, (8, MB)))
        x2s[i] = x2b
        g1s[i] = g1
        pgs[i] = p * gg1
        gfs[i] = g1f
        xqs[i] = xqb
        zqs[i] = dzq
        dys[i] = dyb
        ns[i] = n
        rs[i] = r
        ss[i] = jnp.broadcast_to(s, (MB, hd))
        cs[i] = jnp.broadcast_to(cc, (MB, hd))
        g2s[i] = g2

    def backward(i):
        at = at_block(i)
        q, k = qs[at, :], ks[at, :]
        e = to_column(es[i][0:1, 0:MB])
        w1, w2 = w1b[i], w2b[i]
        d1, d2 = w1c[...].astype(BF16), w2c[...].astype(BF16)
        x2b, g1, g1f, g2 = x2s[i], g1s[i], gfs[i], g2s[i]
        n, s, cc = ns[i], ss[i], cs[i]
        dh1 = -mm(k, d1, NN)
        dh2 = -mm(x2b, d2, NT)
        dg1 = dg1s[i] + e * dh1
        dp = (dg1 * g1).astype(BF16)
        dg2 = dg2s[i] + e * dh2 + mm(dp, w2, NT)
        dt = s * dg2
        mt = mean(dt * n)
        dr = dt - mean(dt) - n * mt
        dn = dr - cc * dt - rs[i] * mt
        du = s * (dn - mean(dn) - n * (mean(dn * n) + mean(dg2 * g2)))
        dub = du.astype(BF16)
        mixed = jnp.concatenate([(-e * g2).astype(BF16), dub], axis=1)
        dx2 = dx2s[i] + mm(mixed, jnp.concatenate([d2, w2], axis=0), NN)
        dz1 = (dg1 * pgs[i] + dx2 * g1).astype(BF16)
        mixed = jnp.concatenate([(-e * g1f).astype(BF16), dz1], axis=1)
        dk = dks[i] + dr + mm(mixed, jnp.concatenate([d1, w1], axis=1), NT)
        w1c[...] = w1c[...] + mm(
            jnp.concatenate([q, k], axis=0), jnp.concatenate([zqs[i], dz1], axis=0), TN
        )
        w2c[...] = w2c[...] + mm(
            jnp.concatenate([dys[i].astype(F32), du, g2], axis=0),
            jnp.concatenate([xqs[i], x2b, dp], axis=0),
            TN,
        )
        extra = jnp.sum(g1f * dh1, axis=1, keepdims=True) + jnp.sum(
            g2 * dh2, axis=1, keepdims=True
        )
        line = (des[i][0:1, 0:MB] + to_line(extra)) * sg[i][0:1, 0:MB]
        lg[i] = padded(jnp.broadcast_to(line, (8, MB)))
        os[at, hd : 2 * hd] = dk.astype(BF16)
        os[at, 2 * hd : 3 * hd] = (-dr).astype(BF16)

    def loop(step, order):
        if blocks <= UNROLL_LIMIT:
            for i in range(blocks):
                step(order(i))
        else:
            lax.fori_loop(0, blocks, lambda i, unused: (step(order(i)), unused)[1], 0)

    loop(forward, lambda i: i)
    w1c[...] = jnp.zeros_like(w1c)
    w2c[...] = jnp.zeros_like(w2c)
    loop(backward, lambda i: blocks - 1 - i)

    res_ref[0:rows, :] = os[pl.ds(pl.multiple_of(place * rows, rows), rows), :]
    res_ref[rows:, :] = jnp.zeros((EXTRA, width), BF16)
    first_row = lax.broadcasted_iota(jnp.int32, (EXTRA, rows), 0) == 0
    lines = jnp.concatenate([lg[place * per + b][0:1, 0:MB] for b in range(per)], axis=1)
    lines = jnp.where(first_row, jnp.broadcast_to(lines, (EXTRA, rows)), 0.0)
    high = lines.astype(BF16)
    res_ref[rows:, 0:rows] = high
    res_ref[rows:, rows : 2 * rows] = (lines - high.astype(F32)).astype(BF16)

    dps, part, unused = dw_ref.shape
    full1, full2 = x2t_pair(w1c, w2c)
    own = dps * part
    for j in range(seqs):
        @pl.when(place == j)
        def keep():
            for d in range(dps):
                at = slice(j * own + d * part, j * own + (d + 1) * part)
                dw_ref[d, :, 0:hd] = full1[at]
                dw_ref[d, :, hd : 2 * hd] = full2[at]


def x2t_pair(first, second):
    return first[...].T, second[...].T


def output_kernel(seqs, dps, share, place_ref, got_ref, rate_ref, *refs):
    w_refs, out_ref, dtok_ref = refs[:seqs], refs[seqs], refs[seqs + 1]
    heads, chunk_rows, width = got_ref.shape
    hd = width // 4
    rows = chunk_rows - EXTRA
    depth = rate_ref.shape[2] // share
    lines = jnp.concatenate(
        [got_ref[h, rows:, 0:rows] for h in range(heads)]
        + [got_ref[h, rows:, rows : 2 * rows] for h in range(heads)],
        axis=0,
    )
    spread = jnp.concatenate([rate_ref[h] for h in range(heads)] * 2, axis=0)
    rate_part = mm(lines.astype(F32).T, spread, NN)
    for r in range(share):
        columns = slice(r * depth, (r + 1) * depth)
        total = None
        grad = rate_part[:, columns]
        for j in range(seqs):
            base = lax.rem(place_ref[0] + j, seqs) * (dps // share)
            for group in range(dps // share):
                w = w_refs[j]
                d = group * share + r
                mine = got_ref[base + group, 0:rows, 3 * hd :]
                term = mm(mine, w[d, 3 * depth : 4 * depth, :], NT)
                total = term if total is None else total + term
                wide = jnp.concatenate(
                    [w[d, c * depth : (c + 1) * depth, :] for c in range(3)], axis=1
                )
                mine = got_ref[base + group, 0:rows, 0 : 3 * hd]
                grad = grad + mm(mine, wide, NT)
        out_ref[:, columns] = total.astype(BF16)
        dtok_ref[:, columns] = grad.astype(BF16)


VMEM = pl.BlockSpec(memory_space=pltpu.VMEM)
SMEM = pl.BlockSpec(memory_space=pltpu.SMEM)
PARAMS = pltpu.CompilerParams(vmem_limit_bytes=48 * 1024 * 1024)


def call(kernel, outs, operands, scratch=()):
    return pl.pallas_call(
        kernel,
        out_shape=outs,
        in_specs=[SMEM] + [VMEM] * (len(operands) - 1),
        out_specs=jax.tree.map(lambda unused: VMEM, outs),
        scratch_shapes=list(scratch),
        compiler_params=PARAMS,
    )(*operands)


def body(tokens, w_qkv, w_lr, w_out, w1_init, w2_init, d_out):
    seqs, heads, dps = (lax.axis_size(a) for a in ("seq", "head", "dp"))
    share = seqs * dps // heads
    rows, features = tokens.shape[1:]
    depth, unused, hd = w_qkv.shape
    inner = w1_init.shape[2]
    blocks = seqs * rows // MB
    place = lax.axis_index("seq").astype(jnp.int32)[None]

    packed = jnp.concatenate([w_qkv.transpose(1, 0, 2).reshape(3 * depth, hd), w_out], axis=0)
    pairs = []
    for seq in range(seqs):
        for head in range(heads):
            for dp in range(dps):
                k = seq * dps + dp
                target = head * share + k % share
                to = ((target // dps) * heads + k // share) * dps + target % dps
                pairs.append(((seq * heads + head) * dps + dp, to))
    swapped = lax.ppermute(packed, ("seq", "head", "dp"), pairs)
    weights = peers_of(gathered(swapped, "dp"), "seq")
    rate_rows = jnp.broadcast_to(
        w_lr[:, 0].reshape(heads, 1, features), (heads, EXTRA, features)
    )
    rate_rows = lax.all_to_all(rate_rows, "head", 0, 0)

    chunk = jax.ShapeDtypeStruct((heads, rows + EXTRA, 4 * hd), BF16)
    partial = call(
        functools.partial(project_kernel, seqs, dps, share),
        chunk,
        (place, tokens[0], d_out[0], rate_rows, *weights),
    )
    summands = peers_of(lax.all_to_all(partial, "head", 0, 0), "seq")

    long = seqs * rows
    scratch = (
        [pltpu.VMEM((long, hd), F32)] * 4
        + [pltpu.VMEM((blocks, 8, 2 * MB), F32)] * 2
        + [pltpu.VMEM((long, 4 * hd), BF16), pltpu.VMEM((blocks, 8, 2 * MB), F32)]
        + [pltpu.VMEM((hd, inner), F32)] * 2
        + [pltpu.VMEM((blocks, hd, inner), BF16)] * 2
        + [pltpu.VMEM((blocks, MB, inner), t) for t in (BF16, F32, F32, F32, BF16, BF16, F32, F32)]
        + [pltpu.VMEM((blocks, MB, hd), t) for t in (BF16, F32, F32, F32, F32, F32, F32, F32)]
        + [pltpu.VMEM((blocks, 8, 2 * MB), F32)]
    )
    part = inner // (seqs * dps)
    result, d_inner = call(
        functools.partial(inner_kernel, seqs),
        (
            jax.ShapeDtypeStruct((rows + EXTRA, 4 * hd), BF16),
            jax.ShapeDtypeStruct((dps, part, 2 * hd), F32),
        ),
        (place, *summands, w1_init[0], w2_init[0]),
        scratch,
    )
    got = gathered(result, "head")
    shares = jnp.sum(lax.all_to_all(d_inner, "dp", 0, 0), axis=0)
    out, d_tokens = call(
        functools.partial(output_kernel, seqs, dps, share),
        (
            jax.ShapeDtypeStruct((rows, features), BF16),
            jax.ShapeDtypeStruct((rows, features), BF16),
        ),
        (place, got, rate_rows, *weights),
    )
    return (out[None], d_tokens[None], shares[:, :hd].transpose(1, 0)[None], shares[:, hd:][None])


def solution(mesh):
    placed = (
        P("dp", "seq", "head"),
        P(("seq", "dp"), None, "head"),
        P(None, "head"),
        P(("seq", "dp"), "head"),
        P("head", None, None),
        P("head", None, None),
        P("dp", "seq", "head"),
    )
    return jax.shard_map(
        body,
        mesh=mesh,
        in_specs=placed,
        out_specs=(
            P("dp", "seq", "head"),
            P("dp", "seq", "head"),
            P("head", None, ("seq", "dp")),
            P("head", ("seq", "dp"), None),
        ),
        check_vma=False,
    )
```

```python
import functools

import jax
import jax.numpy as jnp
from jax import lax
from jax.experimental import pallas as pl
from jax.experimental.pallas import tpu as pltpu
from jax.sharding import PartitionSpec as P

MB = 64
EPSILON = 1e-06
BASE_RATE = 0.1
GELU_SCALE = 0.7978845608028654
GELU_CUBIC = 0.044715
NN = ((1,), (0,))
NT = ((1,), (1,))
TN = ((0,), (0,))
EXTRA = 16
UNROLL_LIMIT = 8
F32 = jnp.float32
BF16 = jnp.bfloat16


def mm(left, right, dims):
    return lax.dot_general(
        left.astype(BF16), right.astype(BF16), (dims, ((), ())), preferred_element_type=F32
    )


def padded(lines):
    return jnp.concatenate([lines, jnp.zeros_like(lines)], axis=1)


def mean(rows):
    return jnp.mean(rows, axis=-1, keepdims=True)


def gelu_parts(v):
    square = v * v
    bend = jnp.tanh(v * (GELU_SCALE + (GELU_SCALE * GELU_CUBIC) * square))
    half = 0.5 + 0.5 * bend
    slope = GELU_SCALE + (3.0 * GELU_SCALE * GELU_CUBIC) * square
    bell = 0.5 - 0.5 * bend * bend
    lean = bell * slope
    second = 2.0 * lean * (1.0 - v * bend * slope) + (6.0 * GELU_SCALE * GELU_CUBIC) * square * bell
    return v * half, half + v * lean, second


def gelu_two(v):
    square = v * v
    bend = jnp.tanh(v * (GELU_SCALE + (GELU_SCALE * GELU_CUBIC) * square))
    half = 0.5 + 0.5 * bend
    slope = GELU_SCALE + (3.0 * GELU_SCALE * GELU_CUBIC) * square
    return v * half, half + v * ((0.5 - 0.5 * bend * bend) * slope)


def mate(index, step, count):
    if count & (count - 1) == 0:
        return index ^ step
    return (index + step) % count


def hop(array, axis, step):
    count = lax.axis_size(axis)
    return lax.ppermute(array, axis, [(mate(i, step, count), i) for i in range(count)])


def peers_of(array, axis):
    return [array] + [hop(array, axis, j) for j in range(1, lax.axis_size(axis))]


def sent_to(arrays, axis):
    count = lax.axis_size(axis)
    back = [arrays[0]]
    for j in range(1, count):
        back.append(lax.ppermute(arrays[j], axis, [(i, mate(i, j, count)) for i in range(count)]))
    return back


def in_plane(array, forward):
    if lax.axis_size("dp") == 4:
        near = [array, hop(array, "dp", 1), hop(array, "dp", 2)]
        near.append(hop(near[forward], "dp", 3 - forward) if forward else hop(array, "dp", 3))
    else:
        near = peers_of(array, "dp")
    columns = [peers_of(piece, "seq") for piece in near]
    return [list(pieces) for pieces in zip(*columns)]


def owner_of(place_ref, seqs, dps, share, j, d):
    seq, dp = place_ref[0], place_ref[2]
    k = mate(seq, j, seqs) * dps + mate(dp, d, dps)
    return k // share, k % share


def rate_line(block, depth):
    rows = block.astype(F32)
    return jnp.concatenate([rows[i : i + 1, :] for i in range(depth // 128)], axis=1)


def outer_kernel(seqs, heads, dps, share, place_ref, tok_ref, dout_ref, *refs):
    w_refs = refs[: seqs * dps]
    out_refs = refs[seqs * dps : seqs * dps + heads]
    tok_s, dout_s, acc = refs[seqs * dps + heads :]
    rows, features = tok_ref.shape
    depth = features // share
    for r in range(share):
        tok_s[r] = tok_ref[:, r * depth : (r + 1) * depth]
        dout_s[r] = dout_ref[:, r * depth : (r + 1) * depth]
    acc[...] = jnp.zeros_like(acc)
    for j in range(seqs):
        for d in range(dps):
            w = w_refs[j * dps + d]
            h, r = owner_of(place_ref, seqs, dps, share, j, d)
            line = rate_line(w[depth:, :], depth)
            logit = mm(jnp.broadcast_to(line, (EXTRA, depth)), tok_s[r], NT)
            back = mm(dout_s[r], w[0:depth, :], NN)
            acc[h] = acc[h] + jnp.concatenate([back, logit], axis=0)
    first_half = lax.broadcasted_iota(jnp.int32, (EXTRA, rows), 0) < EXTRA // 2
    for j in range(heads):
        total = acc[mate(place_ref[1], j, heads)]
        out_refs[j][0:rows, :] = total[0:rows].astype(BF16)
        logit = total[rows:]
        high = logit.astype(BF16).astype(F32)
        out_refs[j][rows:, :] = jnp.where(first_half, high, logit - high).astype(BF16)


def inner_projection_kernel(seqs, heads, dps, share, place_ref, tok_ref, *refs):
    w_refs = refs[: 2 * seqs * dps]
    out_refs = refs[2 * seqs * dps : 2 * seqs * dps + heads]
    tok_s, acc = refs[2 * seqs * dps + heads :]
    rows, features = tok_ref.shape
    depth = features // share
    half = depth // 2
    for r in range(share):
        tok_s[r] = tok_ref[:, r * depth : (r + 1) * depth]
    acc[...] = jnp.zeros_like(acc)
    for part in range(2):
        for j in range(seqs):
            for d in range(dps):
                w = w_refs[(part * seqs + j) * dps + d]
                h, r = owner_of(place_ref, seqs, dps, share, j, d)
                wide = jnp.concatenate([w[c * half : (c + 1) * half, :] for c in range(3)], axis=1)
                acc[h] = acc[h] + mm(tok_s[r][:, part * half : (part + 1) * half], wide, NN)
    for j in range(heads):
        out_refs[j][...] = acc[mate(place_ref[1], j, heads)].astype(BF16)


def inner_kernel(seqs, dps, place_ref, *refs):
    x_refs, y_refs = refs[:seqs], refs[seqs : 2 * seqs]
    w1_ref, w2_ref, res_ref = refs[2 * seqs : 2 * seqs + 3]
    dw_refs = refs[2 * seqs + 3 : 2 * seqs + 3 + dps]
    (
        qs, ks, vs, ds, es, sg, os, lg,
        w1c, w2c, w1b, w2b,
        x2s, g1s, pgs, gfs, xqs, zqs, dx2s, dg1s,
        dys, ns, rs, ss, cs, g2s, dg2s, dks, des, ws,
    ) = refs[2 * seqs + 3 + dps :]
    rows = x_refs[0].shape[0]
    hd = y_refs[0].shape[1]
    width = 4 * hd
    blocks = seqs * rows // MB
    per = rows // MB
    place = place_ref[0]

    for j in range(seqs):
        owner = mate(place, j, seqs)
        at = pl.ds(pl.multiple_of(owner * rows, rows), rows)
        qs[at, :] = x_refs[j][:, 0:hd]
        ks[at, :] = x_refs[j][:, hd : 2 * hd]
        vs[at, :] = x_refs[j][:, 2 * hd : 3 * hd]
        ds[at, :] = y_refs[j][0:rows, :]
        logit = y_refs[j][rows : rows + 8, :] + y_refs[j][rows + 8 : rows + 16, :]
        gate = jax.nn.sigmoid(logit)
        scaled = (BASE_RATE / hd) * gate
        for b in range(per):
            es[owner * per + b] = padded(scaled[:, b * MB : (b + 1) * MB])
            sg[owner * per + b] = padded((scaled * (1.0 - gate))[:, b * MB : (b + 1) * MB])

    w1c[...] = w1_ref[...]
    start = w2_ref[...]
    w2c[...] = (start - mean(start)).T

    at_row = lax.broadcasted_iota(jnp.int32, (MB, MB), 0)
    at_col = lax.broadcasted_iota(jnp.int32, (MB, MB), 1)
    causal = at_col <= at_row
    diagonal = at_col == at_row

    def to_column(line):
        return jnp.sum(jnp.where(diagonal, line, 0.0), axis=1, keepdims=True)

    def to_line(column):
        return jnp.sum(jnp.where(diagonal, column, 0.0), axis=0, keepdims=True)

    def at_block(i):
        if isinstance(i, int):
            return slice(i * MB, (i + 1) * MB)
        return pl.ds(pl.multiple_of(i * MB, MB), MB)

    def forward(i):
        at = at_block(i)
        q, k, v, d_o = qs[at, :], ks[at, :], vs[at, :], ds[at, :]
        line = es[i][0:1, 0:MB]
        e = to_column(line)
        mask = jnp.where(causal, line, 0.0)
        w1 = w1c[...].astype(BF16)
        w2 = w2c[...].astype(BF16)
        w1b[i] = w1
        w2b[i] = w2
        kb, qb = k.astype(BF16), q.astype(BF16)
        gap = v - k
        gap = gap - mean(gap)
        both = mm(jnp.concatenate([kb, qb], axis=0), w1, NN)
        x2, g1, gg1 = gelu_parts(both[:MB])
        x2b = x2.astype(BF16)
        c = mm(x2b, w2, NT)
        var = mean(c * c)
        cross = mean(gap * c)
        s = lax.rsqrt(var + EPSILON)
        n = c * s
        cc = var * s * s - s * cross
        r = n - gap
        g2 = s * (r - n * cc)
        g2b = g2.astype(BF16)
        p = mm(g2b, w2, NN)
        g1f = p * g1
        w1c[...] = w1c[...] - mm(k, e * g1f, TN)
        w2c[...] = w2c[...] - mm(e * g2, x2b, TN)
        g1b = g1f.astype(BF16)
        b1 = mm(qb, kb, NT)
        a1 = (b1 * mask).astype(BF16)
        zq = both[MB:] - mm(a1, g1b, NN)
        xq, gq = gelu_two(zq)
        xqb = xq.astype(BF16)
        b2 = mm(xqb, x2b, NT)
        a2 = (b2 * mask).astype(BF16)
        y = mm(xqb, w2, NT) - mm(a2, g2b, NN)
        sq = lax.rsqrt(mean(y * y) + EPSILON)
        nq = y * sq
        os[at, 3 * hd : 4 * hd] = (q + nq).astype(BF16)
        dy = sq * (d_o - mean(d_o) - nq * mean(d_o * nq))
        dyb = dy.astype(BF16)
        da2 = -mm(dyb, g2b, NT)
        db2 = (da2 * mask).astype(BF16)
        dg2s[i] = -mm(a2, dyb, TN)
        dxq = mm(dyb, w2, NN) + mm(db2, x2b, NN)
        dx2s[i] = mm(db2, xqb, TN)
        dzq = (dxq * gq).astype(BF16)
        da1 = -mm(dzq, g1b, NT)
        db1 = (da1 * mask).astype(BF16)
        dg1s[i] = -mm(a1, dzq, TN)
        dq = d_o + mm(dzq, w1, NT) + mm(db1, kb, NN)
        os[at, 0:hd] = dq.astype(BF16)
        dks[i] = mm(db1, qb, TN)
        de = jnp.sum(jnp.where(causal, da2 * b2 + da1 * b1, 0.0), axis=0, keepdims=True)
        des[i] = padded(jnp.broadcast_to(de, (8, MB)))
        x2s[i] = x2b
        g1s[i] = g1
        pgs[i] = p * gg1
        gfs[i] = g1f
        xqs[i] = xqb
        zqs[i] = dzq
        dys[i] = dyb
        ns[i] = n
        rs[i] = r
        ss[i] = jnp.broadcast_to(s, (MB, hd))
        cs[i] = jnp.broadcast_to(cc, (MB, hd))
        g2s[i] = g2

    def backward(i):
        at = at_block(i)
        q, k = qs[at, :], ks[at, :]
        e = to_column(es[i][0:1, 0:MB])
        w1, w2 = w1b[i], w2b[i]
        d1, d2 = w1c[...].astype(BF16), w2c[...].astype(BF16)
        x2b, g1, g1f, g2 = x2s[i], g1s[i], gfs[i], g2s[i]
        n, s, cc = ns[i], ss[i], cs[i]
        dh1 = -mm(k, d1, NN)
        dh2 = -mm(x2b, d2, NT)
        dg1 = dg1s[i] + e * dh1
        dp = (dg1 * g1).astype(BF16)
        dg2 = dg2s[i] + e * dh2 + mm(dp, w2, NT)
        dt = s * dg2
        mt = mean(dt * n)
        dr = dt - mean(dt) - n * mt
        dn = dr - cc * dt - rs[i] * mt
        du = s * (dn - mean(dn) - n * (mean(dn * n) + mean(dg2 * g2)))
        dub = du.astype(BF16)
        mixed = jnp.concatenate([(-e * g2).astype(BF16), dub], axis=1)
        dx2 = dx2s[i] + mm(mixed, jnp.concatenate([d2, w2], axis=0), NN)
        dz1 = (dg1 * pgs[i] + dx2 * g1).astype(BF16)
        mixed = jnp.concatenate([(-e * g1f).astype(BF16), dz1], axis=1)
        dk = dks[i] + dr + mm(mixed, jnp.concatenate([d1, w1], axis=1), NT)
        w1c[...] = w1c[...] + mm(
            jnp.concatenate([q, k], axis=0), jnp.concatenate([zqs[i], dz1], axis=0), TN
        )
        w2c[...] = w2c[...] + mm(
            jnp.concatenate([dys[i].astype(F32), du, g2], axis=0),
            jnp.concatenate([xqs[i], x2b, dp], axis=0),
            TN,
        )
        extra = jnp.sum(g1f * dh1, axis=1, keepdims=True) + jnp.sum(
            g2 * dh2, axis=1, keepdims=True
        )
        line = (des[i][0:1, 0:MB] + to_line(extra)) * sg[i][0:1, 0:MB]
        lg[i] = padded(jnp.broadcast_to(line, (8, MB)))
        os[at, hd : 2 * hd] = dk.astype(BF16)
        os[at, 2 * hd : 3 * hd] = (-dr).astype(BF16)

    def loop(step, order):
        if blocks <= UNROLL_LIMIT:
            for i in range(blocks):
                step(order(i))
        else:
            lax.fori_loop(0, blocks, lambda i, unused: (step(order(i)), unused)[1], 0)

    loop(forward, lambda i: i)
    w1c[...] = jnp.zeros_like(w1c)
    w2c[...] = jnp.zeros_like(w2c)
    loop(backward, lambda i: blocks - 1 - i)

    res_ref[0:rows, :] = os[pl.ds(pl.multiple_of(place * rows, rows), rows), :]
    res_ref[rows:, :] = jnp.zeros((EXTRA, width), BF16)
    first_row = lax.broadcasted_iota(jnp.int32, (EXTRA, rows), 0) == 0
    lines = jnp.concatenate([lg[place * per + b][0:1, 0:MB] for b in range(per)], axis=1)
    lines = jnp.where(first_row, jnp.broadcast_to(lines, (EXTRA, rows)), 0.0)
    res_ref[rows:, 0:rows] = lines.astype(BF16)

    part = dw_refs[0].shape[0]
    ws[:, 0:hd] = w1c[...].T
    ws[:, hd : 2 * hd] = w2c[...].T
    for d in range(dps):
        first = (place * dps + mate(place_ref[2], d, dps)) * part
        dw_refs[d][...] = ws[pl.ds(pl.multiple_of(first, part), part), :]


def output_kernel(seqs, heads, dps, share, place_ref, *refs):
    got_refs, refs = refs[:heads], refs[heads:]
    o_refs, w_refs = refs[: seqs * dps], refs[seqs * dps : 3 * seqs * dps]
    out_ref, dtok_ref, got, out_s, grad_s = refs[3 * seqs * dps :]
    hd = o_refs[0].shape[1]
    rows, features = out_ref.shape
    depth = features // share
    half = depth // 2
    for j in range(heads):
        got[mate(place_ref[1], j, heads)] = got_refs[j][...]
    out_s[...] = jnp.zeros_like(out_s)
    grad_s[...] = jnp.zeros_like(grad_s)
    for j in range(seqs):
        for d in range(dps):
            o = o_refs[j * dps + d]
            h, r = owner_of(place_ref, seqs, dps, share, j, d)
            out_s[r] = out_s[r] + mm(got[h, 0:rows, 3 * hd :], o[0:depth, :], NT)
            line = rate_line(o[depth:, :], depth)
            logit = got[h, rows:, 0:rows].astype(F32).T
            grad = [mm(logit, jnp.broadcast_to(line, (EXTRA, depth)), NN)]
            mine = got[h, 0:rows, 0 : 3 * hd]
            halves = []
            for part in range(2):
                w = w_refs[(part * seqs + j) * dps + d]
                wide = jnp.concatenate([w[c * half : (c + 1) * half, :] for c in range(3)], axis=1)
                halves.append(mm(mine, wide, NT))
            grad_s[r] = grad_s[r] + grad[0] + jnp.concatenate(halves, axis=1)
    for r in range(share):
        out_ref[:, r * depth : (r + 1) * depth] = out_s[r].astype(BF16)
        dtok_ref[:, r * depth : (r + 1) * depth] = grad_s[r].astype(BF16)


VMEM = pl.BlockSpec(memory_space=pltpu.VMEM)
SMEM = pl.BlockSpec(memory_space=pltpu.SMEM)
PARAMS = pltpu.CompilerParams(vmem_limit_bytes=48 * 1024 * 1024)


def call(kernel, outs, operands, scratch=()):
    return pl.pallas_call(
        kernel,
        out_shape=outs,
        in_specs=[SMEM] + [VMEM] * (len(operands) - 1),
        out_specs=jax.tree.map(lambda unused: VMEM, outs),
        scratch_shapes=list(scratch),
        compiler_params=PARAMS,
    )(*operands)


def body(tokens, w_qkv, w_lr, w_out, w1_init, w2_init, d_out):
    seqs, heads, dps = (lax.axis_size(a) for a in ("seq", "head", "dp"))
    share = seqs * dps // heads
    rows, features = tokens.shape[1:]
    depth, unused, hd = w_qkv.shape
    inner = w1_init.shape[2]
    blocks = seqs * rows // MB
    place = jnp.stack([lax.axis_index(a).astype(jnp.int32) for a in ("seq", "head", "dp")])
    sizes = (seqs, heads, dps, share)

    pairs = []
    for seq in range(seqs):
        for head in range(heads):
            for dp in range(dps):
                k = seq * dps + dp
                target = head * share + k % share
                to = ((target // dps) * heads + k // share) * dps + target % dps
                pairs.append(((seq * heads + head) * dps + dp, to))

    def swapped(array):
        return lax.ppermute(array, ("seq", "head", "dp"), pairs)

    half = depth // 2
    lines = w_lr[:, 0].reshape(seqs * dps, depth // 128, 128)
    line = lax.dynamic_index_in_dim(
        lines, lax.axis_index("seq") * dps + lax.axis_index("dp"), 0, keepdims=False
    )
    line = jnp.pad(line, ((0, EXTRA - depth // 128), (0, 0)))
    outer_w = swapped(jnp.concatenate([w_out, line], axis=0))
    by_kind = w_qkv.transpose(1, 0, 2)
    first_w = swapped(by_kind[:, :half].reshape(3 * half, hd))
    second = by_kind[:, half:].reshape(3 * half, hd)
    second, first_w, outer_w = lax.optimization_barrier((second, first_w, outer_w))
    second_w = swapped(second)
    outer_ws = sum(in_plane(outer_w, 0), [])
    inner_ws = sum(in_plane(first_w, 1), []) + sum(in_plane(second_w, 2), [])

    def summed(arrays):
        return functools.reduce(lambda a, b: a + b, [a.astype(F32) for a in arrays])

    outer_part = call(
        functools.partial(outer_kernel, *sizes),
        (jax.ShapeDtypeStruct((rows + EXTRA, hd), BF16),) * heads,
        (place, tokens[0], d_out[0], *outer_ws),
        [pltpu.VMEM((share, rows, features // share), BF16)] * 2
        + [pltpu.VMEM((heads, rows + EXTRA, hd), F32)],
    )
    outer_all = peers_of(summed(sent_to(outer_part, "head")), "seq")
    inner_part = call(
        functools.partial(inner_projection_kernel, *sizes),
        (jax.ShapeDtypeStruct((rows, 3 * hd), BF16),) * heads,
        (place, tokens[0], *inner_ws),
        [
            pltpu.VMEM((share, rows, features // share), BF16),
            pltpu.VMEM((heads, rows, 3 * hd), F32),
        ],
    )
    inner_all = peers_of(summed(sent_to(inner_part, "head")), "seq")

    long = seqs * rows
    scratch = (
        [pltpu.VMEM((long, hd), F32)] * 4
        + [pltpu.VMEM((blocks, 8, 2 * MB), F32)] * 2
        + [pltpu.VMEM((long, 4 * hd), BF16), pltpu.VMEM((blocks, 8, 2 * MB), F32)]
        + [pltpu.VMEM((hd, inner), F32)] * 2
        + [pltpu.VMEM((blocks, hd, inner), BF16)] * 2
        + [pltpu.VMEM((blocks, MB, inner), t) for t in (BF16, F32, F32, F32, BF16, BF16, F32, F32)]
        + [pltpu.VMEM((blocks, MB, hd), t) for t in (BF16, F32, F32, F32, F32, F32, F32, F32)]
        + [pltpu.VMEM((blocks, 8, 2 * MB), F32), pltpu.VMEM((inner, 2 * hd), F32)]
    )
    part = inner // (seqs * dps)
    result, *d_inner = call(
        functools.partial(inner_kernel, seqs, dps),
        (jax.ShapeDtypeStruct((rows + EXTRA, 4 * hd), BF16),)
        + (jax.ShapeDtypeStruct((part, 2 * hd), F32),) * dps,
        (place, *inner_all, *outer_all, w1_init[0], w2_init[0]),
        scratch,
    )
    got = peers_of(result, "head")
    shares = summed(sent_to(d_inner, "dp"))
    out, d_tokens = call(
        functools.partial(output_kernel, *sizes),
        (jax.ShapeDtypeStruct((rows, features), BF16),) * 2,
        (place, *got, *outer_ws, *inner_ws),
        [
            pltpu.VMEM((heads, rows + EXTRA, 4 * hd), BF16),
            pltpu.VMEM((share, rows, features // share), F32),
            pltpu.VMEM((share, rows, features // share), F32),
        ],
    )
    return (out[None], d_tokens[None], shares[:, :hd].transpose(1, 0)[None], shares[:, hd:][None])


def solution(mesh):
    placed = (
        P("dp", "seq", "head"),
        P(("seq", "dp"), None, "head"),
        P(None, "head"),
        P(("seq", "dp"), "head"),
        P("head", None, None),
        P("head", None, None),
        P("dp", "seq", "head"),
    )
    return jax.shard_map(
        body,
        mesh=mesh,
        in_specs=placed,
        out_specs=(
            P("dp", "seq", "head"),
            P("dp", "seq", "head"),
            P("head", None, ("seq", "dp")),
            P("head", ("seq", "dp"), None),
        ),
        check_vma=False,
    )
```

```python
import functools

import jax
import jax.numpy as jnp
from jax import lax
from jax.experimental import pallas as pl
from jax.experimental.pallas import tpu as pltpu
from jax.sharding import PartitionSpec as P

MB = 64
EPSILON = 1e-06
BASE_RATE = 0.1
GELU_SCALE = 0.7978845608028654
GELU_CUBIC = 0.044715
NN = ((1,), (0,))
NT = ((1,), (1,))
TN = ((0,), (0,))
EXTRA = 16
UNROLL_LIMIT = 8
F32 = jnp.float32
BF16 = jnp.bfloat16


def mm(left, right, dims):
    return lax.dot_general(
        left.astype(BF16), right.astype(BF16), (dims, ((), ())), preferred_element_type=F32
    )


def padded(lines):
    return jnp.concatenate([lines, jnp.zeros_like(lines)], axis=1)


def mean(rows):
    return jnp.mean(rows, axis=-1, keepdims=True)


def gelu_parts(v):
    square = v * v
    bend = jnp.tanh(v * (GELU_SCALE + (GELU_SCALE * GELU_CUBIC) * square))
    half = 0.5 + 0.5 * bend
    slope = GELU_SCALE + (3.0 * GELU_SCALE * GELU_CUBIC) * square
    bell = 0.5 - 0.5 * bend * bend
    lean = bell * slope
    second = 2.0 * lean * (1.0 - v * bend * slope) + (6.0 * GELU_SCALE * GELU_CUBIC) * square * bell
    return v * half, half + v * lean, second


def gelu_two(v):
    square = v * v
    bend = jnp.tanh(v * (GELU_SCALE + (GELU_SCALE * GELU_CUBIC) * square))
    half = 0.5 + 0.5 * bend
    slope = GELU_SCALE + (3.0 * GELU_SCALE * GELU_CUBIC) * square
    return v * half, half + v * ((0.5 - 0.5 * bend * bend) * slope)


def mate(index, step, count):
    if count & (count - 1) == 0:
        return index ^ step
    return (index + step) % count


def hop(array, axis, step):
    count = lax.axis_size(axis)
    return lax.ppermute(array, axis, [(mate(i, step, count), i) for i in range(count)])


def peers_of(array, axis):
    return [array] + [hop(array, axis, j) for j in range(1, lax.axis_size(axis))]


def sent_to(arrays, axis):
    count = lax.axis_size(axis)
    back = [arrays[0]]
    for j in range(1, count):
        back.append(lax.ppermute(arrays[j], axis, [(i, mate(i, j, count)) for i in range(count)]))
    return back


def in_plane(array, forward):
    if lax.axis_size("dp") == 4:
        near = [array, hop(array, "dp", 1), hop(array, "dp", 2)]
        near.append(hop(near[forward], "dp", 3 - forward) if forward else hop(array, "dp", 3))
    else:
        near = peers_of(array, "dp")
    columns = [peers_of(piece, "seq") for piece in near]
    return [list(pieces) for pieces in zip(*columns)]


def owner_of(place_ref, seqs, dps, share, j, d):
    seq, dp = place_ref[0], place_ref[2]
    k = mate(seq, j, seqs) * dps + mate(dp, d, dps)
    return k // share, k % share


def rate_line(block, depth):
    rows = block.astype(F32)
    return jnp.concatenate([rows[i : i + 1, :] for i in range(depth // 128)], axis=1)


def outer_kernel(seqs, heads, dps, share, place_ref, dout_ref, *refs):
    w_refs = refs[: seqs * dps]
    out_refs = refs[seqs * dps : seqs * dps + heads]
    dout_s, acc = refs[seqs * dps + heads :]
    rows, features = dout_ref.shape
    depth = features // share
    for r in range(share):
        dout_s[r] = dout_ref[:, r * depth : (r + 1) * depth]
    acc[...] = jnp.zeros_like(acc)
    for j in range(seqs):
        for d in range(dps):
            h, r = owner_of(place_ref, seqs, dps, share, j, d)
            acc[h] = acc[h] + mm(dout_s[r], w_refs[j * dps + d][0:depth, :], NN)
    for j in range(heads):
        out_refs[j][...] = acc[mate(place_ref[1], j, heads)].astype(BF16)


def projection_kernel(seqs, heads, dps, share, place_ref, *refs):
    tok_refs, refs = refs[:heads], refs[heads:]
    w_refs, rate_ref, out_ref, tok_s = refs[: seqs * dps], *refs[seqs * dps :]
    rows, features = tok_refs[0].shape
    depth = features // share
    for j in range(heads):
        h = mate(place_ref[1], j, heads)
        for r in range(share):
            tok_s[h * share + r] = tok_refs[j][:, r * depth : (r + 1) * depth]
    total = None
    logit = None
    for j in range(seqs):
        for d in range(dps):
            w = w_refs[j * dps + d]
            h, r = owner_of(place_ref, seqs, dps, share, j, d)
            k = h * share + r
            tok = tok_s[k]
            wide = jnp.concatenate([w[c * depth : (c + 1) * depth, :] for c in range(3)], axis=1)
            term = mm(tok, wide, NN)
            line = mm(jnp.broadcast_to(rate_line(rate_ref[k], depth), (EXTRA, depth)), tok, NT)
            total = term if total is None else total + term
            logit = line if logit is None else logit + line
    out_ref[0:rows, :] = total
    out_ref[rows:, :] = jnp.concatenate([logit[0:8]] * (total.shape[1] // rows), axis=1)


def inner_kernel(seqs, dps, place_ref, *refs):
    x_refs, y_refs = refs[:seqs], refs[seqs : 2 * seqs]
    w1_ref, w2_ref, res_ref = refs[2 * seqs : 2 * seqs + 3]
    dw_refs = refs[2 * seqs + 3 : 2 * seqs + 3 + dps]
    (
        qs, ks, vs, ds, es, sg, os, lg,
        w1c, w2c, w1b, w2b,
        x2s, g1s, pgs, gfs, xqs, zqs, dx2s, dg1s,
        dys, ns, rs, ss, cs, g2s, dg2s, dks, des, ws,
    ) = refs[2 * seqs + 3 + dps :]
    rows = y_refs[0].shape[0]
    hd = y_refs[0].shape[1]
    width = 4 * hd
    blocks = seqs * rows // MB
    per = rows // MB
    place = place_ref[0]

    for j in range(seqs):
        owner = mate(place, j, seqs)
        at = pl.ds(pl.multiple_of(owner * rows, rows), rows)
        qs[at, :] = x_refs[j][0:rows, 0:hd]
        ks[at, :] = x_refs[j][0:rows, hd : 2 * hd]
        vs[at, :] = x_refs[j][0:rows, 2 * hd : 3 * hd]
        ds[at, :] = y_refs[j][...]
        gate = jax.nn.sigmoid(x_refs[j][rows:, 0:rows])
        scaled = (BASE_RATE / hd) * gate
        for b in range(per):
            es[owner * per + b] = padded(scaled[:, b * MB : (b + 1) * MB])
            sg[owner * per + b] = padded((scaled * (1.0 - gate))[:, b * MB : (b + 1) * MB])

    w1c[...] = w1_ref[...]
    start = w2_ref[...]
    w2c[...] = (start - mean(start)).T

    at_row = lax.broadcasted_iota(jnp.int32, (MB, MB), 0)
    at_col = lax.broadcasted_iota(jnp.int32, (MB, MB), 1)
    causal = at_col <= at_row
    diagonal = at_col == at_row

    def to_column(line):
        return jnp.sum(jnp.where(diagonal, line, 0.0), axis=1, keepdims=True)

    def to_line(column):
        return jnp.sum(jnp.where(diagonal, column, 0.0), axis=0, keepdims=True)

    def at_block(i):
        if isinstance(i, int):
            return slice(i * MB, (i + 1) * MB)
        return pl.ds(pl.multiple_of(i * MB, MB), MB)

    def forward(i):
        at = at_block(i)
        q, k, v, d_o = qs[at, :], ks[at, :], vs[at, :], ds[at, :]
        line = es[i][0:1, 0:MB]
        e = to_column(line)
        mask = jnp.where(causal, line, 0.0)
        w1 = w1c[...].astype(BF16)
        w2 = w2c[...].astype(BF16)
        w1b[i] = w1
        w2b[i] = w2
        kb, qb = k.astype(BF16), q.astype(BF16)
        gap = v - k
        gap = gap - mean(gap)
        both = mm(jnp.concatenate([kb, qb], axis=0), w1, NN)
        x2, g1, gg1 = gelu_parts(both[:MB])
        x2b = x2.astype(BF16)
        c = mm(x2b, w2, NT)
        var = mean(c * c)
        cross = mean(gap * c)
        s = lax.rsqrt(var + EPSILON)
        n = c * s
        cc = var * s * s - s * cross
        r = n - gap
        g2 = s * (r - n * cc)
        g2b = g2.astype(BF16)
        p = mm(g2b, w2, NN)
        g1f = p * g1
        w1c[...] = w1c[...] - mm(k, e * g1f, TN)
        w2c[...] = w2c[...] - mm(e * g2, x2b, TN)
        g1b = g1f.astype(BF16)
        b1 = mm(qb, kb, NT)
        a1 = (b1 * mask).astype(BF16)
        zq = both[MB:] - mm(a1, g1b, NN)
        xq, gq = gelu_two(zq)
        xqb = xq.astype(BF16)
        b2 = mm(xqb, x2b, NT)
        a2 = (b2 * mask).astype(BF16)
        y = mm(xqb, w2, NT) - mm(a2, g2b, NN)
        sq = lax.rsqrt(mean(y * y) + EPSILON)
        nq = y * sq
        os[at, 3 * hd : 4 * hd] = (q + nq).astype(BF16)
        dy = sq * (d_o - mean(d_o) - nq * mean(d_o * nq))
        dyb = dy.astype(BF16)
        da2 = -mm(dyb, g2b, NT)
        db2 = (da2 * mask).astype(BF16)
        dg2s[i] = -mm(a2, dyb, TN)
        dxq = mm(dyb, w2, NN) + mm(db2, x2b, NN)
        dx2s[i] = mm(db2, xqb, TN)
        dzq = (dxq * gq).astype(BF16)
        da1 = -mm(dzq, g1b, NT)
        db1 = (da1 * mask).astype(BF16)
        dg1s[i] = -mm(a1, dzq, TN)
        dq = d_o + mm(dzq, w1, NT) + mm(db1, kb, NN)
        os[at, 0:hd] = dq.astype(BF16)
        dks[i] = mm(db1, qb, TN)
        de = jnp.sum(jnp.where(causal, da2 * b2 + da1 * b1, 0.0), axis=0, keepdims=True)
        des[i] = padded(jnp.broadcast_to(de, (8, MB)))
        x2s[i] = x2b
        g1s[i] = g1
        pgs[i] = p * gg1
        gfs[i] = g1f
        xqs[i] = xqb
        zqs[i] = dzq
        dys[i] = dyb
        ns[i] = n
        rs[i] = r
        ss[i] = jnp.broadcast_to(s, (MB, hd))
        cs[i] = jnp.broadcast_to(cc, (MB, hd))
        g2s[i] = g2

    def backward(i):
        at = at_block(i)
        q, k = qs[at, :], ks[at, :]
        e = to_column(es[i][0:1, 0:MB])
        w1, w2 = w1b[i], w2b[i]
        d1, d2 = w1c[...].astype(BF16), w2c[...].astype(BF16)
        x2b, g1, g1f, g2 = x2s[i], g1s[i], gfs[i], g2s[i]
        n, s, cc = ns[i], ss[i], cs[i]
        dh1 = -mm(k, d1, NN)
        dh2 = -mm(x2b, d2, NT)
        dg1 = dg1s[i] + e * dh1
        dp = (dg1 * g1).astype(BF16)
        dg2 = dg2s[i] + e * dh2 + mm(dp, w2, NT)
        dt = s * dg2
        mt = mean(dt * n)
        dr = dt - mean(dt) - n * mt
        dn = dr - cc * dt - rs[i] * mt
        du = s * (dn - mean(dn) - n * (mean(dn * n) + mean(dg2 * g2)))
        dub = du.astype(BF16)
        mixed = jnp.concatenate([(-e * g2).astype(BF16), dub], axis=1)
        dx2 = dx2s[i] + mm(mixed, jnp.concatenate([d2, w2], axis=0), NN)
        dz1 = (dg1 * pgs[i] + dx2 * g1).astype(BF16)
        mixed = jnp.concatenate([(-e * g1f).astype(BF16), dz1], axis=1)
        dk = dks[i] + dr + mm(mixed, jnp.concatenate([d1, w1], axis=1), NT)
        w1c[...] = w1c[...] + mm(
            jnp.concatenate([q, k], axis=0), jnp.concatenate([zqs[i], dz1], axis=0), TN
        )
        w2c[...] = w2c[...] + mm(
            jnp.concatenate([dys[i].astype(F32), du, g2], axis=0),
            jnp.concatenate([xqs[i], x2b, dp], axis=0),
            TN,
        )
        extra = jnp.sum(g1f * dh1, axis=1, keepdims=True) + jnp.sum(
            g2 * dh2, axis=1, keepdims=True
        )
        line = (des[i][0:1, 0:MB] + to_line(extra)) * sg[i][0:1, 0:MB]
        lg[i] = padded(jnp.broadcast_to(line, (8, MB)))
        os[at, hd : 2 * hd] = dk.astype(BF16)
        os[at, 2 * hd : 3 * hd] = (-dr).astype(BF16)

    def loop(step, order):
        if blocks <= UNROLL_LIMIT:
            for i in range(blocks):
                step(order(i))
        else:
            lax.fori_loop(0, blocks, lambda i, unused: (step(order(i)), unused)[1], 0)

    loop(forward, lambda i: i)
    w1c[...] = jnp.zeros_like(w1c)
    w2c[...] = jnp.zeros_like(w2c)
    loop(backward, lambda i: blocks - 1 - i)

    res_ref[0:rows, :] = os[pl.ds(pl.multiple_of(place * rows, rows), rows), :]
    res_ref[rows:, :] = jnp.zeros((EXTRA, width), BF16)
    first_row = lax.broadcasted_iota(jnp.int32, (EXTRA, rows), 0) == 0
    lines = jnp.concatenate([lg[place * per + b][0:1, 0:MB] for b in range(per)], axis=1)
    lines = jnp.where(first_row, jnp.broadcast_to(lines, (EXTRA, rows)), 0.0)
    res_ref[rows:, 0:rows] = lines.astype(BF16)

    part = dw_refs[0].shape[0]
    ws[:, 0:hd] = w1c[...].T
    ws[:, hd : 2 * hd] = w2c[...].T
    for d in range(dps):
        first = (place * dps + mate(place_ref[2], d, dps)) * part
        dw_refs[d][...] = ws[pl.ds(pl.multiple_of(first, part), part), :]


def output_kernel(seqs, heads, dps, share, place_ref, *refs):
    got_refs, refs = refs[:heads], refs[heads:]
    o_refs, w_refs = refs[: seqs * dps], refs[seqs * dps : 3 * seqs * dps]
    out_ref, dtok_ref, got, out_s, grad_s = refs[3 * seqs * dps :]
    hd = o_refs[0].shape[1]
    rows, features = out_ref.shape
    depth = features // share
    half = depth // 2
    for j in range(heads):
        got[mate(place_ref[1], j, heads)] = got_refs[j][...]
    out_s[...] = jnp.zeros_like(out_s)
    grad_s[...] = jnp.zeros_like(grad_s)
    for j in range(seqs):
        for d in range(dps):
            o = o_refs[j * dps + d]
            h, r = owner_of(place_ref, seqs, dps, share, j, d)
            out_s[r] = out_s[r] + mm(got[h, 0:rows, 3 * hd :], o[0:depth, :], NT)
            line = rate_line(o[depth:, :], depth)
            logit = got[h, rows:, 0:rows].astype(F32).T
            grad = [mm(logit, jnp.broadcast_to(line, (EXTRA, depth)), NN)]
            mine = got[h, 0:rows, 0 : 3 * hd]
            halves = []
            for part in range(2):
                w = w_refs[(part * seqs + j) * dps + d]
                wide = jnp.concatenate([w[c * half : (c + 1) * half, :] for c in range(3)], axis=1)
                halves.append(mm(mine, wide, NT))
            grad_s[r] = grad_s[r] + grad[0] + jnp.concatenate(halves, axis=1)
    for r in range(share):
        out_ref[:, r * depth : (r + 1) * depth] = out_s[r].astype(BF16)
        dtok_ref[:, r * depth : (r + 1) * depth] = grad_s[r].astype(BF16)


VMEM = pl.BlockSpec(memory_space=pltpu.VMEM)
SMEM = pl.BlockSpec(memory_space=pltpu.SMEM)
PARAMS = pltpu.CompilerParams(vmem_limit_bytes=48 * 1024 * 1024)


def call(kernel, outs, operands, scratch=()):
    return pl.pallas_call(
        kernel,
        out_shape=outs,
        in_specs=[SMEM] + [VMEM] * (len(operands) - 1),
        out_specs=jax.tree.map(lambda unused: VMEM, outs),
        scratch_shapes=list(scratch),
        compiler_params=PARAMS,
    )(*operands)


def body(tokens, w_qkv, w_lr, w_out, w1_init, w2_init, d_out):
    seqs, heads, dps = (lax.axis_size(a) for a in ("seq", "head", "dp"))
    share = seqs * dps // heads
    rows, features = tokens.shape[1:]
    depth, unused, hd = w_qkv.shape
    inner = w1_init.shape[2]
    blocks = seqs * rows // MB
    place = jnp.stack([lax.axis_index(a).astype(jnp.int32) for a in ("seq", "head", "dp")])
    sizes = (seqs, heads, dps, share)

    pairs = []
    for seq in range(seqs):
        for head in range(heads):
            for dp in range(dps):
                k = seq * dps + dp
                target = head * share + k % share
                to = ((target // dps) * heads + k // share) * dps + target % dps
                pairs.append(((seq * heads + head) * dps + dp, to))

    def swapped(array):
        return lax.ppermute(array, ("seq", "head", "dp"), pairs)

    half = depth // 2
    count = depth // 128
    lines = jnp.pad(
        w_lr[:, 0].reshape(seqs * dps, count, 128), ((0, 0), (0, EXTRA - count), (0, 0))
    )
    own = lax.axis_index("seq") * dps + lax.axis_index("dp")
    line = lax.dynamic_index_in_dim(lines, own, 0, keepdims=False)
    by_kind = w_qkv.transpose(1, 0, 2)

    outer_w = swapped(jnp.concatenate([w_out, line], axis=0))
    near = peers_of(by_kind.reshape(3 * depth, hd), "dp")
    head_ws = [list(pieces) for pieces in zip(*[peers_of(piece, "seq") for piece in near])]
    own_tokens, outer_w = lax.optimization_barrier((tokens[0], outer_w))
    features_of = peers_of(own_tokens, "head")
    projected = call(
        functools.partial(projection_kernel, *sizes),
        jax.ShapeDtypeStruct((rows + 8, 3 * hd), F32),
        (place, *features_of, *sum(head_ws, []), lines),
        [pltpu.VMEM((seqs * dps, rows, depth), BF16)],
    )

    outer_w, *near = lax.optimization_barrier((outer_w, *near))
    outer_ws = sum(in_plane(outer_w, 0), [])
    first, *features_of = lax.optimization_barrier(
        (by_kind[:, :half].reshape(3 * half, hd), *features_of)
    )
    first_w = swapped(first)
    second, first_w = lax.optimization_barrier((by_kind[:, half:].reshape(3 * half, hd), first_w))
    second_w = swapped(second)
    inner_ws = sum(in_plane(first_w, 1), []) + sum(in_plane(second_w, 2), [])

    def summed(arrays):
        return functools.reduce(lambda a, b: a + b, [a.astype(F32) for a in arrays])

    outer_part = call(
        functools.partial(outer_kernel, *sizes),
        (jax.ShapeDtypeStruct((rows, hd), BF16),) * heads,
        (place, d_out[0], *outer_ws),
        [pltpu.VMEM((share, rows, depth), BF16), pltpu.VMEM((heads, rows, hd), F32)],
    )
    outer_all = peers_of(summed(sent_to(outer_part, "head")), "seq")
    inner_all = peers_of(projected, "seq")

    long = seqs * rows
    scratch = (
        [pltpu.VMEM((long, hd), F32)] * 4
        + [pltpu.VMEM((blocks, 8, 2 * MB), F32)] * 2
        + [pltpu.VMEM((long, 4 * hd), BF16), pltpu.VMEM((blocks, 8, 2 * MB), F32)]
        + [pltpu.VMEM((hd, inner), F32)] * 2
        + [pltpu.VMEM((blocks, hd, inner), BF16)] * 2
        + [pltpu.VMEM((blocks, MB, inner), t) for t in (BF16, F32, F32, F32, BF16, BF16, F32, F32)]
        + [pltpu.VMEM((blocks, MB, hd), t) for t in (BF16, F32, F32, F32, F32, F32, F32, F32)]
        + [pltpu.VMEM((blocks, 8, 2 * MB), F32), pltpu.VMEM((inner, 2 * hd), F32)]
    )
    part = inner // (seqs * dps)
    result, *d_inner = call(
        functools.partial(inner_kernel, seqs, dps),
        (jax.ShapeDtypeStruct((rows + EXTRA, 4 * hd), BF16),)
        + (jax.ShapeDtypeStruct((part, 2 * hd), F32),) * dps,
        (place, *inner_all, *outer_all, w1_init[0], w2_init[0]),
        scratch,
    )
    got = peers_of(result, "head")
    got[1], *d_inner = lax.optimization_barrier((got[1], *d_inner))
    shares = summed(sent_to(d_inner, "dp"))
    out, d_tokens = call(
        functools.partial(output_kernel, *sizes),
        (jax.ShapeDtypeStruct((rows, features), BF16),) * 2,
        (place, *got, *outer_ws, *inner_ws),
        [
            pltpu.VMEM((heads, rows + EXTRA, 4 * hd), BF16),
            pltpu.VMEM((share, rows, features // share), F32),
            pltpu.VMEM((share, rows, features // share), F32),
        ],
    )
    return (out[None], d_tokens[None], shares[:, :hd].transpose(1, 0)[None], shares[:, hd:][None])


def solution(mesh):
    placed = (
        P("dp", "seq", "head"),
        P(("seq", "dp"), None, "head"),
        P(None, "head"),
        P(("seq", "dp"), "head"),
        P("head", None, None),
        P("head", None, None),
        P("dp", "seq", "head"),
    )
    return jax.shard_map(
        body,
        mesh=mesh,
        in_specs=placed,
        out_specs=(
            P("dp", "seq", "head"),
            P("dp", "seq", "head"),
            P("head", None, ("seq", "dp")),
            P("head", ("seq", "dp"), None),
        ),
        check_vma=False,
    )
```

```python
import functools

import jax
import jax.numpy as jnp
from jax import lax
from jax.experimental import pallas as pl
from jax.experimental.pallas import tpu as pltpu
from jax.sharding import PartitionSpec as P

MB = 64
EPSILON = 1e-06
BASE_RATE = 0.1
GELU_SCALE = 0.7978845608028654
GELU_CUBIC = 0.044715
NN = ((1,), (0,))
NT = ((1,), (1,))
TN = ((0,), (0,))
EXTRA = 16
UNROLL_LIMIT = 8
F32 = jnp.float32
BF16 = jnp.bfloat16


def mm(left, right, dims):
    return lax.dot_general(
        left.astype(BF16), right.astype(BF16), (dims, ((), ())), preferred_element_type=F32
    )


def padded(lines):
    return jnp.concatenate([lines, jnp.zeros_like(lines)], axis=1)


def mean(rows):
    return jnp.mean(rows, axis=-1, keepdims=True)


def gelu_parts(v):
    square = v * v
    bend = jnp.tanh(v * (GELU_SCALE + (GELU_SCALE * GELU_CUBIC) * square))
    half = 0.5 + 0.5 * bend
    slope = GELU_SCALE + (3.0 * GELU_SCALE * GELU_CUBIC) * square
    bell = 0.5 - 0.5 * bend * bend
    lean = bell * slope
    second = 2.0 * lean * (1.0 - v * bend * slope) + (6.0 * GELU_SCALE * GELU_CUBIC) * square * bell
    return v * half, half + v * lean, second


def gelu_two(v):
    square = v * v
    bend = jnp.tanh(v * (GELU_SCALE + (GELU_SCALE * GELU_CUBIC) * square))
    half = 0.5 + 0.5 * bend
    slope = GELU_SCALE + (3.0 * GELU_SCALE * GELU_CUBIC) * square
    return v * half, half + v * ((0.5 - 0.5 * bend * bend) * slope)


def mate(index, step, count):
    if count & (count - 1) == 0:
        return index ^ step
    return (index + step) % count


def hop(array, axis, step):
    count = lax.axis_size(axis)
    return lax.ppermute(array, axis, [(mate(i, step, count), i) for i in range(count)])


def peers_of(array, axis):
    return [array] + [hop(array, axis, j) for j in range(1, lax.axis_size(axis))]


def sent_to(arrays, axis):
    count = lax.axis_size(axis)
    back = [arrays[0]]
    for j in range(1, count):
        back.append(lax.ppermute(arrays[j], axis, [(i, mate(i, j, count)) for i in range(count)]))
    return back


def gathered(array, axis):
    count = lax.axis_size(axis)
    return lax.all_to_all(jnp.broadcast_to(array[None], (count,) + array.shape), axis, 0, 0)


def over_seq(near):
    return sum([list(pieces) for pieces in zip(*[peers_of(piece, "seq") for piece in near])], [])


def owner_of(place_ref, seqs, dps, share, j, d):
    seq, dp = place_ref[0], place_ref[2]
    k = mate(seq, j, seqs) * dps + mate(dp, d, dps)
    return k // share, k % share


def rate_line(block, depth):
    rows = block.astype(F32)
    return jnp.concatenate([rows[i : i + 1, :] for i in range(depth // 128)], axis=1)


def outer_kernel(seqs, heads, dps, share, place_ref, dout_ref, *refs):
    w_refs = refs[: seqs * dps]
    out_refs = refs[seqs * dps : seqs * dps + heads]
    dout_s, acc = refs[seqs * dps + heads :]
    rows, features = dout_ref.shape
    depth = features // share
    for r in range(share):
        dout_s[r] = dout_ref[:, r * depth : (r + 1) * depth]
    acc[...] = jnp.zeros_like(acc)
    for j in range(seqs):
        for d in range(dps):
            h, r = owner_of(place_ref, seqs, dps, share, j, d)
            acc[h] = acc[h] + mm(dout_s[r], w_refs[j * dps + d][...], NN)
    for j in range(heads):
        out_refs[j][...] = acc[mate(place_ref[1], j, heads)].astype(BF16)


def projection_kernel(seqs, heads, dps, share, place_ref, *refs):
    tok_ref, refs = refs[0], refs[1:]
    w_refs, rate_ref, out_ref, tok_s = refs[: seqs * dps], *refs[seqs * dps :]
    unused, rows, features = tok_ref.shape
    depth = features // share
    for h in range(heads):
        for r in range(share):
            tok_s[h * share + r] = tok_ref[h, :, r * depth : (r + 1) * depth]
    total = None
    logit = None
    for j in range(seqs):
        for d in range(dps):
            w = w_refs[j * dps + d]
            h, r = owner_of(place_ref, seqs, dps, share, j, d)
            k = h * share + r
            tok = tok_s[k]
            wide = jnp.concatenate([w[c * depth : (c + 1) * depth, :] for c in range(3)], axis=1)
            term = mm(tok, wide, NN)
            line = mm(jnp.broadcast_to(rate_line(rate_ref[k], depth), (EXTRA, depth)), tok, NT)
            total = term if total is None else total + term
            logit = line if logit is None else logit + line
    out_ref[0:rows, :] = total
    out_ref[rows:, :] = jnp.concatenate([logit[0:8]] * (total.shape[1] // rows), axis=1)


def inner_kernel(seqs, dps, place_ref, *refs):
    x_refs, y_refs = refs[:seqs], refs[seqs : 2 * seqs]
    w1_ref, w2_ref, res_ref, ttt_ref = refs[2 * seqs : 2 * seqs + 4]
    dw_refs = refs[2 * seqs + 4 : 2 * seqs + 4 + dps]
    (
        qs, ks, vs, ds, es, sg, os, lg,
        w1c, w2c, w1b, w2b,
        x2s, g1s, pgs, gfs, xqs, zqs, dx2s, dg1s,
        dys, ns, rs, ss, cs, g2s, dg2s, dks, des, ws,
    ) = refs[2 * seqs + 4 + dps :]
    rows = y_refs[0].shape[0]
    hd = y_refs[0].shape[1]
    blocks = seqs * rows // MB
    per = rows // MB
    place = place_ref[0]

    for j in range(seqs):
        owner = mate(place, j, seqs)
        at = pl.ds(pl.multiple_of(owner * rows, rows), rows)
        qs[at, :] = x_refs[j][0:rows, 0:hd]
        ks[at, :] = x_refs[j][0:rows, hd : 2 * hd]
        vs[at, :] = x_refs[j][0:rows, 2 * hd : 3 * hd]
        ds[at, :] = y_refs[j][...]
        gate = jax.nn.sigmoid(x_refs[j][rows:, 0:rows])
        scaled = (BASE_RATE / hd) * gate
        for b in range(per):
            es[owner * per + b] = padded(scaled[:, b * MB : (b + 1) * MB])
            sg[owner * per + b] = padded((scaled * (1.0 - gate))[:, b * MB : (b + 1) * MB])

    w1c[...] = w1_ref[...]
    start = w2_ref[...]
    w2c[...] = (start - mean(start)).T

    at_row = lax.broadcasted_iota(jnp.int32, (MB, MB), 0)
    at_col = lax.broadcasted_iota(jnp.int32, (MB, MB), 1)
    causal = at_col <= at_row
    diagonal = at_col == at_row

    def to_column(line):
        return jnp.sum(jnp.where(diagonal, line, 0.0), axis=1, keepdims=True)

    def to_line(column):
        return jnp.sum(jnp.where(diagonal, column, 0.0), axis=0, keepdims=True)

    def at_block(i):
        if isinstance(i, int):
            return slice(i * MB, (i + 1) * MB)
        return pl.ds(pl.multiple_of(i * MB, MB), MB)

    def forward(i):
        at = at_block(i)
        q, k, v, d_o = qs[at, :], ks[at, :], vs[at, :], ds[at, :]
        line = es[i][0:1, 0:MB]
        e = to_column(line)
        mask = jnp.where(causal, line, 0.0)
        w1 = w1c[...].astype(BF16)
        w2 = w2c[...].astype(BF16)
        w1b[i] = w1
        w2b[i] = w2
        kb, qb = k.astype(BF16), q.astype(BF16)
        gap = v - k
        gap = gap - mean(gap)
        both = mm(jnp.concatenate([kb, qb], axis=0), w1, NN)
        x2, g1, gg1 = gelu_parts(both[:MB])
        x2b = x2.astype(BF16)
        c = mm(x2b, w2, NT)
        var = mean(c * c)
        cross = mean(gap * c)
        s = lax.rsqrt(var + EPSILON)
        n = c * s
        cc = var * s * s - s * cross
        r = n - gap
        g2 = s * (r - n * cc)
        g2b = g2.astype(BF16)
        p = mm(g2b, w2, NN)
        g1f = p * g1
        w1c[...] = w1c[...] - mm(k, e * g1f, TN)
        w2c[...] = w2c[...] - mm(e * g2, x2b, TN)
        g1b = g1f.astype(BF16)
        b1 = mm(qb, kb, NT)
        a1 = (b1 * mask).astype(BF16)
        zq = both[MB:] - mm(a1, g1b, NN)
        xq, gq = gelu_two(zq)
        xqb = xq.astype(BF16)
        b2 = mm(xqb, x2b, NT)
        a2 = (b2 * mask).astype(BF16)
        y = mm(xqb, w2, NT) - mm(a2, g2b, NN)
        sq = lax.rsqrt(mean(y * y) + EPSILON)
        nq = y * sq
        os[at, 3 * hd : 4 * hd] = (q + nq).astype(BF16)
        dy = sq * (d_o - mean(d_o) - nq * mean(d_o * nq))
        dyb = dy.astype(BF16)
        da2 = -mm(dyb, g2b, NT)
        db2 = (da2 * mask).astype(BF16)
        dg2s[i] = -mm(a2, dyb, TN)
        dxq = mm(dyb, w2, NN) + mm(db2, x2b, NN)
        dx2s[i] = mm(db2, xqb, TN)
        dzq = (dxq * gq).astype(BF16)
        da1 = -mm(dzq, g1b, NT)
        db1 = (da1 * mask).astype(BF16)
        dg1s[i] = -mm(a1, dzq, TN)
        dq = d_o + mm(dzq, w1, NT) + mm(db1, kb, NN)
        os[at, 0:hd] = dq.astype(BF16)
        dks[i] = mm(db1, qb, TN)
        de = jnp.sum(jnp.where(causal, da2 * b2 + da1 * b1, 0.0), axis=0, keepdims=True)
        des[i] = padded(jnp.broadcast_to(de, (8, MB)))
        x2s[i] = x2b
        g1s[i] = g1
        pgs[i] = p * gg1
        gfs[i] = g1f
        xqs[i] = xqb
        zqs[i] = dzq
        dys[i] = dyb
        ns[i] = n
        rs[i] = r
        ss[i] = jnp.broadcast_to(s, (MB, hd))
        cs[i] = jnp.broadcast_to(cc, (MB, hd))
        g2s[i] = g2

    def backward(i):
        at = at_block(i)
        q, k = qs[at, :], ks[at, :]
        e = to_column(es[i][0:1, 0:MB])
        w1, w2 = w1b[i], w2b[i]
        d1, d2 = w1c[...].astype(BF16), w2c[...].astype(BF16)
        x2b, g1, g1f, g2 = x2s[i], g1s[i], gfs[i], g2s[i]
        n, s, cc = ns[i], ss[i], cs[i]
        dh1 = -mm(k, d1, NN)
        dh2 = -mm(x2b, d2, NT)
        dg1 = dg1s[i] + e * dh1
        dp = (dg1 * g1).astype(BF16)
        dg2 = dg2s[i] + e * dh2 + mm(dp, w2, NT)
        dt = s * dg2
        mt = mean(dt * n)
        dr = dt - mean(dt) - n * mt
        dn = dr - cc * dt - rs[i] * mt
        du = s * (dn - mean(dn) - n * (mean(dn * n) + mean(dg2 * g2)))
        dub = du.astype(BF16)
        mixed = jnp.concatenate([(-e * g2).astype(BF16), dub], axis=1)
        dx2 = dx2s[i] + mm(mixed, jnp.concatenate([d2, w2], axis=0), NN)
        dz1 = (dg1 * pgs[i] + dx2 * g1).astype(BF16)
        mixed = jnp.concatenate([(-e * g1f).astype(BF16), dz1], axis=1)
        dk = dks[i] + dr + mm(mixed, jnp.concatenate([d1, w1], axis=1), NT)
        w1c[...] = w1c[...] + mm(
            jnp.concatenate([q, k], axis=0), jnp.concatenate([zqs[i], dz1], axis=0), TN
        )
        w2c[...] = w2c[...] + mm(
            jnp.concatenate([dys[i].astype(F32), du, g2], axis=0),
            jnp.concatenate([xqs[i], x2b, dp], axis=0),
            TN,
        )
        extra = jnp.sum(g1f * dh1, axis=1, keepdims=True) + jnp.sum(
            g2 * dh2, axis=1, keepdims=True
        )
        line = (des[i][0:1, 0:MB] + to_line(extra)) * sg[i][0:1, 0:MB]
        lg[i] = padded(jnp.broadcast_to(line, (8, MB)))
        os[at, hd : 2 * hd] = dk.astype(BF16)
        os[at, 2 * hd : 3 * hd] = (-dr).astype(BF16)

    def loop(step, order):
        if blocks <= UNROLL_LIMIT:
            for i in range(blocks):
                step(order(i))
        else:
            lax.fori_loop(0, blocks, lambda i, unused: (step(order(i)), unused)[1], 0)

    loop(forward, lambda i: i)
    w1c[...] = jnp.zeros_like(w1c)
    w2c[...] = jnp.zeros_like(w2c)
    loop(backward, lambda i: blocks - 1 - i)

    at = pl.ds(pl.multiple_of(place * rows, rows), rows)
    res_ref[0:rows, :] = os[at, 0 : 3 * hd]
    ttt_ref[...] = os[at, 3 * hd :]
    res_ref[rows:, :] = jnp.zeros((EXTRA, 3 * hd), BF16)
    first_row = lax.broadcasted_iota(jnp.int32, (EXTRA, rows), 0) == 0
    lines = jnp.concatenate([lg[place * per + b][0:1, 0:MB] for b in range(per)], axis=1)
    lines = jnp.where(first_row, jnp.broadcast_to(lines, (EXTRA, rows)), 0.0)
    res_ref[rows:, 0:rows] = lines.astype(BF16)

    part = dw_refs[0].shape[0]
    ws[:, 0:hd] = w1c[...].T
    ws[:, hd : 2 * hd] = w2c[...].T
    for d in range(dps):
        first = (place * dps + mate(place_ref[2], d, dps)) * part
        dw_refs[d][...] = ws[pl.ds(pl.multiple_of(first, part), part), :]


def output_kernel(seqs, heads, dps, share, place_ref, *refs):
    got_refs, w_refs = refs[:heads], refs[heads : heads + seqs * dps]
    out_ref, got, out_s = refs[heads + seqs * dps :]
    rows, features = out_ref.shape
    depth = features // share
    for j in range(heads):
        got[mate(place_ref[1], j, heads)] = got_refs[j][...]
    out_s[...] = jnp.zeros_like(out_s)
    for j in range(seqs):
        for d in range(dps):
            h, r = owner_of(place_ref, seqs, dps, share, j, d)
            out_s[r] = out_s[r] + mm(got[h], w_refs[j * dps + d][...], NT)
    for r in range(share):
        out_ref[:, r * depth : (r + 1) * depth] = out_s[r].astype(BF16)


def token_grad_kernel(seqs, heads, dps, share, place_ref, grad_ref, *refs):
    w_refs, rate_ref = refs[: seqs * dps], refs[seqs * dps]
    out_refs, full = refs[seqs * dps + 1 :][:heads], refs[-1]
    rows, features = out_refs[0].shape
    depth = features // share
    grad = grad_ref[0:rows, :]
    logit = grad_ref[rows:, 0:rows].astype(F32).T.astype(BF16)
    for j in range(seqs):
        for d in range(dps):
            w = w_refs[j * dps + d]
            h, r = owner_of(place_ref, seqs, dps, share, j, d)
            k = h * share + r
            wide = jnp.concatenate([w[c * depth : (c + 1) * depth, :] for c in range(3)], axis=1)
            line = jnp.broadcast_to(rate_line(rate_ref[k], depth), (EXTRA, depth))
            full[k] = (mm(grad, wide, NT) + mm(logit, line, NN)).astype(BF16)
    for j in range(heads):
        h = mate(place_ref[1], j, heads)
        for r in range(share):
            out_refs[j][:, r * depth : (r + 1) * depth] = full[h * share + r]


VMEM = pl.BlockSpec(memory_space=pltpu.VMEM)
SMEM = pl.BlockSpec(memory_space=pltpu.SMEM)
PARAMS = pltpu.CompilerParams(vmem_limit_bytes=48 * 1024 * 1024)


def call(kernel, outs, operands, scratch=()):
    return pl.pallas_call(
        kernel,
        out_shape=outs,
        in_specs=[SMEM] + [VMEM] * (len(operands) - 1),
        out_specs=jax.tree.map(lambda unused: VMEM, outs),
        scratch_shapes=list(scratch),
        compiler_params=PARAMS,
    )(*operands)


def body(tokens, w_qkv, w_lr, w_out, w1_init, w2_init, d_out):
    seqs, heads, dps = (lax.axis_size(a) for a in ("seq", "head", "dp"))
    share = seqs * dps // heads
    rows, features = tokens.shape[1:]
    depth, unused, hd = w_qkv.shape
    inner = w1_init.shape[2]
    blocks = seqs * rows // MB
    place = jnp.stack([lax.axis_index(a).astype(jnp.int32) for a in ("seq", "head", "dp")])
    sizes = (seqs, heads, dps, share)

    pairs = []
    for seq in range(seqs):
        for head in range(heads):
            for dp in range(dps):
                k = seq * dps + dp
                target = head * share + k % share
                to = ((target // dps) * heads + k // share) * dps + target % dps
                pairs.append(((seq * heads + head) * dps + dp, to))

    def swapped(array):
        return lax.ppermute(array, ("seq", "head", "dp"), pairs)

    count = depth // 128
    lines = jnp.pad(
        w_lr[:, 0].reshape(seqs * dps, count, 128), ((0, 0), (0, EXTRA - count), (0, 0))
    )

    def summed(arrays):
        return functools.reduce(lambda a, b: a + b, [a.astype(F32) for a in arrays])

    outer_w = swapped(w_out)
    near = peers_of(w_qkv.transpose(1, 0, 2).reshape(3 * depth, hd), "dp")
    features_of = gathered(tokens[0], "head")
    head_ws = over_seq(near)
    projected = call(
        functools.partial(projection_kernel, *sizes),
        jax.ShapeDtypeStruct((rows + 8, 3 * hd), F32),
        (place, features_of, *head_ws, lines),
        [pltpu.VMEM((seqs * dps, rows, depth), BF16)],
    )
    inner_all = peers_of(projected, "seq")

    outer_w, *near = lax.optimization_barrier((outer_w, *near))
    outer_near = peers_of(outer_w, "dp")
    *outer_near, unused = lax.optimization_barrier((*outer_near, head_ws[-1]))
    outer_ws = over_seq(outer_near)
    own_d_out, projected = lax.optimization_barrier((d_out[0], projected))
    outer_part = call(
        functools.partial(outer_kernel, *sizes),
        (jax.ShapeDtypeStruct((rows, hd), BF16),) * heads,
        (place, own_d_out, *outer_ws),
        [pltpu.VMEM((share, rows, depth), BF16), pltpu.VMEM((heads, rows, hd), F32)],
    )
    outer_all = peers_of(summed(sent_to(outer_part, "head")), "seq")

    long = seqs * rows
    scratch = (
        [pltpu.VMEM((long, hd), F32)] * 4
        + [pltpu.VMEM((blocks, 8, 2 * MB), F32)] * 2
        + [pltpu.VMEM((long, 4 * hd), BF16), pltpu.VMEM((blocks, 8, 2 * MB), F32)]
        + [pltpu.VMEM((hd, inner), F32)] * 2
        + [pltpu.VMEM((blocks, hd, inner), BF16)] * 2
        + [pltpu.VMEM((blocks, MB, inner), t) for t in (BF16, F32, F32, F32, BF16, BF16, F32, F32)]
        + [pltpu.VMEM((blocks, MB, hd), t) for t in (BF16, F32, F32, F32, F32, F32, F32, F32)]
        + [pltpu.VMEM((blocks, 8, 2 * MB), F32), pltpu.VMEM((inner, 2 * hd), F32)]
    )
    part = inner // (seqs * dps)
    result, ttt, *d_inner = call(
        functools.partial(inner_kernel, seqs, dps),
        (
            jax.ShapeDtypeStruct((rows + EXTRA, 3 * hd), BF16),
            jax.ShapeDtypeStruct((rows, hd), BF16),
        )
        + (jax.ShapeDtypeStruct((part, 2 * hd), F32),) * dps,
        (place, *inner_all, *outer_all, w1_init[0], w2_init[0]),
        scratch,
    )
    got = peers_of(ttt, "head")
    token_part = call(
        functools.partial(token_grad_kernel, *sizes),
        (jax.ShapeDtypeStruct((rows, features), BF16),) * heads,
        (place, result, *head_ws, lines),
        [pltpu.VMEM((seqs * dps, rows, depth), BF16)],
    )
    back = sent_to(token_part, "head")
    d_tokens = summed(back).astype(BF16)
    unused, *d_inner = lax.optimization_barrier((back[1], *d_inner))
    shares = summed(sent_to(d_inner, "dp"))
    out = call(
        functools.partial(output_kernel, *sizes),
        jax.ShapeDtypeStruct((rows, features), BF16),
        (place, *got, *outer_ws),
        [pltpu.VMEM((heads, rows, hd), BF16), pltpu.VMEM((share, rows, depth), F32)],
    )
    return (out[None], d_tokens[None], shares[:, :hd].transpose(1, 0)[None], shares[:, hd:][None])


def solution(mesh):
    placed = (
        P("dp", "seq", "head"),
        P(("seq", "dp"), None, "head"),
        P(None, "head"),
        P(("seq", "dp"), "head"),
        P("head", None, None),
        P("head", None, None),
        P("dp", "seq", "head"),
    )
    return jax.shard_map(
        body,
        mesh=mesh,
        in_specs=placed,
        out_specs=(
            P("dp", "seq", "head"),
            P("dp", "seq", "head"),
            P("head", None, ("seq", "dp")),
            P("head", ("seq", "dp"), None),
        ),
        check_vma=False,
    )
```

```python
import functools

import jax
import jax.numpy as jnp
from jax import lax
from jax.experimental import pallas as pl
from jax.experimental.pallas import tpu as pltpu
from jax.sharding import PartitionSpec as P

MB = 64
EPSILON = 1e-06
BASE_RATE = 0.1
GELU_SCALE = 0.7978845608028654
GELU_CUBIC = 0.044715
NN = ((1,), (0,))
NT = ((1,), (1,))
TN = ((0,), (0,))
EXTRA = 16
UNROLL_LIMIT = 8
F32 = jnp.float32
BF16 = jnp.bfloat16


def mm(left, right, dims):
    return lax.dot_general(
        left.astype(BF16), right.astype(BF16), (dims, ((), ())), preferred_element_type=F32
    )


def padded(lines):
    return jnp.concatenate([lines, jnp.zeros_like(lines)], axis=1)


def mean(rows):
    return jnp.mean(rows, axis=-1, keepdims=True)


def gelu_parts(v):
    square = v * v
    bend = jnp.tanh(v * (GELU_SCALE + (GELU_SCALE * GELU_CUBIC) * square))
    half = 0.5 + 0.5 * bend
    slope = GELU_SCALE + (3.0 * GELU_SCALE * GELU_CUBIC) * square
    bell = 0.5 - 0.5 * bend * bend
    lean = bell * slope
    second = 2.0 * lean * (1.0 - v * bend * slope) + (6.0 * GELU_SCALE * GELU_CUBIC) * square * bell
    return v * half, half + v * lean, second


def gelu_two(v):
    square = v * v
    bend = jnp.tanh(v * (GELU_SCALE + (GELU_SCALE * GELU_CUBIC) * square))
    half = 0.5 + 0.5 * bend
    slope = GELU_SCALE + (3.0 * GELU_SCALE * GELU_CUBIC) * square
    return v * half, half + v * ((0.5 - 0.5 * bend * bend) * slope)


def mate(index, step, count):
    if count & (count - 1) == 0:
        return index ^ step
    return (index + step) % count


def hop(array, axis, step):
    count = lax.axis_size(axis)
    return lax.ppermute(array, axis, [(mate(i, step, count), i) for i in range(count)])


def peers_of(array, axis):
    return [array] + [hop(array, axis, j) for j in range(1, lax.axis_size(axis))]


def sent_to(arrays, axis):
    count = lax.axis_size(axis)
    back = [arrays[0]]
    for j in range(1, count):
        back.append(lax.ppermute(arrays[j], axis, [(i, mate(i, j, count)) for i in range(count)]))
    return back


def gathered(array, axis):
    count = lax.axis_size(axis)
    return lax.all_to_all(jnp.broadcast_to(array[None], (count,) + array.shape), axis, 0, 0)


def over_seq(near):
    return sum([list(pieces) for pieces in zip(*[peers_of(piece, "seq") for piece in near])], [])


def owner_of(place_ref, seqs, dps, share, j, d):
    seq, dp = place_ref[0], place_ref[2]
    k = mate(seq, j, seqs) * dps + mate(dp, d, dps)
    return k // share, k % share


def rate_line(block, depth):
    rows = block.astype(F32)
    return jnp.concatenate([rows[i : i + 1, :] for i in range(depth // 128)], axis=1)


def outer_kernel(seqs, heads, dps, share, place_ref, dout_ref, *refs):
    w_refs = refs[: seqs * dps]
    out_refs = refs[seqs * dps : seqs * dps + heads]
    dout_s, acc = refs[seqs * dps + heads :]
    rows, features = dout_ref.shape
    depth = features // share
    for r in range(share):
        dout_s[r] = dout_ref[:, r * depth : (r + 1) * depth]
    acc[...] = jnp.zeros_like(acc)
    for j in range(seqs):
        for d in range(dps):
            h, r = owner_of(place_ref, seqs, dps, share, j, d)
            acc[h] = acc[h] + mm(dout_s[r], w_refs[j * dps + d][0:depth, :], NN)
    for j in range(heads):
        out_refs[j][...] = acc[mate(place_ref[1], j, heads)].astype(BF16)


def projection_kernel(seqs, heads, dps, share, place_ref, *refs):
    tok_ref, refs = refs[0], refs[1:]
    w_refs, rate_ref, out_ref, tok_s = refs[: seqs * dps], *refs[seqs * dps :]
    unused, rows, features = tok_ref.shape
    depth = features // share
    for h in range(heads):
        for r in range(share):
            tok_s[h * share + r] = tok_ref[h, :, r * depth : (r + 1) * depth]
    total = None
    logit = None
    for j in range(seqs):
        for d in range(dps):
            w = w_refs[j * dps + d]
            h, r = owner_of(place_ref, seqs, dps, share, j, d)
            k = h * share + r
            tok = tok_s[k]
            wide = jnp.concatenate([w[c * depth : (c + 1) * depth, :] for c in range(3)], axis=1)
            term = mm(tok, wide, NN)
            line = mm(jnp.broadcast_to(rate_line(rate_ref[k], depth), (EXTRA, depth)), tok, NT)
            total = term if total is None else total + term
            logit = line if logit is None else logit + line
    out_ref[0:rows, :] = total
    out_ref[rows:, :] = jnp.concatenate([logit[0:8]] * (total.shape[1] // rows), axis=1)


def inner_kernel(seqs, dps, place_ref, *refs):
    x_refs, y_refs = refs[:seqs], refs[seqs : 2 * seqs]
    w1_ref, w2_ref, res_ref = refs[2 * seqs : 2 * seqs + 3]
    dw_refs = refs[2 * seqs + 3 : 2 * seqs + 3 + dps]
    (
        qs, ks, vs, ds, es, sg, os, lg,
        w1c, w2c, w1b, w2b,
        x2s, g1s, pgs, gfs, xqs, zqs, dx2s, dg1s,
        dys, ns, rs, ss, cs, g2s, dg2s, dks, des, ws,
    ) = refs[2 * seqs + 3 + dps :]
    rows = y_refs[0].shape[0]
    hd = y_refs[0].shape[1]
    blocks = seqs * rows // MB
    per = rows // MB
    place = place_ref[0]

    for j in range(seqs):
        owner = mate(place, j, seqs)
        at = pl.ds(pl.multiple_of(owner * rows, rows), rows)
        qs[at, :] = x_refs[j][0:rows, 0:hd]
        ks[at, :] = x_refs[j][0:rows, hd : 2 * hd]
        vs[at, :] = x_refs[j][0:rows, 2 * hd : 3 * hd]
        ds[at, :] = y_refs[j][...]
        gate = jax.nn.sigmoid(x_refs[j][rows:, 0:rows])
        scaled = (BASE_RATE / hd) * gate
        for b in range(per):
            es[owner * per + b] = padded(scaled[:, b * MB : (b + 1) * MB])
            sg[owner * per + b] = padded((scaled * (1.0 - gate))[:, b * MB : (b + 1) * MB])

    w1c[...] = w1_ref[...]
    start = w2_ref[...]
    w2c[...] = (start - mean(start)).T

    at_row = lax.broadcasted_iota(jnp.int32, (MB, MB), 0)
    at_col = lax.broadcasted_iota(jnp.int32, (MB, MB), 1)
    causal = at_col <= at_row
    diagonal = at_col == at_row

    def to_column(line):
        return jnp.sum(jnp.where(diagonal, line, 0.0), axis=1, keepdims=True)

    def to_line(column):
        return jnp.sum(jnp.where(diagonal, column, 0.0), axis=0, keepdims=True)

    def at_block(i):
        if isinstance(i, int):
            return slice(i * MB, (i + 1) * MB)
        return pl.ds(pl.multiple_of(i * MB, MB), MB)

    def forward(i):
        at = at_block(i)
        q, k, v, d_o = qs[at, :], ks[at, :], vs[at, :], ds[at, :]
        line = es[i][0:1, 0:MB]
        e = to_column(line)
        mask = jnp.where(causal, line, 0.0)
        w1 = w1c[...].astype(BF16)
        w2 = w2c[...].astype(BF16)
        w1b[i] = w1
        w2b[i] = w2
        kb, qb = k.astype(BF16), q.astype(BF16)
        gap = v - k
        gap = gap - mean(gap)
        both = mm(jnp.concatenate([kb, qb], axis=0), w1, NN)
        x2, g1, gg1 = gelu_parts(both[:MB])
        x2b = x2.astype(BF16)
        c = mm(x2b, w2, NT)
        var = mean(c * c)
        cross = mean(gap * c)
        s = lax.rsqrt(var + EPSILON)
        n = c * s
        cc = var * s * s - s * cross
        r = n - gap
        g2 = s * (r - n * cc)
        g2b = g2.astype(BF16)
        p = mm(g2b, w2, NN)
        g1f = p * g1
        w1c[...] = w1c[...] - mm(k, e * g1f, TN)
        w2c[...] = w2c[...] - mm(e * g2, x2b, TN)
        g1b = g1f.astype(BF16)
        b1 = mm(qb, kb, NT)
        a1 = (b1 * mask).astype(BF16)
        zq = both[MB:] - mm(a1, g1b, NN)
        xq, gq = gelu_two(zq)
        xqb = xq.astype(BF16)
        b2 = mm(xqb, x2b, NT)
        a2 = (b2 * mask).astype(BF16)
        y = mm(xqb, w2, NT) - mm(a2, g2b, NN)
        sq = lax.rsqrt(mean(y * y) + EPSILON)
        nq = y * sq
        os[at, 3 * hd : 4 * hd] = (q + nq).astype(BF16)
        dy = sq * (d_o - mean(d_o) - nq * mean(d_o * nq))
        dyb = dy.astype(BF16)
        da2 = -mm(dyb, g2b, NT)
        db2 = (da2 * mask).astype(BF16)
        dg2s[i] = -mm(a2, dyb, TN)
        dxq = mm(dyb, w2, NN) + mm(db2, x2b, NN)
        dx2s[i] = mm(db2, xqb, TN)
        dzq = (dxq * gq).astype(BF16)
        da1 = -mm(dzq, g1b, NT)
        db1 = (da1 * mask).astype(BF16)
        dg1s[i] = -mm(a1, dzq, TN)
        dq = d_o + mm(dzq, w1, NT) + mm(db1, kb, NN)
        os[at, 0:hd] = dq.astype(BF16)
        dks[i] = mm(db1, qb, TN)
        de = jnp.sum(jnp.where(causal, da2 * b2 + da1 * b1, 0.0), axis=0, keepdims=True)
        des[i] = padded(jnp.broadcast_to(de, (8, MB)))
        x2s[i] = x2b
        g1s[i] = g1
        pgs[i] = p * gg1
        gfs[i] = g1f
        xqs[i] = xqb
        zqs[i] = dzq
        dys[i] = dyb
        ns[i] = n
        rs[i] = r
        ss[i] = jnp.broadcast_to(s, (MB, hd))
        cs[i] = jnp.broadcast_to(cc, (MB, hd))
        g2s[i] = g2

    def backward(i):
        at = at_block(i)
        q, k = qs[at, :], ks[at, :]
        e = to_column(es[i][0:1, 0:MB])
        w1, w2 = w1b[i], w2b[i]
        d1, d2 = w1c[...].astype(BF16), w2c[...].astype(BF16)
        x2b, g1, g1f, g2 = x2s[i], g1s[i], gfs[i], g2s[i]
        n, s, cc = ns[i], ss[i], cs[i]
        dh1 = -mm(k, d1, NN)
        dh2 = -mm(x2b, d2, NT)
        dg1 = dg1s[i] + e * dh1
        dp = (dg1 * g1).astype(BF16)
        dg2 = dg2s[i] + e * dh2 + mm(dp, w2, NT)
        dt = s * dg2
        mt = mean(dt * n)
        dr = dt - mean(dt) - n * mt
        dn = dr - cc * dt - rs[i] * mt
        du = s * (dn - mean(dn) - n * (mean(dn * n) + mean(dg2 * g2)))
        dub = du.astype(BF16)
        mixed = jnp.concatenate([(-e * g2).astype(BF16), dub], axis=1)
        dx2 = dx2s[i] + mm(mixed, jnp.concatenate([d2, w2], axis=0), NN)
        dz1 = (dg1 * pgs[i] + dx2 * g1).astype(BF16)
        mixed = jnp.concatenate([(-e * g1f).astype(BF16), dz1], axis=1)
        dk = dks[i] + dr + mm(mixed, jnp.concatenate([d1, w1], axis=1), NT)
        w1c[...] = w1c[...] + mm(
            jnp.concatenate([q, k], axis=0), jnp.concatenate([zqs[i], dz1], axis=0), TN
        )
        w2c[...] = w2c[...] + mm(
            jnp.concatenate([dys[i].astype(F32), du, g2], axis=0),
            jnp.concatenate([xqs[i], x2b, dp], axis=0),
            TN,
        )
        extra = jnp.sum(g1f * dh1, axis=1, keepdims=True) + jnp.sum(
            g2 * dh2, axis=1, keepdims=True
        )
        line = (des[i][0:1, 0:MB] + to_line(extra)) * sg[i][0:1, 0:MB]
        lg[i] = padded(jnp.broadcast_to(line, (8, MB)))
        os[at, hd : 2 * hd] = dk.astype(BF16)
        os[at, 2 * hd : 3 * hd] = (-dr).astype(BF16)

    def loop(step, order):
        if blocks <= UNROLL_LIMIT:
            for i in range(blocks):
                step(order(i))
        else:
            lax.fori_loop(0, blocks, lambda i, unused: (step(order(i)), unused)[1], 0)

    loop(forward, lambda i: i)
    w1c[...] = jnp.zeros_like(w1c)
    w2c[...] = jnp.zeros_like(w2c)
    loop(backward, lambda i: blocks - 1 - i)

    at = pl.ds(pl.multiple_of(place * rows, rows), rows)
    res_ref[0:rows, :] = os[at, :]
    res_ref[rows:, :] = jnp.zeros((EXTRA, 4 * hd), BF16)
    first_row = lax.broadcasted_iota(jnp.int32, (EXTRA, rows), 0) == 0
    lines = jnp.concatenate([lg[place * per + b][0:1, 0:MB] for b in range(per)], axis=1)
    lines = jnp.where(first_row, jnp.broadcast_to(lines, (EXTRA, rows)), 0.0)
    res_ref[rows:, 0:rows] = lines.astype(BF16)

    part = dw_refs[0].shape[0]
    ws[:, 0:hd] = w1c[...].T
    ws[:, hd : 2 * hd] = w2c[...].T
    for d in range(dps):
        first = (place * dps + mate(place_ref[2], d, dps)) * part
        dw_refs[d][...] = ws[pl.ds(pl.multiple_of(first, part), part), :]


def output_kernel(seqs, heads, dps, share, place_ref, *refs):
    got, refs = refs[0], refs[1:]
    o_refs, w_refs = refs[: seqs * dps], refs[seqs * dps : 2 * seqs * dps]
    out_ref, dtok_ref, out_s, grad_s = refs[2 * seqs * dps :]
    hd = o_refs[0].shape[1]
    rows, features = out_ref.shape
    depth = features // share
    out_s[...] = jnp.zeros_like(out_s)
    grad_s[...] = jnp.zeros_like(grad_s)
    for j in range(seqs):
        for d in range(dps):
            at = j * dps + d
            h, r = owner_of(place_ref, seqs, dps, share, j, d)
            out_s[r] = out_s[r] + mm(got[h, 0:rows, 3 * hd :], o_refs[at][0:depth, :], NT)
            line = rate_line(o_refs[at][depth:, :], depth)
            logit = got[h, rows:, 0:rows].astype(F32).T
            w = w_refs[at]
            wide = jnp.concatenate([w[c * depth : (c + 1) * depth, :] for c in range(3)], axis=1)
            grad = mm(logit, jnp.broadcast_to(line, (EXTRA, depth)), NN)
            grad_s[r] = grad_s[r] + grad + mm(got[h, 0:rows, 0 : 3 * hd], wide, NT)
    for r in range(share):
        out_ref[:, r * depth : (r + 1) * depth] = out_s[r].astype(BF16)
        dtok_ref[:, r * depth : (r + 1) * depth] = grad_s[r].astype(BF16)


VMEM = pl.BlockSpec(memory_space=pltpu.VMEM)
SMEM = pl.BlockSpec(memory_space=pltpu.SMEM)
PARAMS = pltpu.CompilerParams(vmem_limit_bytes=48 * 1024 * 1024)


def call(kernel, outs, operands, scratch=()):
    return pl.pallas_call(
        kernel,
        out_shape=outs,
        in_specs=[SMEM] + [VMEM] * (len(operands) - 1),
        out_specs=jax.tree.map(lambda unused: VMEM, outs),
        scratch_shapes=list(scratch),
        compiler_params=PARAMS,
    )(*operands)


def body(tokens, w_qkv, w_lr, w_out, w1_init, w2_init, d_out):
    seqs, heads, dps = (lax.axis_size(a) for a in ("seq", "head", "dp"))
    share = seqs * dps // heads
    rows, features = tokens.shape[1:]
    depth, unused, hd = w_qkv.shape
    inner = w1_init.shape[2]
    blocks = seqs * rows // MB
    place = jnp.stack([lax.axis_index(a).astype(jnp.int32) for a in ("seq", "head", "dp")])
    sizes = (seqs, heads, dps, share)

    pairs = []
    for seq in range(seqs):
        for head in range(heads):
            for dp in range(dps):
                k = seq * dps + dp
                target = head * share + k % share
                to = ((target // dps) * heads + k // share) * dps + target % dps
                pairs.append(((seq * heads + head) * dps + dp, to))

    def swapped(array):
        return lax.ppermute(array, ("seq", "head", "dp"), pairs)

    count = depth // 128
    lines = jnp.pad(
        w_lr[:, 0].reshape(seqs * dps, count, 128), ((0, 0), (0, EXTRA - count), (0, 0))
    )

    def summed(arrays):
        return functools.reduce(lambda a, b: a + b, [a.astype(F32) for a in arrays])

    own = lax.axis_index("seq") * dps + lax.axis_index("dp")
    line = lax.dynamic_index_in_dim(lines, own, 0, keepdims=False)
    kinds = w_qkv.transpose(1, 0, 2).reshape(3 * depth, hd)

    near = [kinds, hop(kinds, "dp", 1), hop(kinds, "dp", 2)]
    outer_w = swapped(jnp.concatenate([w_out, line], axis=0))
    outer_near = peers_of(outer_w, "dp")
    own_tokens, outer_w, lines = lax.optimization_barrier((tokens[0], outer_w, lines))
    features_of = gathered(own_tokens, "head")

    *outer_near, far = lax.optimization_barrier((*outer_near, kinds))
    near += [hop(far, "dp", j) for j in range(3, dps)]
    outer_ws = over_seq(outer_near)
    outer_part = call(
        functools.partial(outer_kernel, *sizes),
        (jax.ShapeDtypeStruct((rows, hd), BF16),) * heads,
        (place, d_out[0], *outer_ws),
        [pltpu.VMEM((share, rows, depth), BF16), pltpu.VMEM((heads, rows, hd), F32)],
    )
    outer_back = sent_to(outer_part, "head")

    head_ws = over_seq(near)
    features_of, swap = lax.optimization_barrier((features_of, kinds))
    swap = swapped(swap)
    projected = call(
        functools.partial(projection_kernel, *sizes),
        jax.ShapeDtypeStruct((rows + 8, 3 * hd), F32),
        (place, features_of, *head_ws, lines),
        [pltpu.VMEM((seqs * dps, rows, depth), BF16)],
    )
    inner_all = peers_of(projected, "seq")
    outer_all = peers_of(summed(outer_back), "seq")

    long = seqs * rows
    scratch = (
        [pltpu.VMEM((long, hd), F32)] * 4
        + [pltpu.VMEM((blocks, 8, 2 * MB), F32)] * 2
        + [pltpu.VMEM((long, 4 * hd), BF16), pltpu.VMEM((blocks, 8, 2 * MB), F32)]
        + [pltpu.VMEM((hd, inner), F32)] * 2
        + [pltpu.VMEM((blocks, hd, inner), BF16)] * 2
        + [pltpu.VMEM((blocks, MB, inner), t) for t in (BF16, F32, F32, F32, BF16, BF16, F32, F32)]
        + [pltpu.VMEM((blocks, MB, hd), t) for t in (BF16, F32, F32, F32, F32, F32, F32, F32)]
        + [pltpu.VMEM((blocks, 8, 2 * MB), F32), pltpu.VMEM((inner, 2 * hd), F32)]
    )
    part = inner // (seqs * dps)
    result, *d_inner = call(
        functools.partial(inner_kernel, seqs, dps),
        (jax.ShapeDtypeStruct((rows + EXTRA, 4 * hd), BF16),)
        + (jax.ShapeDtypeStruct((part, 2 * hd), F32),) * dps,
        (place, *inner_all, *outer_all, w1_init[0], w2_init[0]),
        scratch,
    )
    result, swap = lax.optimization_barrier((result, swap))
    got = gathered(result, "head")
    swap_near = peers_of(swap, "dp")
    inner_ws = over_seq(swap_near)
    unused, *d_inner = lax.optimization_barrier((swap_near[1], *d_inner))
    shares = summed(sent_to(d_inner, "dp"))
    out, d_tokens = call(
        functools.partial(output_kernel, *sizes),
        (jax.ShapeDtypeStruct((rows, features), BF16),) * 2,
        (place, got, *outer_ws, *inner_ws),
        [
            pltpu.VMEM((share, rows, depth), F32),
            pltpu.VMEM((share, rows, depth), F32),
        ],
    )
    return (out[None], d_tokens[None], shares[:, :hd].transpose(1, 0)[None], shares[:, hd:][None])


def solution(mesh):
    placed = (
        P("dp", "seq", "head"),
        P(("seq", "dp"), None, "head"),
        P(None, "head"),
        P(("seq", "dp"), "head"),
        P("head", None, None),
        P("head", None, None),
        P("dp", "seq", "head"),
    )
    return jax.shard_map(
        body,
        mesh=mesh,
        in_specs=placed,
        out_specs=(
            P("dp", "seq", "head"),
            P("dp", "seq", "head"),
            P("head", None, ("seq", "dp")),
            P("head", ("seq", "dp"), None),
        ),
        check_vma=False,
    )
```

```python
import functools

import jax
import jax.numpy as jnp
from jax import lax
from jax.experimental import pallas as pl
from jax.experimental.pallas import tpu as pltpu
from jax.sharding import PartitionSpec as P

MB = 64
EPSILON = 1e-06
BASE_RATE = 0.1
GELU_SCALE = 0.7978845608028654
GELU_CUBIC = 0.044715
NN = ((1,), (0,))
NT = ((1,), (1,))
TN = ((0,), (0,))
EXTRA = 16
UNROLL_LIMIT = 8
F32 = jnp.float32
BF16 = jnp.bfloat16


def mm(left, right, dims):
    return lax.dot_general(
        left.astype(BF16), right.astype(BF16), (dims, ((), ())), preferred_element_type=F32
    )


def padded(lines):
    return jnp.concatenate([lines, jnp.zeros_like(lines)], axis=1)


def mean(rows):
    return jnp.mean(rows, axis=-1, keepdims=True)


def gelu_parts(v):
    square = v * v
    bend = jnp.tanh(v * (GELU_SCALE + (GELU_SCALE * GELU_CUBIC) * square))
    half = 0.5 + 0.5 * bend
    slope = GELU_SCALE + (3.0 * GELU_SCALE * GELU_CUBIC) * square
    bell = 0.5 - 0.5 * bend * bend
    lean = bell * slope
    second = 2.0 * lean * (1.0 - v * bend * slope) + (6.0 * GELU_SCALE * GELU_CUBIC) * square * bell
    return v * half, half + v * lean, second


def gelu_two(v):
    square = v * v
    bend = jnp.tanh(v * (GELU_SCALE + (GELU_SCALE * GELU_CUBIC) * square))
    half = 0.5 + 0.5 * bend
    slope = GELU_SCALE + (3.0 * GELU_SCALE * GELU_CUBIC) * square
    return v * half, half + v * ((0.5 - 0.5 * bend * bend) * slope)


def mate(index, step, count):
    if count & (count - 1) == 0:
        return index ^ step
    return (index + step) % count


def hop(array, axis, step):
    count = lax.axis_size(axis)
    return lax.ppermute(array, axis, [(mate(i, step, count), i) for i in range(count)])


def peers_of(array, axis):
    return [array] + [hop(array, axis, j) for j in range(1, lax.axis_size(axis))]


def sent_to(arrays, axis):
    count = lax.axis_size(axis)
    back = [arrays[0]]
    for j in range(1, count):
        back.append(lax.ppermute(arrays[j], axis, [(i, mate(i, j, count)) for i in range(count)]))
    return back


def gathered(array, axis):
    count = lax.axis_size(axis)
    return lax.all_to_all(jnp.broadcast_to(array[None], (count,) + array.shape), axis, 0, 0)


def over_seq(near):
    return sum([list(pieces) for pieces in zip(*[peers_of(piece, "seq") for piece in near])], [])


def owner_of(place_ref, seqs, dps, share, j, d):
    seq, dp = place_ref[0], place_ref[2]
    k = mate(seq, j, seqs) * dps + mate(dp, d, dps)
    return k // share, k % share


def rate_line(block, depth):
    rows = block.astype(F32)
    return jnp.concatenate([rows[i : i + 1, :] for i in range(depth // 128)], axis=1)


def outer_kernel(seqs, heads, dps, share, place_ref, dout_ref, *refs):
    w_refs = refs[: seqs * dps]
    out_refs = refs[seqs * dps : seqs * dps + heads]
    dout_s, acc = refs[seqs * dps + heads :]
    rows, features = dout_ref.shape
    depth = features // share
    for r in range(share):
        dout_s[r] = dout_ref[:, r * depth : (r + 1) * depth]
    acc[...] = jnp.zeros_like(acc)
    for j in range(seqs):
        for d in range(dps):
            h, r = owner_of(place_ref, seqs, dps, share, j, d)
            acc[h] = acc[h] + mm(dout_s[r], w_refs[j * dps + d][0:depth, :], NN)
    for j in range(heads):
        out_refs[j][...] = acc[mate(place_ref[1], j, heads)].astype(BF16)


def projection_kernel(seqs, heads, dps, share, place_ref, *refs):
    tok_ref, refs = refs[0], refs[1:]
    w_refs, rate_ref, out_ref, tok_s = refs[: seqs * dps], *refs[seqs * dps :]
    unused, rows, features = tok_ref.shape
    depth = features // share
    for h in range(heads):
        for r in range(share):
            tok_s[h * share + r] = tok_ref[h, :, r * depth : (r + 1) * depth]
    total = None
    logit = None
    for j in range(seqs):
        for d in range(dps):
            w = w_refs[j * dps + d]
            h, r = owner_of(place_ref, seqs, dps, share, j, d)
            k = h * share + r
            tok = tok_s[k]
            wide = jnp.concatenate([w[c * depth : (c + 1) * depth, :] for c in range(3)], axis=1)
            term = mm(tok, wide, NN)
            line = mm(jnp.broadcast_to(rate_line(rate_ref[k], depth), (EXTRA, depth)), tok, NT)
            total = term if total is None else total + term
            logit = line if logit is None else logit + line
    out_ref[0:rows, :] = total
    out_ref[rows:, :] = jnp.concatenate([logit[0:8]] * (total.shape[1] // rows), axis=1)


def inner_kernel(seqs, dps, place_ref, *refs):
    x_refs, y_refs = refs[:seqs], refs[seqs : 2 * seqs]
    w1_ref, w2_ref, res_ref = refs[2 * seqs : 2 * seqs + 3]
    dw_refs = refs[2 * seqs + 3 : 2 * seqs + 3 + dps]
    (
        qs, ks, vs, ds, es, sg, os, lg,
        w1c, w2c, w1b, w2b,
        x2s, g1s, pgs, gfs, xqs, zqs, dx2s, dg1s,
        dys, ns, rs, ss, cs, g2s, dg2s, dks, des, ws,
    ) = refs[2 * seqs + 3 + dps :]
    rows = y_refs[0].shape[0]
    hd = y_refs[0].shape[1]
    blocks = seqs * rows // MB
    per = rows // MB
    place = place_ref[0]

    for j in range(seqs):
        owner = mate(place, j, seqs)
        at = pl.ds(pl.multiple_of(owner * rows, rows), rows)
        qs[at, :] = x_refs[j][0:rows, 0:hd]
        ks[at, :] = x_refs[j][0:rows, hd : 2 * hd]
        vs[at, :] = x_refs[j][0:rows, 2 * hd : 3 * hd]
        ds[at, :] = y_refs[j][...]
        gate = jax.nn.sigmoid(x_refs[j][rows:, 0:rows])
        scaled = (BASE_RATE / hd) * gate
        for b in range(per):
            es[owner * per + b] = padded(scaled[:, b * MB : (b + 1) * MB])
            sg[owner * per + b] = padded((scaled * (1.0 - gate))[:, b * MB : (b + 1) * MB])

    w1c[...] = w1_ref[...]
    start = w2_ref[...]
    w2c[...] = (start - mean(start)).T

    at_row = lax.broadcasted_iota(jnp.int32, (MB, MB), 0)
    at_col = lax.broadcasted_iota(jnp.int32, (MB, MB), 1)
    causal = at_col <= at_row
    diagonal = at_col == at_row

    def to_column(line):
        return jnp.sum(jnp.where(diagonal, line, 0.0), axis=1, keepdims=True)

    def to_line(column):
        return jnp.sum(jnp.where(diagonal, column, 0.0), axis=0, keepdims=True)

    def at_block(i):
        if isinstance(i, int):
            return slice(i * MB, (i + 1) * MB)
        return pl.ds(pl.multiple_of(i * MB, MB), MB)

    def forward(i):
        at = at_block(i)
        q, k, v, d_o = qs[at, :], ks[at, :], vs[at, :], ds[at, :]
        line = es[i][0:1, 0:MB]
        e = to_column(line)
        mask = jnp.where(causal, line, 0.0)
        w1 = w1c[...].astype(BF16)
        w2 = w2c[...].astype(BF16)
        w1b[i] = w1
        w2b[i] = w2
        kb, qb = k.astype(BF16), q.astype(BF16)
        gap = v - k
        gap = gap - mean(gap)
        both = mm(jnp.concatenate([kb, qb], axis=0), w1, NN)
        x2, g1, gg1 = gelu_parts(both[:MB])
        x2b = x2.astype(BF16)
        c = mm(x2b, w2, NT)
        var = mean(c * c)
        cross = mean(gap * c)
        s = lax.rsqrt(var + EPSILON)
        n = c * s
        cc = var * s * s - s * cross
        r = n - gap
        g2 = s * (r - n * cc)
        g2b = g2.astype(BF16)
        p = mm(g2b, w2, NN)
        g1f = p * g1
        w1c[...] = w1c[...] - mm(k, e * g1f, TN)
        w2c[...] = w2c[...] - mm(e * g2, x2b, TN)
        g1b = g1f.astype(BF16)
        b1 = mm(qb, kb, NT)
        a1 = (b1 * mask).astype(BF16)
        zq = both[MB:] - mm(a1, g1b, NN)
        xq, gq = gelu_two(zq)
        xqb = xq.astype(BF16)
        b2 = mm(xqb, x2b, NT)
        a2 = (b2 * mask).astype(BF16)
        y = mm(xqb, w2, NT) - mm(a2, g2b, NN)
        sq = lax.rsqrt(mean(y * y) + EPSILON)
        nq = y * sq
        os[at, 3 * hd : 4 * hd] = (q + nq).astype(BF16)
        dy = sq * (d_o - mean(d_o) - nq * mean(d_o * nq))
        dyb = dy.astype(BF16)
        da2 = -mm(dyb, g2b, NT)
        db2 = (da2 * mask).astype(BF16)
        dg2s[i] = -mm(a2, dyb, TN)
        dxq = mm(dyb, w2, NN) + mm(db2, x2b, NN)
        dx2s[i] = mm(db2, xqb, TN)
        dzq = (dxq * gq).astype(BF16)
        da1 = -mm(dzq, g1b, NT)
        db1 = (da1 * mask).astype(BF16)
        dg1s[i] = -mm(a1, dzq, TN)
        dq = d_o + mm(dzq, w1, NT) + mm(db1, kb, NN)
        os[at, 0:hd] = dq.astype(BF16)
        dks[i] = mm(db1, qb, TN)
        de = jnp.sum(jnp.where(causal, da2 * b2 + da1 * b1, 0.0), axis=0, keepdims=True)
        des[i] = padded(jnp.broadcast_to(de, (8, MB)))
        x2s[i] = x2b
        g1s[i] = g1
        pgs[i] = p * gg1
        gfs[i] = g1f
        xqs[i] = xqb
        zqs[i] = dzq
        dys[i] = dyb
        ns[i] = n
        rs[i] = r
        ss[i] = jnp.broadcast_to(s, (MB, hd))
        cs[i] = jnp.broadcast_to(cc, (MB, hd))
        g2s[i] = g2

    def backward(i):
        at = at_block(i)
        q, k = qs[at, :], ks[at, :]
        e = to_column(es[i][0:1, 0:MB])
        w1, w2 = w1b[i], w2b[i]
        d1, d2 = w1c[...].astype(BF16), w2c[...].astype(BF16)
        x2b, g1, g1f, g2 = x2s[i], g1s[i], gfs[i], g2s[i]
        n, s, cc = ns[i], ss[i], cs[i]
        dh1 = -mm(k, d1, NN)
        dh2 = -mm(x2b, d2, NT)
        dg1 = dg1s[i] + e * dh1
        dp = (dg1 * g1).astype(BF16)
        dg2 = dg2s[i] + e * dh2 + mm(dp, w2, NT)
        dt = s * dg2
        mt = mean(dt * n)
        dr = dt - mean(dt) - n * mt
        dn = dr - cc * dt - rs[i] * mt
        du = s * (dn - mean(dn) - n * (mean(dn * n) + mean(dg2 * g2)))
        dub = du.astype(BF16)
        mixed = jnp.concatenate([(-e * g2).astype(BF16), dub], axis=1)
        dx2 = dx2s[i] + mm(mixed, jnp.concatenate([d2, w2], axis=0), NN)
        dz1 = (dg1 * pgs[i] + dx2 * g1).astype(BF16)
        mixed = jnp.concatenate([(-e * g1f).astype(BF16), dz1], axis=1)
        dk = dks[i] + dr + mm(mixed, jnp.concatenate([d1, w1], axis=1), NT)
        w1c[...] = w1c[...] + mm(
            jnp.concatenate([q, k], axis=0), jnp.concatenate([zqs[i], dz1], axis=0), TN
        )
        w2c[...] = w2c[...] + mm(
            jnp.concatenate([dys[i].astype(F32), du, g2], axis=0),
            jnp.concatenate([xqs[i], x2b, dp], axis=0),
            TN,
        )
        extra = jnp.sum(g1f * dh1, axis=1, keepdims=True) + jnp.sum(
            g2 * dh2, axis=1, keepdims=True
        )
        line = (des[i][0:1, 0:MB] + to_line(extra)) * sg[i][0:1, 0:MB]
        lg[i] = padded(jnp.broadcast_to(line, (8, MB)))
        os[at, hd : 2 * hd] = dk.astype(BF16)
        os[at, 2 * hd : 3 * hd] = (-dr).astype(BF16)

    def loop(step, order):
        if blocks <= UNROLL_LIMIT:
            for i in range(blocks):
                step(order(i))
        else:
            lax.fori_loop(0, blocks, lambda i, unused: (step(order(i)), unused)[1], 0)

    loop(forward, lambda i: i)
    w1c[...] = jnp.zeros_like(w1c)
    w2c[...] = jnp.zeros_like(w2c)
    loop(backward, lambda i: blocks - 1 - i)

    at = pl.ds(pl.multiple_of(place * rows, rows), rows)
    res_ref[0:rows, :] = os[at, :]
    res_ref[rows:, :] = jnp.zeros((EXTRA, 4 * hd), BF16)
    first_row = lax.broadcasted_iota(jnp.int32, (EXTRA, rows), 0) == 0
    lines = jnp.concatenate([lg[place * per + b][0:1, 0:MB] for b in range(per)], axis=1)
    lines = jnp.where(first_row, jnp.broadcast_to(lines, (EXTRA, rows)), 0.0)
    res_ref[rows:, 0:rows] = lines.astype(BF16)

    part = dw_refs[0].shape[0]
    ws[:, 0:hd] = w1c[...].T
    ws[:, hd : 2 * hd] = w2c[...].T
    for d in range(dps):
        first = (place * dps + mate(place_ref[2], d, dps)) * part
        dw_refs[d][...] = ws[pl.ds(pl.multiple_of(first, part), part), :]


def output_kernel(seqs, heads, dps, share, place_ref, *refs):
    got_refs, refs = refs[:heads], refs[heads:]
    o_refs, w_refs = refs[: seqs * dps], refs[seqs * dps : 2 * seqs * dps]
    out_ref, dtok_ref, got, out_s, grad_s = refs[2 * seqs * dps :]
    hd = o_refs[0].shape[1]
    rows, features = out_ref.shape
    depth = features // share
    for j in range(heads):
        got[mate(place_ref[1], j, heads)] = got_refs[j][...]
    out_s[...] = jnp.zeros_like(out_s)
    grad_s[...] = jnp.zeros_like(grad_s)
    for j in range(seqs):
        for d in range(dps):
            at = j * dps + d
            h, r = owner_of(place_ref, seqs, dps, share, j, d)
            out_s[r] = out_s[r] + mm(got[h, 0:rows, 3 * hd :], o_refs[at][0:depth, :], NT)
            line = rate_line(o_refs[at][depth:, :], depth)
            logit = got[h, rows:, 0:rows].astype(F32).T
            w = w_refs[at]
            wide = jnp.concatenate([w[c * depth : (c + 1) * depth, :] for c in range(3)], axis=1)
            grad = mm(logit, jnp.broadcast_to(line, (EXTRA, depth)), NN)
            grad_s[r] = grad_s[r] + grad + mm(got[h, 0:rows, 0 : 3 * hd], wide, NT)
    for r in range(share):
        out_ref[:, r * depth : (r + 1) * depth] = out_s[r].astype(BF16)
        dtok_ref[:, r * depth : (r + 1) * depth] = grad_s[r].astype(BF16)


VMEM = pl.BlockSpec(memory_space=pltpu.VMEM)
SMEM = pl.BlockSpec(memory_space=pltpu.SMEM)
PARAMS = pltpu.CompilerParams(vmem_limit_bytes=48 * 1024 * 1024)


def call(kernel, outs, operands, scratch=()):
    return pl.pallas_call(
        kernel,
        out_shape=outs,
        in_specs=[SMEM] + [VMEM] * (len(operands) - 1),
        out_specs=jax.tree.map(lambda unused: VMEM, outs),
        scratch_shapes=list(scratch),
        compiler_params=PARAMS,
    )(*operands)


def body(tokens, w_qkv, w_lr, w_out, w1_init, w2_init, d_out):
    seqs, heads, dps = (lax.axis_size(a) for a in ("seq", "head", "dp"))
    share = seqs * dps // heads
    rows, features = tokens.shape[1:]
    depth, unused, hd = w_qkv.shape
    inner = w1_init.shape[2]
    blocks = seqs * rows // MB
    place = jnp.stack([lax.axis_index(a).astype(jnp.int32) for a in ("seq", "head", "dp")])
    sizes = (seqs, heads, dps, share)

    pairs = []
    for seq in range(seqs):
        for head in range(heads):
            for dp in range(dps):
                k = seq * dps + dp
                target = head * share + k % share
                to = ((target // dps) * heads + k // share) * dps + target % dps
                pairs.append(((seq * heads + head) * dps + dp, to))

    def swapped(array):
        return lax.ppermute(array, ("seq", "head", "dp"), pairs)

    count = depth // 128
    lines = jnp.pad(
        w_lr[:, 0].reshape(seqs * dps, count, 128), ((0, 0), (0, EXTRA - count), (0, 0))
    )

    def summed(arrays):
        return functools.reduce(lambda a, b: a + b, [a.astype(F32) for a in arrays])

    own = lax.axis_index("seq") * dps + lax.axis_index("dp")
    line = lax.dynamic_index_in_dim(lines, own, 0, keepdims=False)
    kinds = w_qkv.transpose(1, 0, 2).reshape(3 * depth, hd)

    near = peers_of(kinds, "dp")
    outer_w = swapped(jnp.concatenate([w_out, line], axis=0))
    swap = swapped(kinds)
    outer_near = peers_of(outer_w, "dp")
    own_tokens, swap, lines = lax.optimization_barrier((tokens[0], swap, lines))
    features_of = gathered(own_tokens, "head")
    *outer_near, swap = lax.optimization_barrier((*outer_near, swap))
    outer_ws = over_seq(outer_near)
    inner_ws = over_seq(peers_of(swap, "dp"))

    outer_part = call(
        functools.partial(outer_kernel, *sizes),
        (jax.ShapeDtypeStruct((rows, hd), BF16),) * heads,
        (place, d_out[0], *outer_ws),
        [pltpu.VMEM((share, rows, depth), BF16), pltpu.VMEM((heads, rows, hd), F32)],
    )
    outer_back = sent_to(outer_part, "head")

    head_ws = over_seq(near)
    projected = call(
        functools.partial(projection_kernel, *sizes),
        jax.ShapeDtypeStruct((rows + 8, 3 * hd), F32),
        (place, features_of, *head_ws, lines),
        [pltpu.VMEM((seqs * dps, rows, depth), BF16)],
    )
    inner_all = peers_of(projected, "seq")
    outer_all = peers_of(summed(outer_back), "seq")

    long = seqs * rows
    scratch = (
        [pltpu.VMEM((long, hd), F32)] * 4
        + [pltpu.VMEM((blocks, 8, 2 * MB), F32)] * 2
        + [pltpu.VMEM((long, 4 * hd), BF16), pltpu.VMEM((blocks, 8, 2 * MB), F32)]
        + [pltpu.VMEM((hd, inner), F32)] * 2
        + [pltpu.VMEM((blocks, hd, inner), BF16)] * 2
        + [pltpu.VMEM((blocks, MB, inner), t) for t in (BF16, F32, F32, F32, BF16, BF16, F32, F32)]
        + [pltpu.VMEM((blocks, MB, hd), t) for t in (BF16, F32, F32, F32, F32, F32, F32, F32)]
        + [pltpu.VMEM((blocks, 8, 2 * MB), F32), pltpu.VMEM((inner, 2 * hd), F32)]
    )
    part = inner // (seqs * dps)
    result, *d_inner = call(
        functools.partial(inner_kernel, seqs, dps),
        (jax.ShapeDtypeStruct((rows + EXTRA, 4 * hd), BF16),)
        + (jax.ShapeDtypeStruct((part, 2 * hd), F32),) * dps,
        (place, *inner_all, *outer_all, w1_init[0], w2_init[0]),
        scratch,
    )
    got = peers_of(result, "head")
    unused, *d_inner = lax.optimization_barrier((got[1], *d_inner))
    shares = summed(sent_to(d_inner, "dp"))
    out, d_tokens = call(
        functools.partial(output_kernel, *sizes),
        (jax.ShapeDtypeStruct((rows, features), BF16),) * 2,
        (place, *got, *outer_ws, *inner_ws),
        [
            pltpu.VMEM((heads, rows + EXTRA, 4 * hd), BF16),
            pltpu.VMEM((share, rows, depth), F32),
            pltpu.VMEM((share, rows, depth), F32),
        ],
    )
    return (out[None], d_tokens[None], shares[:, :hd].transpose(1, 0)[None], shares[:, hd:][None])


def solution(mesh):
    placed = (
        P("dp", "seq", "head"),
        P(("seq", "dp"), None, "head"),
        P(None, "head"),
        P(("seq", "dp"), "head"),
        P("head", None, None),
        P("head", None, None),
        P("dp", "seq", "head"),
    )
    return jax.shard_map(
        body,
        mesh=mesh,
        in_specs=placed,
        out_specs=(
            P("dp", "seq", "head"),
            P("dp", "seq", "head"),
            P("head", None, ("seq", "dp")),
            P("head", ("seq", "dp"), None),
        ),
        check_vma=False,
    )
```

```python
import functools

import jax
import jax.numpy as jnp
from jax import lax
from jax.experimental import pallas as pl
from jax.experimental.pallas import tpu as pltpu
from jax.sharding import PartitionSpec as P

MB = 64
EPSILON = 1e-06
BASE_RATE = 0.1
GELU_SCALE = 0.7978845608028654
GELU_CUBIC = 0.044715
NN = ((1,), (0,))
NT = ((1,), (1,))
TN = ((0,), (0,))
EXTRA = 16
UNROLL_LIMIT = 8
F32 = jnp.float32
BF16 = jnp.bfloat16


def mm(left, right, dims):
    return lax.dot_general(
        left.astype(BF16), right.astype(BF16), (dims, ((), ())), preferred_element_type=F32
    )


def padded(lines):
    return jnp.concatenate([lines, jnp.zeros_like(lines)], axis=1)


def mean(rows):
    return jnp.mean(rows, axis=-1, keepdims=True)


def gelu_parts(v):
    square = v * v
    bend = jnp.tanh(v * (GELU_SCALE + (GELU_SCALE * GELU_CUBIC) * square))
    half = 0.5 + 0.5 * bend
    slope = GELU_SCALE + (3.0 * GELU_SCALE * GELU_CUBIC) * square
    bell = 0.5 - 0.5 * bend * bend
    lean = bell * slope
    second = 2.0 * lean * (1.0 - v * bend * slope) + (6.0 * GELU_SCALE * GELU_CUBIC) * square * bell
    return v * half, half + v * lean, second


def gelu_two(v):
    square = v * v
    bend = jnp.tanh(v * (GELU_SCALE + (GELU_SCALE * GELU_CUBIC) * square))
    half = 0.5 + 0.5 * bend
    slope = GELU_SCALE + (3.0 * GELU_SCALE * GELU_CUBIC) * square
    return v * half, half + v * ((0.5 - 0.5 * bend * bend) * slope)


def mate(index, step, count):
    if count & (count - 1) == 0:
        return index ^ step
    return (index + step) % count


def hop(array, axis, step):
    count = lax.axis_size(axis)
    return lax.ppermute(array, axis, [(mate(i, step, count), i) for i in range(count)])


def peers_of(array, axis):
    return [array] + [hop(array, axis, j) for j in range(1, lax.axis_size(axis))]


def sent_to(arrays, axis):
    count = lax.axis_size(axis)
    back = [arrays[0]]
    for j in range(1, count):
        back.append(lax.ppermute(arrays[j], axis, [(i, mate(i, j, count)) for i in range(count)]))
    return back


def over_seq(near):
    return sum([list(pieces) for pieces in zip(*[peers_of(piece, "seq") for piece in near])], [])


def owner_of(place_ref, seqs, dps, share, j, d):
    seq, dp = place_ref[0], place_ref[2]
    k = mate(seq, j, seqs) * dps + mate(dp, d, dps)
    return k // share, k % share


def rate_line(block, depth):
    rows = block.astype(F32)
    return jnp.concatenate([rows[i : i + 1, :] for i in range(depth // 128)], axis=1)


def outer_kernel(seqs, heads, dps, share, place_ref, tok_ref, dout_ref, *refs):
    w_refs = refs[: seqs * dps]
    out_refs = refs[seqs * dps : seqs * dps + heads]
    tok_s, dout_s, acc = refs[seqs * dps + heads :]
    rows, features = tok_ref.shape
    depth = features // share
    for r in range(share):
        tok_s[r] = tok_ref[:, r * depth : (r + 1) * depth]
        dout_s[r] = dout_ref[:, r * depth : (r + 1) * depth]
    acc[...] = jnp.zeros_like(acc)
    for j in range(seqs):
        for d in range(dps):
            w = w_refs[j * dps + d]
            h, r = owner_of(place_ref, seqs, dps, share, j, d)
            line = rate_line(w[depth:, :], depth)
            logit = mm(jnp.broadcast_to(line, (EXTRA, depth)), tok_s[r], NT)
            back = mm(dout_s[r], w[0:depth, :], NN)
            acc[h] = acc[h] + jnp.concatenate([back, logit], axis=0)
    first_half = lax.broadcasted_iota(jnp.int32, (EXTRA, rows), 0) < EXTRA // 2
    for j in range(heads):
        total = acc[mate(place_ref[1], j, heads)]
        out_refs[j][0:rows, :] = total[0:rows].astype(BF16)
        logit = total[rows:]
        high = logit.astype(BF16).astype(F32)
        out_refs[j][rows:, :] = jnp.where(first_half, high, logit - high).astype(BF16)


def inner_projection_kernel(seqs, heads, dps, share, place_ref, tok_ref, *refs):
    w_refs = refs[: 2 * seqs * dps]
    out_refs = refs[2 * seqs * dps : 2 * seqs * dps + heads]
    tok_s, acc = refs[2 * seqs * dps + heads :]
    rows, features = tok_ref.shape
    depth = features // share
    half = depth // 2
    for r in range(share):
        tok_s[r] = tok_ref[:, r * depth : (r + 1) * depth]
    acc[...] = jnp.zeros_like(acc)
    for part in range(2):
        for j in range(seqs):
            for d in range(dps):
                w = w_refs[(part * seqs + j) * dps + d]
                h, r = owner_of(place_ref, seqs, dps, share, j, d)
                wide = jnp.concatenate([w[c * half : (c + 1) * half, :] for c in range(3)], axis=1)
                acc[h] = acc[h] + mm(tok_s[r][:, part * half : (part + 1) * half], wide, NN)
    for j in range(heads):
        out_refs[j][...] = acc[mate(place_ref[1], j, heads)].astype(BF16)


def inner_kernel(seqs, dps, place_ref, *refs):
    x_refs, y_refs = refs[:seqs], refs[seqs : 2 * seqs]
    w1_ref, w2_ref, res_ref = refs[2 * seqs : 2 * seqs + 3]
    dw_refs = refs[2 * seqs + 3 : 2 * seqs + 3 + dps]
    (
        qs, ks, vs, ds, es, sg, os, lg,
        w1c, w2c, w1b, w2b,
        x2s, g1s, pgs, gfs, xqs, zqs, dx2s, dg1s,
        dys, ns, rs, ss, cs, g2s, dg2s, dks, des, ws,
    ) = refs[2 * seqs + 3 + dps :]
    rows = x_refs[0].shape[0]
    hd = y_refs[0].shape[1]
    width = 4 * hd
    blocks = seqs * rows // MB
    per = rows // MB
    place = place_ref[0]

    for j in range(seqs):
        owner = mate(place, j, seqs)
        at = pl.ds(pl.multiple_of(owner * rows, rows), rows)
        qs[at, :] = x_refs[j][:, 0:hd]
        ks[at, :] = x_refs[j][:, hd : 2 * hd]
        vs[at, :] = x_refs[j][:, 2 * hd : 3 * hd]
        ds[at, :] = y_refs[j][0:rows, :]
        logit = y_refs[j][rows : rows + 8, :] + y_refs[j][rows + 8 : rows + 16, :]
        gate = jax.nn.sigmoid(logit)
        scaled = (BASE_RATE / hd) * gate
        for b in range(per):
            es[owner * per + b] = padded(scaled[:, b * MB : (b + 1) * MB])
            sg[owner * per + b] = padded((scaled * (1.0 - gate))[:, b * MB : (b + 1) * MB])

    w1c[...] = w1_ref[...]
    start = w2_ref[...]
    w2c[...] = (start - mean(start)).T

    at_row = lax.broadcasted_iota(jnp.int32, (MB, MB), 0)
    at_col = lax.broadcasted_iota(jnp.int32, (MB, MB), 1)
    causal = at_col <= at_row
    diagonal = at_col == at_row

    def to_column(line):
        return jnp.sum(jnp.where(diagonal, line, 0.0), axis=1, keepdims=True)

    def to_line(column):
        return jnp.sum(jnp.where(diagonal, column, 0.0), axis=0, keepdims=True)

    def at_block(i):
        if isinstance(i, int):
            return slice(i * MB, (i + 1) * MB)
        return pl.ds(pl.multiple_of(i * MB, MB), MB)

    def forward(i):
        at = at_block(i)
        q, k, v, d_o = qs[at, :], ks[at, :], vs[at, :], ds[at, :]
        line = es[i][0:1, 0:MB]
        e = to_column(line)
        mask = jnp.where(causal, line, 0.0)
        w1 = w1c[...].astype(BF16)
        w2 = w2c[...].astype(BF16)
        w1b[i] = w1
        w2b[i] = w2
        kb, qb = k.astype(BF16), q.astype(BF16)
        gap = v - k
        gap = gap - mean(gap)
        both = mm(jnp.concatenate([kb, qb], axis=0), w1, NN)
        x2, g1, gg1 = gelu_parts(both[:MB])
        x2b = x2.astype(BF16)
        c = mm(x2b, w2, NT)
        var = mean(c * c)
        cross = mean(gap * c)
        s = lax.rsqrt(var + EPSILON)
        n = c * s
        cc = var * s * s - s * cross
        r = n - gap
        g2 = s * (r - n * cc)
        g2b = g2.astype(BF16)
        p = mm(g2b, w2, NN)
        g1f = p * g1
        w1c[...] = w1c[...] - mm(k, e * g1f, TN)
        w2c[...] = w2c[...] - mm(e * g2, x2b, TN)
        g1b = g1f.astype(BF16)
        b1 = mm(qb, kb, NT)
        a1 = (b1 * mask).astype(BF16)
        zq = both[MB:] - mm(a1, g1b, NN)
        xq, gq = gelu_two(zq)
        xqb = xq.astype(BF16)
        b2 = mm(xqb, x2b, NT)
        a2 = (b2 * mask).astype(BF16)
        y = mm(xqb, w2, NT) - mm(a2, g2b, NN)
        sq = lax.rsqrt(mean(y * y) + EPSILON)
        nq = y * sq
        os[at, 3 * hd : 4 * hd] = (q + nq).astype(BF16)
        dy = sq * (d_o - mean(d_o) - nq * mean(d_o * nq))
        dyb = dy.astype(BF16)
        da2 = -mm(dyb, g2b, NT)
        db2 = (da2 * mask).astype(BF16)
        dg2s[i] = -mm(a2, dyb, TN)
        dxq = mm(dyb, w2, NN) + mm(db2, x2b, NN)
        dx2s[i] = mm(db2, xqb, TN)
        dzq = (dxq * gq).astype(BF16)
        da1 = -mm(dzq, g1b, NT)
        db1 = (da1 * mask).astype(BF16)
        dg1s[i] = -mm(a1, dzq, TN)
        dq = d_o + mm(dzq, w1, NT) + mm(db1, kb, NN)
        os[at, 0:hd] = dq.astype(BF16)
        dks[i] = mm(db1, qb, TN)
        de = jnp.sum(jnp.where(causal, da2 * b2 + da1 * b1, 0.0), axis=0, keepdims=True)
        des[i] = padded(jnp.broadcast_to(de, (8, MB)))
        x2s[i] = x2b
        g1s[i] = g1
        pgs[i] = p * gg1
        gfs[i] = g1f
        xqs[i] = xqb
        zqs[i] = dzq
        dys[i] = dyb
        ns[i] = n
        rs[i] = r
        ss[i] = jnp.broadcast_to(s, (MB, hd))
        cs[i] = jnp.broadcast_to(cc, (MB, hd))
        g2s[i] = g2

    def backward(i):
        at = at_block(i)
        q, k = qs[at, :], ks[at, :]
        e = to_column(es[i][0:1, 0:MB])
        w1, w2 = w1b[i], w2b[i]
        d1, d2 = w1c[...].astype(BF16), w2c[...].astype(BF16)
        x2b, g1, g1f, g2 = x2s[i], g1s[i], gfs[i], g2s[i]
        n, s, cc = ns[i], ss[i], cs[i]
        dh1 = -mm(k, d1, NN)
        dh2 = -mm(x2b, d2, NT)
        dg1 = dg1s[i] + e * dh1
        dp = (dg1 * g1).astype(BF16)
        dg2 = dg2s[i] + e * dh2 + mm(dp, w2, NT)
        dt = s * dg2
        mt = mean(dt * n)
        dr = dt - mean(dt) - n * mt
        dn = dr - cc * dt - rs[i] * mt
        du = s * (dn - mean(dn) - n * (mean(dn * n) + mean(dg2 * g2)))
        dub = du.astype(BF16)
        mixed = jnp.concatenate([(-e * g2).astype(BF16), dub], axis=1)
        dx2 = dx2s[i] + mm(mixed, jnp.concatenate([d2, w2], axis=0), NN)
        dz1 = (dg1 * pgs[i] + dx2 * g1).astype(BF16)
        mixed = jnp.concatenate([(-e * g1f).astype(BF16), dz1], axis=1)
        dk = dks[i] + dr + mm(mixed, jnp.concatenate([d1, w1], axis=1), NT)
        w1c[...] = w1c[...] + mm(
            jnp.concatenate([q, k], axis=0), jnp.concatenate([zqs[i], dz1], axis=0), TN
        )
        w2c[...] = w2c[...] + mm(
            jnp.concatenate([dys[i].astype(F32), du, g2], axis=0),
            jnp.concatenate([xqs[i], x2b, dp], axis=0),
            TN,
        )
        extra = jnp.sum(g1f * dh1, axis=1, keepdims=True) + jnp.sum(
            g2 * dh2, axis=1, keepdims=True
        )
        line = (des[i][0:1, 0:MB] + to_line(extra)) * sg[i][0:1, 0:MB]
        lg[i] = padded(jnp.broadcast_to(line, (8, MB)))
        os[at, hd : 2 * hd] = dk.astype(BF16)
        os[at, 2 * hd : 3 * hd] = (-dr).astype(BF16)

    def loop(step, order):
        if blocks <= UNROLL_LIMIT:
            for i in range(blocks):
                step(order(i))
        else:
            lax.fori_loop(0, blocks, lambda i, unused: (step(order(i)), unused)[1], 0)

    loop(forward, lambda i: i)
    w1c[...] = jnp.zeros_like(w1c)
    w2c[...] = jnp.zeros_like(w2c)
    loop(backward, lambda i: blocks - 1 - i)

    res_ref[0:rows, :] = os[pl.ds(pl.multiple_of(place * rows, rows), rows), :]
    res_ref[rows:, :] = jnp.zeros((EXTRA, width), BF16)
    first_row = lax.broadcasted_iota(jnp.int32, (EXTRA, rows), 0) == 0
    lines = jnp.concatenate([lg[place * per + b][0:1, 0:MB] for b in range(per)], axis=1)
    lines = jnp.where(first_row, jnp.broadcast_to(lines, (EXTRA, rows)), 0.0)
    res_ref[rows:, 0:rows] = lines.astype(BF16)

    part = dw_refs[0].shape[0]
    ws[:, 0:hd] = w1c[...].T
    ws[:, hd : 2 * hd] = w2c[...].T
    for d in range(dps):
        first = (place * dps + mate(place_ref[2], d, dps)) * part
        dw_refs[d][...] = ws[pl.ds(pl.multiple_of(first, part), part), :]


def output_kernel(seqs, heads, dps, share, place_ref, *refs):
    got_refs, refs = refs[:heads], refs[heads:]
    o_refs, w_refs = refs[: seqs * dps], refs[seqs * dps : 3 * seqs * dps]
    out_ref, dtok_ref, got, out_s, grad_s = refs[3 * seqs * dps :]
    hd = o_refs[0].shape[1]
    rows, features = out_ref.shape
    depth = features // share
    half = depth // 2
    for j in range(heads):
        got[mate(place_ref[1], j, heads)] = got_refs[j][...]
    out_s[...] = jnp.zeros_like(out_s)
    grad_s[...] = jnp.zeros_like(grad_s)
    for j in range(seqs):
        for d in range(dps):
            o = o_refs[j * dps + d]
            h, r = owner_of(place_ref, seqs, dps, share, j, d)
            out_s[r] = out_s[r] + mm(got[h, 0:rows, 3 * hd :], o[0:depth, :], NT)
            line = rate_line(o[depth:, :], depth)
            logit = got[h, rows:, 0:rows].astype(F32).T
            grad = [mm(logit, jnp.broadcast_to(line, (EXTRA, depth)), NN)]
            mine = got[h, 0:rows, 0 : 3 * hd]
            halves = []
            for part in range(2):
                w = w_refs[(part * seqs + j) * dps + d]
                wide = jnp.concatenate([w[c * half : (c + 1) * half, :] for c in range(3)], axis=1)
                halves.append(mm(mine, wide, NT))
            grad_s[r] = grad_s[r] + grad[0] + jnp.concatenate(halves, axis=1)
    for r in range(share):
        out_ref[:, r * depth : (r + 1) * depth] = out_s[r].astype(BF16)
        dtok_ref[:, r * depth : (r + 1) * depth] = grad_s[r].astype(BF16)


VMEM = pl.BlockSpec(memory_space=pltpu.VMEM)
SMEM = pl.BlockSpec(memory_space=pltpu.SMEM)
PARAMS = pltpu.CompilerParams(vmem_limit_bytes=48 * 1024 * 1024)


def call(kernel, outs, operands, scratch=()):
    return pl.pallas_call(
        kernel,
        out_shape=outs,
        in_specs=[SMEM] + [VMEM] * (len(operands) - 1),
        out_specs=jax.tree.map(lambda unused: VMEM, outs),
        scratch_shapes=list(scratch),
        compiler_params=PARAMS,
    )(*operands)


def body(tokens, w_qkv, w_lr, w_out, w1_init, w2_init, d_out):
    seqs, heads, dps = (lax.axis_size(a) for a in ("seq", "head", "dp"))
    share = seqs * dps // heads
    rows, features = tokens.shape[1:]
    depth, unused, hd = w_qkv.shape
    inner = w1_init.shape[2]
    blocks = seqs * rows // MB
    place = jnp.stack([lax.axis_index(a).astype(jnp.int32) for a in ("seq", "head", "dp")])
    sizes = (seqs, heads, dps, share)

    pairs = []
    for seq in range(seqs):
        for head in range(heads):
            for dp in range(dps):
                k = seq * dps + dp
                target = head * share + k % share
                to = ((target // dps) * heads + k // share) * dps + target % dps
                pairs.append(((seq * heads + head) * dps + dp, to))

    def swapped(array):
        return lax.ppermute(array, ("seq", "head", "dp"), pairs)

    half = depth // 2
    lines = w_lr[:, 0].reshape(seqs * dps, depth // 128, 128)
    line = lax.dynamic_index_in_dim(
        lines, lax.axis_index("seq") * dps + lax.axis_index("dp"), 0, keepdims=False
    )
    line = jnp.pad(line, ((0, EXTRA - depth // 128), (0, 0)))
    outer_w = swapped(jnp.concatenate([w_out, line], axis=0))
    by_kind = w_qkv.transpose(1, 0, 2)
    first_w = swapped(by_kind[:, :half].reshape(3 * half, hd))
    second = by_kind[:, half:].reshape(3 * half, hd)
    second_w = swapped(second)
    outer_near = peers_of(outer_w, "dp")
    first_near = [first_w, hop(first_w, "dp", 1), hop(first_w, "dp", 2)]
    second_w, *outer_near = lax.optimization_barrier((second_w, *outer_near))
    second_near = [second_w, hop(second_w, "dp", 1), hop(second_w, "dp", 2)]
    outer_ws = over_seq(outer_near)
    if dps == 4:
        first_near[1], second_near[2], unused = lax.optimization_barrier(
            (first_near[1], second_near[2], outer_ws[-1])
        )
        first_near.append(hop(first_near[1], "dp", 2))
        second_near.append(hop(second_near[2], "dp", 1))
    else:
        first_near += [hop(first_w, "dp", j) for j in range(3, dps)]
        second_near += [hop(second_w, "dp", j) for j in range(3, dps)]
    inner_ws = over_seq(first_near) + over_seq(second_near)

    def summed(arrays):
        return functools.reduce(lambda a, b: a + b, [a.astype(F32) for a in arrays])

    outer_part = call(
        functools.partial(outer_kernel, *sizes),
        (jax.ShapeDtypeStruct((rows + EXTRA, hd), BF16),) * heads,
        (place, tokens[0], d_out[0], *outer_ws),
        [pltpu.VMEM((share, rows, features // share), BF16)] * 2
        + [pltpu.VMEM((heads, rows + EXTRA, hd), F32)],
    )
    outer_all = peers_of(summed(sent_to(outer_part, "head")), "seq")
    own_tokens, unused = lax.optimization_barrier((tokens[0], outer_part[0]))
    inner_part = call(
        functools.partial(inner_projection_kernel, *sizes),
        (jax.ShapeDtypeStruct((rows, 3 * hd), BF16),) * heads,
        (place, own_tokens, *inner_ws),
        [
            pltpu.VMEM((share, rows, features // share), BF16),
            pltpu.VMEM((heads, rows, 3 * hd), F32),
        ],
    )
    inner_all = peers_of(summed(sent_to(inner_part, "head")), "seq")

    long = seqs * rows
    scratch = (
        [pltpu.VMEM((long, hd), F32)] * 4
        + [pltpu.VMEM((blocks, 8, 2 * MB), F32)] * 2
        + [pltpu.VMEM((long, 4 * hd), BF16), pltpu.VMEM((blocks, 8, 2 * MB), F32)]
        + [pltpu.VMEM((hd, inner), F32)] * 2
        + [pltpu.VMEM((blocks, hd, inner), BF16)] * 2
        + [pltpu.VMEM((blocks, MB, inner), t) for t in (BF16, F32, F32, F32, BF16, BF16, F32, F32)]
        + [pltpu.VMEM((blocks, MB, hd), t) for t in (BF16, F32, F32, F32, F32, F32, F32, F32)]
        + [pltpu.VMEM((blocks, 8, 2 * MB), F32), pltpu.VMEM((inner, 2 * hd), F32)]
    )
    part = inner // (seqs * dps)
    result, *d_inner = call(
        functools.partial(inner_kernel, seqs, dps),
        (jax.ShapeDtypeStruct((rows + EXTRA, 4 * hd), BF16),)
        + (jax.ShapeDtypeStruct((part, 2 * hd), F32),) * dps,
        (place, *inner_all, *outer_all, w1_init[0], w2_init[0]),
        scratch,
    )
    got = peers_of(result, "head")
    unused, *d_inner = lax.optimization_barrier((got[1], *d_inner))
    shares = summed(sent_to(d_inner, "dp"))
    out, d_tokens = call(
        functools.partial(output_kernel, *sizes),
        (jax.ShapeDtypeStruct((rows, features), BF16),) * 2,
        (place, *got, *outer_ws, *inner_ws),
        [
            pltpu.VMEM((heads, rows + EXTRA, 4 * hd), BF16),
            pltpu.VMEM((share, rows, features // share), F32),
            pltpu.VMEM((share, rows, features // share), F32),
        ],
    )
    return (out[None], d_tokens[None], shares[:, :hd].transpose(1, 0)[None], shares[:, hd:][None])


def solution(mesh):
    placed = (
        P("dp", "seq", "head"),
        P(("seq", "dp"), None, "head"),
        P(None, "head"),
        P(("seq", "dp"), "head"),
        P("head", None, None),
        P("head", None, None),
        P("dp", "seq", "head"),
    )
    return jax.shard_map(
        body,
        mesh=mesh,
        in_specs=placed,
        out_specs=(
            P("dp", "seq", "head"),
            P("dp", "seq", "head"),
            P("head", None, ("seq", "dp")),
            P("head", ("seq", "dp"), None),
        ),
        check_vma=False,
    )
```

```python
import functools

import jax
import jax.numpy as jnp
from jax import lax
from jax.experimental import pallas as pl
from jax.experimental.pallas import tpu as pltpu
from jax.sharding import PartitionSpec as P

MB = 64
EPSILON = 1e-06
BASE_RATE = 0.1
GELU_SCALE = 0.7978845608028654
GELU_CUBIC = 0.044715
NN = ((1,), (0,))
NT = ((1,), (1,))
TN = ((0,), (0,))
EXTRA = 16
UNROLL_LIMIT = 8
F32 = jnp.float32
BF16 = jnp.bfloat16


def mm(left, right, dims):
    return lax.dot_general(
        left.astype(BF16), right.astype(BF16), (dims, ((), ())), preferred_element_type=F32
    )


def padded(lines):
    return jnp.concatenate([lines, jnp.zeros_like(lines)], axis=1)


def mean(rows):
    return jnp.mean(rows, axis=-1, keepdims=True)


def gelu_parts(v):
    square = v * v
    bend = jnp.tanh(v * (GELU_SCALE + (GELU_SCALE * GELU_CUBIC) * square))
    half = 0.5 + 0.5 * bend
    slope = GELU_SCALE + (3.0 * GELU_SCALE * GELU_CUBIC) * square
    bell = 0.5 - 0.5 * bend * bend
    lean = bell * slope
    second = 2.0 * lean * (1.0 - v * bend * slope) + (6.0 * GELU_SCALE * GELU_CUBIC) * square * bell
    return v * half, half + v * lean, second


def gelu_two(v):
    square = v * v
    bend = jnp.tanh(v * (GELU_SCALE + (GELU_SCALE * GELU_CUBIC) * square))
    half = 0.5 + 0.5 * bend
    slope = GELU_SCALE + (3.0 * GELU_SCALE * GELU_CUBIC) * square
    return v * half, half + v * ((0.5 - 0.5 * bend * bend) * slope)


def mate(index, step, count):
    if count & (count - 1) == 0:
        return index ^ step
    return (index + step) % count


def hop(array, axis, step):
    count = lax.axis_size(axis)
    return lax.ppermute(array, axis, [(mate(i, step, count), i) for i in range(count)])


def peers_of(array, axis):
    return [array] + [hop(array, axis, j) for j in range(1, lax.axis_size(axis))]


def sent_to(arrays, axis):
    count = lax.axis_size(axis)
    back = [arrays[0]]
    for j in range(1, count):
        back.append(lax.ppermute(arrays[j], axis, [(i, mate(i, j, count)) for i in range(count)]))
    return back


def in_plane(array, forward):
    if lax.axis_size("dp") == 4:
        near = [array, hop(array, "dp", 1), hop(array, "dp", 2)]
        near.append(hop(near[forward], "dp", 3 - forward) if forward else hop(array, "dp", 3))
    else:
        near = peers_of(array, "dp")
    columns = [peers_of(piece, "seq") for piece in near]
    return [list(pieces) for pieces in zip(*columns)]


def owner_of(place_ref, seqs, dps, share, j, d):
    seq, dp = place_ref[0], place_ref[2]
    k = mate(seq, j, seqs) * dps + mate(dp, d, dps)
    return k // share, k % share


def rate_line(block, depth):
    rows = block.astype(F32)
    return jnp.concatenate([rows[i : i + 1, :] for i in range(depth // 128)], axis=1)


def outer_kernel(seqs, heads, dps, share, place_ref, tok_ref, dout_ref, *refs):
    w_refs = refs[: seqs * dps]
    out_refs = refs[seqs * dps : seqs * dps + heads]
    tok_s, dout_s, acc = refs[seqs * dps + heads :]
    rows, features = tok_ref.shape
    depth = features // share
    for r in range(share):
        tok_s[r] = tok_ref[:, r * depth : (r + 1) * depth]
        dout_s[r] = dout_ref[:, r * depth : (r + 1) * depth]
    acc[...] = jnp.zeros_like(acc)
    for j in range(seqs):
        for d in range(dps):
            w = w_refs[j * dps + d]
            h, r = owner_of(place_ref, seqs, dps, share, j, d)
            line = rate_line(w[depth:, :], depth)
            logit = mm(jnp.broadcast_to(line, (EXTRA, depth)), tok_s[r], NT)
            back = mm(dout_s[r], w[0:depth, :], NN)
            acc[h] = acc[h] + jnp.concatenate([back, logit], axis=0)
    first_half = lax.broadcasted_iota(jnp.int32, (EXTRA, rows), 0) < EXTRA // 2
    for j in range(heads):
        total = acc[mate(place_ref[1], j, heads)]
        out_refs[j][0:rows, :] = total[0:rows].astype(BF16)
        logit = total[rows:]
        high = logit.astype(BF16).astype(F32)
        out_refs[j][rows:, :] = jnp.where(first_half, high, logit - high).astype(BF16)


def inner_projection_kernel(seqs, heads, dps, share, place_ref, tok_ref, *refs):
    w_refs = refs[: 2 * seqs * dps]
    out_refs = refs[2 * seqs * dps : 2 * seqs * dps + heads]
    tok_s, acc = refs[2 * seqs * dps + heads :]
    rows, features = tok_ref.shape
    depth = features // share
    half = depth // 2
    for r in range(share):
        tok_s[r] = tok_ref[:, r * depth : (r + 1) * depth]
    acc[...] = jnp.zeros_like(acc)
    for part in range(2):
        for j in range(seqs):
            for d in range(dps):
                w = w_refs[(part * seqs + j) * dps + d]
                h, r = owner_of(place_ref, seqs, dps, share, j, d)
                wide = jnp.concatenate([w[c * half : (c + 1) * half, :] for c in range(3)], axis=1)
                acc[h] = acc[h] + mm(tok_s[r][:, part * half : (part + 1) * half], wide, NN)
    for j in range(heads):
        out_refs[j][...] = acc[mate(place_ref[1], j, heads)].astype(BF16)


def inner_kernel(seqs, dps, place_ref, *refs):
    x_refs, y_refs = refs[:seqs], refs[seqs : 2 * seqs]
    w1_ref, w2_ref, res_ref = refs[2 * seqs : 2 * seqs + 3]
    dw_refs = refs[2 * seqs + 3 : 2 * seqs + 3 + dps]
    (
        qs, ks, vs, ds, es, sg, os, lg,
        w1c, w2c, w1b, w2b,
        x2s, g1s, pgs, gfs, xqs, zqs, dx2s, dg1s,
        dys, ns, rs, ss, cs, g2s, dg2s, dks, des, ws,
    ) = refs[2 * seqs + 3 + dps :]
    rows = x_refs[0].shape[0]
    hd = y_refs[0].shape[1]
    width = 4 * hd
    blocks = seqs * rows // MB
    per = rows // MB
    place = place_ref[0]

    for j in range(seqs):
        owner = mate(place, j, seqs)
        at = pl.ds(pl.multiple_of(owner * rows, rows), rows)
        qs[at, :] = x_refs[j][:, 0:hd]
        ks[at, :] = x_refs[j][:, hd : 2 * hd]
        vs[at, :] = x_refs[j][:, 2 * hd : 3 * hd]
        ds[at, :] = y_refs[j][0:rows, :]
        logit = y_refs[j][rows : rows + 8, :] + y_refs[j][rows + 8 : rows + 16, :]
        gate = jax.nn.sigmoid(logit)
        scaled = (BASE_RATE / hd) * gate
        for b in range(per):
            es[owner * per + b] = padded(scaled[:, b * MB : (b + 1) * MB])
            sg[owner * per + b] = padded((scaled * (1.0 - gate))[:, b * MB : (b + 1) * MB])

    w1c[...] = w1_ref[...]
    start = w2_ref[...]
    w2c[...] = (start - mean(start)).T

    at_row = lax.broadcasted_iota(jnp.int32, (MB, MB), 0)
    at_col = lax.broadcasted_iota(jnp.int32, (MB, MB), 1)
    causal = at_col <= at_row
    diagonal = at_col == at_row

    def to_column(line):
        return jnp.sum(jnp.where(diagonal, line, 0.0), axis=1, keepdims=True)

    def to_line(column):
        return jnp.sum(jnp.where(diagonal, column, 0.0), axis=0, keepdims=True)

    def at_block(i):
        if isinstance(i, int):
            return slice(i * MB, (i + 1) * MB)
        return pl.ds(pl.multiple_of(i * MB, MB), MB)

    def forward(i):
        at = at_block(i)
        q, k, v, d_o = qs[at, :], ks[at, :], vs[at, :], ds[at, :]
        line = es[i][0:1, 0:MB]
        e = to_column(line)
        mask = jnp.where(causal, line, 0.0)
        w1 = w1c[...].astype(BF16)
        w2 = w2c[...].astype(BF16)
        w1b[i] = w1
        w2b[i] = w2
        kb, qb = k.astype(BF16), q.astype(BF16)
        gap = v - k
        gap = gap - mean(gap)
        both = mm(jnp.concatenate([kb, qb], axis=0), w1, NN)
        x2, g1, gg1 = gelu_parts(both[:MB])
        x2b = x2.astype(BF16)
        c = mm(x2b, w2, NT)
        var = mean(c * c)
        cross = mean(gap * c)
        s = lax.rsqrt(var + EPSILON)
        n = c * s
        cc = var * s * s - s * cross
        r = n - gap
        g2 = s * (r - n * cc)
        g2b = g2.astype(BF16)
        p = mm(g2b, w2, NN)
        g1f = p * g1
        w1c[...] = w1c[...] - mm(k, e * g1f, TN)
        w2c[...] = w2c[...] - mm(e * g2, x2b, TN)
        g1b = g1f.astype(BF16)
        b1 = mm(qb, kb, NT)
        a1 = (b1 * mask).astype(BF16)
        zq = both[MB:] - mm(a1, g1b, NN)
        xq, gq = gelu_two(zq)
        xqb = xq.astype(BF16)
        b2 = mm(xqb, x2b, NT)
        a2 = (b2 * mask).astype(BF16)
        y = mm(xqb, w2, NT) - mm(a2, g2b, NN)
        sq = lax.rsqrt(mean(y * y) + EPSILON)
        nq = y * sq
        os[at, 3 * hd : 4 * hd] = (q + nq).astype(BF16)
        dy = sq * (d_o - mean(d_o) - nq * mean(d_o * nq))
        dyb = dy.astype(BF16)
        da2 = -mm(dyb, g2b, NT)
        db2 = (da2 * mask).astype(BF16)
        dg2s[i] = -mm(a2, dyb, TN)
        dxq = mm(dyb, w2, NN) + mm(db2, x2b, NN)
        dx2s[i] = mm(db2, xqb, TN)
        dzq = (dxq * gq).astype(BF16)
        da1 = -mm(dzq, g1b, NT)
        db1 = (da1 * mask).astype(BF16)
        dg1s[i] = -mm(a1, dzq, TN)
        dq = d_o + mm(dzq, w1, NT) + mm(db1, kb, NN)
        os[at, 0:hd] = dq.astype(BF16)
        dks[i] = mm(db1, qb, TN)
        de = jnp.sum(jnp.where(causal, da2 * b2 + da1 * b1, 0.0), axis=0, keepdims=True)
        des[i] = padded(jnp.broadcast_to(de, (8, MB)))
        x2s[i] = x2b
        g1s[i] = g1
        pgs[i] = p * gg1
        gfs[i] = g1f
        xqs[i] = xqb
        zqs[i] = dzq
        dys[i] = dyb
        ns[i] = n
        rs[i] = r
        ss[i] = jnp.broadcast_to(s, (MB, hd))
        cs[i] = jnp.broadcast_to(cc, (MB, hd))
        g2s[i] = g2

    def backward(i):
        at = at_block(i)
        q, k = qs[at, :], ks[at, :]
        e = to_column(es[i][0:1, 0:MB])
        w1, w2 = w1b[i], w2b[i]
        d1, d2 = w1c[...].astype(BF16), w2c[...].astype(BF16)
        x2b, g1, g1f, g2 = x2s[i], g1s[i], gfs[i], g2s[i]
        n, s, cc = ns[i], ss[i], cs[i]
        dh1 = -mm(k, d1, NN)
        dh2 = -mm(x2b, d2, NT)
        dg1 = dg1s[i] + e * dh1
        dp = (dg1 * g1).astype(BF16)
        dg2 = dg2s[i] + e * dh2 + mm(dp, w2, NT)
        dt = s * dg2
        mt = mean(dt * n)
        dr = dt - mean(dt) - n * mt
        dn = dr - cc * dt - rs[i] * mt
        du = s * (dn - mean(dn) - n * (mean(dn * n) + mean(dg2 * g2)))
        dub = du.astype(BF16)
        mixed = jnp.concatenate([(-e * g2).astype(BF16), dub], axis=1)
        dx2 = dx2s[i] + mm(mixed, jnp.concatenate([d2, w2], axis=0), NN)
        dz1 = (dg1 * pgs[i] + dx2 * g1).astype(BF16)
        mixed = jnp.concatenate([(-e * g1f).astype(BF16), dz1], axis=1)
        dk = dks[i] + dr + mm(mixed, jnp.concatenate([d1, w1], axis=1), NT)
        w1c[...] = w1c[...] + mm(
            jnp.concatenate([q, k], axis=0), jnp.concatenate([zqs[i], dz1], axis=0), TN
        )
        w2c[...] = w2c[...] + mm(
            jnp.concatenate([dys[i].astype(F32), du, g2], axis=0),
            jnp.concatenate([xqs[i], x2b, dp], axis=0),
            TN,
        )
        extra = jnp.sum(g1f * dh1, axis=1, keepdims=True) + jnp.sum(
            g2 * dh2, axis=1, keepdims=True
        )
        line = (des[i][0:1, 0:MB] + to_line(extra)) * sg[i][0:1, 0:MB]
        lg[i] = padded(jnp.broadcast_to(line, (8, MB)))
        os[at, hd : 2 * hd] = dk.astype(BF16)
        os[at, 2 * hd : 3 * hd] = (-dr).astype(BF16)

    def loop(step, order):
        if blocks <= UNROLL_LIMIT:
            for i in range(blocks):
                step(order(i))
        else:
            lax.fori_loop(0, blocks, lambda i, unused: (step(order(i)), unused)[1], 0)

    loop(forward, lambda i: i)
    w1c[...] = jnp.zeros_like(w1c)
    w2c[...] = jnp.zeros_like(w2c)
    loop(backward, lambda i: blocks - 1 - i)

    res_ref[0:rows, :] = os[pl.ds(pl.multiple_of(place * rows, rows), rows), :]
    res_ref[rows:, :] = jnp.zeros((EXTRA, width), BF16)
    first_row = lax.broadcasted_iota(jnp.int32, (EXTRA, rows), 0) == 0
    lines = jnp.concatenate([lg[place * per + b][0:1, 0:MB] for b in range(per)], axis=1)
    lines = jnp.where(first_row, jnp.broadcast_to(lines, (EXTRA, rows)), 0.0)
    res_ref[rows:, 0:rows] = lines.astype(BF16)

    part = dw_refs[0].shape[0]
    ws[:, 0:hd] = w1c[...].T
    ws[:, hd : 2 * hd] = w2c[...].T
    for d in range(dps):
        first = (place * dps + mate(place_ref[2], d, dps)) * part
        dw_refs[d][...] = ws[pl.ds(pl.multiple_of(first, part), part), :]


def output_kernel(seqs, heads, dps, share, place_ref, *refs):
    got_refs, refs = refs[:heads], refs[heads:]
    o_refs, w_refs = refs[: seqs * dps], refs[seqs * dps : 3 * seqs * dps]
    out_ref, dtok_ref, got, out_s, grad_s = refs[3 * seqs * dps :]
    hd = o_refs[0].shape[1]
    rows, features = out_ref.shape
    depth = features // share
    half = depth // 2
    for j in range(heads):
        got[mate(place_ref[1], j, heads)] = got_refs[j][...]
    out_s[...] = jnp.zeros_like(out_s)
    grad_s[...] = jnp.zeros_like(grad_s)
    for j in range(seqs):
        for d in range(dps):
            o = o_refs[j * dps + d]
            h, r = owner_of(place_ref, seqs, dps, share, j, d)
            out_s[r] = out_s[r] + mm(got[h, 0:rows, 3 * hd :], o[0:depth, :], NT)
            line = rate_line(o[depth:, :], depth)
            logit = got[h, rows:, 0:rows].astype(F32).T
            grad = [mm(logit, jnp.broadcast_to(line, (EXTRA, depth)), NN)]
            mine = got[h, 0:rows, 0 : 3 * hd]
            halves = []
            for part in range(2):
                w = w_refs[(part * seqs + j) * dps + d]
                wide = jnp.concatenate([w[c * half : (c + 1) * half, :] for c in range(3)], axis=1)
                halves.append(mm(mine, wide, NT))
            grad_s[r] = grad_s[r] + grad[0] + jnp.concatenate(halves, axis=1)
    for r in range(share):
        out_ref[:, r * depth : (r + 1) * depth] = out_s[r].astype(BF16)
        dtok_ref[:, r * depth : (r + 1) * depth] = grad_s[r].astype(BF16)


VMEM = pl.BlockSpec(memory_space=pltpu.VMEM)
SMEM = pl.BlockSpec(memory_space=pltpu.SMEM)
PARAMS = pltpu.CompilerParams(vmem_limit_bytes=48 * 1024 * 1024)


def call(kernel, outs, operands, scratch=()):
    return pl.pallas_call(
        kernel,
        out_shape=outs,
        in_specs=[SMEM] + [VMEM] * (len(operands) - 1),
        out_specs=jax.tree.map(lambda unused: VMEM, outs),
        scratch_shapes=list(scratch),
        compiler_params=PARAMS,
    )(*operands)


def body(tokens, w_qkv, w_lr, w_out, w1_init, w2_init, d_out):
    seqs, heads, dps = (lax.axis_size(a) for a in ("seq", "head", "dp"))
    share = seqs * dps // heads
    rows, features = tokens.shape[1:]
    depth, unused, hd = w_qkv.shape
    inner = w1_init.shape[2]
    blocks = seqs * rows // MB
    place = jnp.stack([lax.axis_index(a).astype(jnp.int32) for a in ("seq", "head", "dp")])
    sizes = (seqs, heads, dps, share)

    pairs = []
    for seq in range(seqs):
        for head in range(heads):
            for dp in range(dps):
                k = seq * dps + dp
                target = head * share + k % share
                to = ((target // dps) * heads + k // share) * dps + target % dps
                pairs.append(((seq * heads + head) * dps + dp, to))

    def swapped(array):
        return lax.ppermute(array, ("seq", "head", "dp"), pairs)

    half = depth // 2
    lines = w_lr[:, 0].reshape(seqs * dps, depth // 128, 128)
    line = lax.dynamic_index_in_dim(
        lines, lax.axis_index("seq") * dps + lax.axis_index("dp"), 0, keepdims=False
    )
    line = jnp.pad(line, ((0, EXTRA - depth // 128), (0, 0)))
    outer_w = swapped(jnp.concatenate([w_out, line], axis=0))
    by_kind = w_qkv.transpose(1, 0, 2)
    first_w = swapped(by_kind[:, :half].reshape(3 * half, hd))
    second = by_kind[:, half:].reshape(3 * half, hd)
    second, first_w, outer_w = lax.optimization_barrier((second, first_w, outer_w))
    second_w = swapped(second)
    outer_ws = sum(in_plane(outer_w, 0), [])
    inner_ws = sum(in_plane(first_w, 1), []) + sum(in_plane(second_w, 2), [])

    def summed(arrays):
        return functools.reduce(lambda a, b: a + b, [a.astype(F32) for a in arrays])

    outer_part = call(
        functools.partial(outer_kernel, *sizes),
        (jax.ShapeDtypeStruct((rows + EXTRA, hd), BF16),) * heads,
        (place, tokens[0], d_out[0], *outer_ws),
        [pltpu.VMEM((share, rows, features // share), BF16)] * 2
        + [pltpu.VMEM((heads, rows + EXTRA, hd), F32)],
    )
    outer_all = peers_of(summed(sent_to(outer_part, "head")), "seq")
    later_place, unused = lax.optimization_barrier((place, outer_part[0]))
    inner_part = call(
        functools.partial(inner_projection_kernel, *sizes),
        (jax.ShapeDtypeStruct((rows, 3 * hd), BF16),) * heads,
        (later_place, tokens[0], *inner_ws),
        [
            pltpu.VMEM((share, rows, features // share), BF16),
            pltpu.VMEM((heads, rows, 3 * hd), F32),
        ],
    )
    inner_all = peers_of(summed(sent_to(inner_part, "head")), "seq")

    long = seqs * rows
    scratch = (
        [pltpu.VMEM((long, hd), F32)] * 4
        + [pltpu.VMEM((blocks, 8, 2 * MB), F32)] * 2
        + [pltpu.VMEM((long, 4 * hd), BF16), pltpu.VMEM((blocks, 8, 2 * MB), F32)]
        + [pltpu.VMEM((hd, inner), F32)] * 2
        + [pltpu.VMEM((blocks, hd, inner), BF16)] * 2
        + [pltpu.VMEM((blocks, MB, inner), t) for t in (BF16, F32, F32, F32, BF16, BF16, F32, F32)]
        + [pltpu.VMEM((blocks, MB, hd), t) for t in (BF16, F32, F32, F32, F32, F32, F32, F32)]
        + [pltpu.VMEM((blocks, 8, 2 * MB), F32), pltpu.VMEM((inner, 2 * hd), F32)]
    )
    part = inner // (seqs * dps)
    result, *d_inner = call(
        functools.partial(inner_kernel, seqs, dps),
        (jax.ShapeDtypeStruct((rows + EXTRA, 4 * hd), BF16),)
        + (jax.ShapeDtypeStruct((part, 2 * hd), F32),) * dps,
        (place, *inner_all, *outer_all, w1_init[0], w2_init[0]),
        scratch,
    )
    got = peers_of(result, "head")
    unused, *d_inner = lax.optimization_barrier((got[1], *d_inner))
    shares = summed(sent_to(d_inner, "dp"))
    out, d_tokens = call(
        functools.partial(output_kernel, *sizes),
        (jax.ShapeDtypeStruct((rows, features), BF16),) * 2,
        (place, *got, *outer_ws, *inner_ws),
        [
            pltpu.VMEM((heads, rows + EXTRA, 4 * hd), BF16),
            pltpu.VMEM((share, rows, features // share), F32),
            pltpu.VMEM((share, rows, features // share), F32),
        ],
    )
    return (out[None], d_tokens[None], shares[:, :hd].transpose(1, 0)[None], shares[:, hd:][None])


def solution(mesh):
    placed = (
        P("dp", "seq", "head"),
        P(("seq", "dp"), None, "head"),
        P(None, "head"),
        P(("seq", "dp"), "head"),
        P("head", None, None),
        P("head", None, None),
        P("dp", "seq", "head"),
    )
    return jax.shard_map(
        body,
        mesh=mesh,
        in_specs=placed,
        out_specs=(
            P("dp", "seq", "head"),
            P("dp", "seq", "head"),
            P("head", None, ("seq", "dp")),
            P("head", ("seq", "dp"), None),
        ),
        check_vma=False,
    )
```

```python
import functools

import jax
import jax.numpy as jnp
from jax import lax
from jax.experimental import pallas as pl
from jax.experimental.pallas import tpu as pltpu
from jax.sharding import PartitionSpec as P

MB = 64
EPSILON = 1e-06
BASE_RATE = 0.1
GELU_SCALE = 0.7978845608028654
GELU_CUBIC = 0.044715
NN = ((1,), (0,))
NT = ((1,), (1,))
TN = ((0,), (0,))
EXTRA = 16
UNROLL_LIMIT = 8
F32 = jnp.float32
BF16 = jnp.bfloat16


def mm(left, right, dims):
    return lax.dot_general(
        left.astype(BF16), right.astype(BF16), (dims, ((), ())), preferred_element_type=F32
    )


def padded(lines):
    return jnp.concatenate([lines, jnp.zeros_like(lines)], axis=1)


def mean(rows):
    return jnp.mean(rows, axis=-1, keepdims=True)


def gelu_parts(v):
    square = v * v
    bend = jnp.tanh(v * (GELU_SCALE + (GELU_SCALE * GELU_CUBIC) * square))
    half = 0.5 + 0.5 * bend
    slope = GELU_SCALE + (3.0 * GELU_SCALE * GELU_CUBIC) * square
    bell = 0.5 - 0.5 * bend * bend
    lean = bell * slope
    second = 2.0 * lean * (1.0 - v * bend * slope) + (6.0 * GELU_SCALE * GELU_CUBIC) * square * bell
    return v * half, half + v * lean, second


def gelu_two(v):
    square = v * v
    bend = jnp.tanh(v * (GELU_SCALE + (GELU_SCALE * GELU_CUBIC) * square))
    half = 0.5 + 0.5 * bend
    slope = GELU_SCALE + (3.0 * GELU_SCALE * GELU_CUBIC) * square
    return v * half, half + v * ((0.5 - 0.5 * bend * bend) * slope)


def mate(index, step, count):
    if count & (count - 1) == 0:
        return index ^ step
    return (index + step) % count


def hop(array, axis, step):
    count = lax.axis_size(axis)
    return lax.ppermute(array, axis, [(mate(i, step, count), i) for i in range(count)])


def peers_of(array, axis):
    return [array] + [hop(array, axis, j) for j in range(1, lax.axis_size(axis))]


def sent_to(arrays, axis):
    count = lax.axis_size(axis)
    back = [arrays[0]]
    for j in range(1, count):
        back.append(lax.ppermute(arrays[j], axis, [(i, mate(i, j, count)) for i in range(count)]))
    return back


def in_plane(array, forward):
    if lax.axis_size("dp") == 4:
        near = [array, hop(array, "dp", 1), hop(array, "dp", 2)]
        near.append(hop(near[forward], "dp", 3 - forward) if forward else hop(array, "dp", 3))
    else:
        near = peers_of(array, "dp")
    columns = [peers_of(piece, "seq") for piece in near]
    return [list(pieces) for pieces in zip(*columns)]


def owner_of(place_ref, seqs, dps, share, j, d):
    seq, dp = place_ref[0], place_ref[2]
    k = mate(seq, j, seqs) * dps + mate(dp, d, dps)
    return k // share, k % share


def rate_line(block, depth):
    rows = block.astype(F32)
    return jnp.concatenate([rows[i : i + 1, :] for i in range(depth // 128)], axis=1)


def outer_kernel(seqs, heads, dps, share, place_ref, tok_ref, dout_ref, *refs):
    w_refs = refs[: seqs * dps]
    out_refs = refs[seqs * dps : seqs * dps + heads]
    tok_s, dout_s, acc = refs[seqs * dps + heads :]
    rows, features = tok_ref.shape
    depth = features // share
    for r in range(share):
        tok_s[r] = tok_ref[:, r * depth : (r + 1) * depth]
        dout_s[r] = dout_ref[:, r * depth : (r + 1) * depth]
    acc[...] = jnp.zeros_like(acc)
    for j in range(seqs):
        for d in range(dps):
            w = w_refs[j * dps + d]
            h, r = owner_of(place_ref, seqs, dps, share, j, d)
            line = rate_line(w[depth:, :], depth)
            logit = mm(jnp.broadcast_to(line, (EXTRA, depth)), tok_s[r], NT)
            back = mm(dout_s[r], w[0:depth, :], NN)
            acc[h] = acc[h] + jnp.concatenate([back, logit], axis=0)
    first_half = lax.broadcasted_iota(jnp.int32, (EXTRA, rows), 0) < EXTRA // 2
    for j in range(heads):
        total = acc[mate(place_ref[1], j, heads)]
        out_refs[j][0:rows, :] = total[0:rows].astype(BF16)
        logit = total[rows:]
        high = logit.astype(BF16).astype(F32)
        out_refs[j][rows:, :] = jnp.where(first_half, high, logit - high).astype(BF16)


def inner_projection_kernel(seqs, heads, dps, share, place_ref, tok_ref, *refs):
    w_refs = refs[: 2 * seqs * dps]
    out_refs = refs[2 * seqs * dps : 2 * seqs * dps + heads]
    tok_s, acc = refs[2 * seqs * dps + heads :]
    rows, features = tok_ref.shape
    depth = features // share
    half = depth // 2
    for r in range(share):
        tok_s[r] = tok_ref[:, r * depth : (r + 1) * depth]
    acc[...] = jnp.zeros_like(acc)
    for part in range(2):
        for j in range(seqs):
            for d in range(dps):
                w = w_refs[(part * seqs + j) * dps + d]
                h, r = owner_of(place_ref, seqs, dps, share, j, d)
                wide = jnp.concatenate([w[c * half : (c + 1) * half, :] for c in range(3)], axis=1)
                acc[h] = acc[h] + mm(tok_s[r][:, part * half : (part + 1) * half], wide, NN)
    for j in range(heads):
        out_refs[j][...] = acc[mate(place_ref[1], j, heads)].astype(BF16)


def inner_kernel(seqs, dps, place_ref, *refs):
    x_refs, y_refs = refs[:seqs], refs[seqs : 2 * seqs]
    w1_ref, w2_ref, res_ref = refs[2 * seqs : 2 * seqs + 3]
    dw_refs = refs[2 * seqs + 3 : 2 * seqs + 3 + dps]
    (
        qs, ks, vs, ds, es, sg, os, lg,
        w1c, w2c, w1b, w2b,
        x2s, g1s, pgs, gfs, xqs, zqs, dx2s, dg1s,
        dys, ns, rs, ss, cs, g2s, dg2s, dks, des, ws,
    ) = refs[2 * seqs + 3 + dps :]
    rows = x_refs[0].shape[0]
    hd = y_refs[0].shape[1]
    width = 4 * hd
    blocks = seqs * rows // MB
    per = rows // MB
    place = place_ref[0]

    for j in range(seqs):
        owner = mate(place, j, seqs)
        at = pl.ds(pl.multiple_of(owner * rows, rows), rows)
        qs[at, :] = x_refs[j][:, 0:hd]
        ks[at, :] = x_refs[j][:, hd : 2 * hd]
        vs[at, :] = x_refs[j][:, 2 * hd : 3 * hd]
        ds[at, :] = y_refs[j][0:rows, :]
        logit = y_refs[j][rows : rows + 8, :] + y_refs[j][rows + 8 : rows + 16, :]
        gate = jax.nn.sigmoid(logit)
        scaled = (BASE_RATE / hd) * gate
        for b in range(per):
            es[owner * per + b] = padded(scaled[:, b * MB : (b + 1) * MB])
            sg[owner * per + b] = padded((scaled * (1.0 - gate))[:, b * MB : (b + 1) * MB])

    w1c[...] = w1_ref[...]
    start = w2_ref[...]
    w2c[...] = (start - mean(start)).T

    at_row = lax.broadcasted_iota(jnp.int32, (MB, MB), 0)
    at_col = lax.broadcasted_iota(jnp.int32, (MB, MB), 1)
    causal = at_col <= at_row
    diagonal = at_col == at_row

    def to_column(line):
        return jnp.sum(jnp.where(diagonal, line, 0.0), axis=1, keepdims=True)

    def to_line(column):
        return jnp.sum(jnp.where(diagonal, column, 0.0), axis=0, keepdims=True)

    def at_block(i):
        if isinstance(i, int):
            return slice(i * MB, (i + 1) * MB)
        return pl.ds(pl.multiple_of(i * MB, MB), MB)

    def forward(i):
        at = at_block(i)
        q, k, v, d_o = qs[at, :], ks[at, :], vs[at, :], ds[at, :]
        line = es[i][0:1, 0:MB]
        e = to_column(line)
        mask = jnp.where(causal, line, 0.0)
        w1 = w1c[...].astype(BF16)
        w2 = w2c[...].astype(BF16)
        w1b[i] = w1
        w2b[i] = w2
        kb, qb = k.astype(BF16), q.astype(BF16)
        gap = v - k
        gap = gap - mean(gap)
        both = mm(jnp.concatenate([kb, qb], axis=0), w1, NN)
        x2, g1, gg1 = gelu_parts(both[:MB])
        x2b = x2.astype(BF16)
        c = mm(x2b, w2, NT)
        var = mean(c * c)
        cross = mean(gap * c)
        s = lax.rsqrt(var + EPSILON)
        n = c * s
        cc = var * s * s - s * cross
        r = n - gap
        g2 = s * (r - n * cc)
        g2b = g2.astype(BF16)
        p = mm(g2b, w2, NN)
        g1f = p * g1
        w1c[...] = w1c[...] - mm(k, e * g1f, TN)
        w2c[...] = w2c[...] - mm(e * g2, x2b, TN)
        g1b = g1f.astype(BF16)
        b1 = mm(qb, kb, NT)
        a1 = (b1 * mask).astype(BF16)
        zq = both[MB:] - mm(a1, g1b, NN)
        xq, gq = gelu_two(zq)
        xqb = xq.astype(BF16)
        b2 = mm(xqb, x2b, NT)
        a2 = (b2 * mask).astype(BF16)
        y = mm(xqb, w2, NT) - mm(a2, g2b, NN)
        sq = lax.rsqrt(mean(y * y) + EPSILON)
        nq = y * sq
        os[at, 3 * hd : 4 * hd] = (q + nq).astype(BF16)
        dy = sq * (d_o - mean(d_o) - nq * mean(d_o * nq))
        dyb = dy.astype(BF16)
        da2 = -mm(dyb, g2b, NT)
        db2 = (da2 * mask).astype(BF16)
        dg2s[i] = -mm(a2, dyb, TN)
        dxq = mm(dyb, w2, NN) + mm(db2, x2b, NN)
        dx2s[i] = mm(db2, xqb, TN)
        dzq = (dxq * gq).astype(BF16)
        da1 = -mm(dzq, g1b, NT)
        db1 = (da1 * mask).astype(BF16)
        dg1s[i] = -mm(a1, dzq, TN)
        dq = d_o + mm(dzq, w1, NT) + mm(db1, kb, NN)
        os[at, 0:hd] = dq.astype(BF16)
        dks[i] = mm(db1, qb, TN)
        de = jnp.sum(jnp.where(causal, da2 * b2 + da1 * b1, 0.0), axis=0, keepdims=True)
        des[i] = padded(jnp.broadcast_to(de, (8, MB)))
        x2s[i] = x2b
        g1s[i] = g1
        pgs[i] = p * gg1
        gfs[i] = g1f
        xqs[i] = xqb
        zqs[i] = dzq
        dys[i] = dyb
        ns[i] = n
        rs[i] = r
        ss[i] = jnp.broadcast_to(s, (MB, hd))
        cs[i] = jnp.broadcast_to(cc, (MB, hd))
        g2s[i] = g2

    def backward(i):
        at = at_block(i)
        q, k = qs[at, :], ks[at, :]
        e = to_column(es[i][0:1, 0:MB])
        w1, w2 = w1b[i], w2b[i]
        d1, d2 = w1c[...].astype(BF16), w2c[...].astype(BF16)
        x2b, g1, g1f, g2 = x2s[i], g1s[i], gfs[i], g2s[i]
        n, s, cc = ns[i], ss[i], cs[i]
        dh1 = -mm(k, d1, NN)
        dh2 = -mm(x2b, d2, NT)
        dg1 = dg1s[i] + e * dh1
        dp = (dg1 * g1).astype(BF16)
        dg2 = dg2s[i] + e * dh2 + mm(dp, w2, NT)
        dt = s * dg2
        mt = mean(dt * n)
        dr = dt - mean(dt) - n * mt
        dn = dr - cc * dt - rs[i] * mt
        du = s * (dn - mean(dn) - n * (mean(dn * n) + mean(dg2 * g2)))
        dub = du.astype(BF16)
        mixed = jnp.concatenate([(-e * g2).astype(BF16), dub], axis=1)
        dx2 = dx2s[i] + mm(mixed, jnp.concatenate([d2, w2], axis=0), NN)
        dz1 = (dg1 * pgs[i] + dx2 * g1).astype(BF16)
        mixed = jnp.concatenate([(-e * g1f).astype(BF16), dz1], axis=1)
        dk = dks[i] + dr + mm(mixed, jnp.concatenate([d1, w1], axis=1), NT)
        w1c[...] = w1c[...] + mm(
            jnp.concatenate([q, k], axis=0), jnp.concatenate([zqs[i], dz1], axis=0), TN
        )
        w2c[...] = w2c[...] + mm(
            jnp.concatenate([dys[i].astype(F32), du, g2], axis=0),
            jnp.concatenate([xqs[i], x2b, dp], axis=0),
            TN,
        )
        extra = jnp.sum(g1f * dh1, axis=1, keepdims=True) + jnp.sum(
            g2 * dh2, axis=1, keepdims=True
        )
        line = (des[i][0:1, 0:MB] + to_line(extra)) * sg[i][0:1, 0:MB]
        lg[i] = padded(jnp.broadcast_to(line, (8, MB)))
        os[at, hd : 2 * hd] = dk.astype(BF16)
        os[at, 2 * hd : 3 * hd] = (-dr).astype(BF16)

    def loop(step, order):
        if blocks <= UNROLL_LIMIT:
            for i in range(blocks):
                step(order(i))
        else:
            lax.fori_loop(0, blocks, lambda i, unused: (step(order(i)), unused)[1], 0)

    loop(forward, lambda i: i)
    w1c[...] = jnp.zeros_like(w1c)
    w2c[...] = jnp.zeros_like(w2c)
    loop(backward, lambda i: blocks - 1 - i)

    res_ref[0:rows, :] = os[pl.ds(pl.multiple_of(place * rows, rows), rows), :]
    res_ref[rows:, :] = jnp.zeros((EXTRA, width), BF16)
    first_row = lax.broadcasted_iota(jnp.int32, (EXTRA, rows), 0) == 0
    lines = jnp.concatenate([lg[place * per + b][0:1, 0:MB] for b in range(per)], axis=1)
    lines = jnp.where(first_row, jnp.broadcast_to(lines, (EXTRA, rows)), 0.0)
    res_ref[rows:, 0:rows] = lines.astype(BF16)

    part = dw_refs[0].shape[0]
    ws[:, 0:hd] = w1c[...].T
    ws[:, hd : 2 * hd] = w2c[...].T
    for d in range(dps):
        first = (place * dps + mate(place_ref[2], d, dps)) * part
        dw_refs[d][...] = ws[pl.ds(pl.multiple_of(first, part), part), :]


def output_kernel(seqs, heads, dps, share, place_ref, *refs):
    got_refs, refs = refs[:heads], refs[heads:]
    o_refs, w_refs = refs[: seqs * dps], refs[seqs * dps : 3 * seqs * dps]
    out_ref, dtok_ref, got, out_s, grad_s = refs[3 * seqs * dps :]
    hd = o_refs[0].shape[1]
    rows, features = out_ref.shape
    depth = features // share
    half = depth // 2
    for j in range(heads):
        got[mate(place_ref[1], j, heads)] = got_refs[j][...]
    out_s[...] = jnp.zeros_like(out_s)
    grad_s[...] = jnp.zeros_like(grad_s)
    for j in range(seqs):
        for d in range(dps):
            o = o_refs[j * dps + d]
            h, r = owner_of(place_ref, seqs, dps, share, j, d)
            out_s[r] = out_s[r] + mm(got[h, 0:rows, 3 * hd :], o[0:depth, :], NT)
            line = rate_line(o[depth:, :], depth)
            logit = got[h, rows:, 0:rows].astype(F32).T
            grad = [mm(logit, jnp.broadcast_to(line, (EXTRA, depth)), NN)]
            mine = got[h, 0:rows, 0 : 3 * hd]
            halves = []
            for part in range(2):
                w = w_refs[(part * seqs + j) * dps + d]
                wide = jnp.concatenate([w[c * half : (c + 1) * half, :] for c in range(3)], axis=1)
                halves.append(mm(mine, wide, NT))
            grad_s[r] = grad_s[r] + grad[0] + jnp.concatenate(halves, axis=1)
    for r in range(share):
        out_ref[:, r * depth : (r + 1) * depth] = out_s[r].astype(BF16)
        dtok_ref[:, r * depth : (r + 1) * depth] = grad_s[r].astype(BF16)


VMEM = pl.BlockSpec(memory_space=pltpu.VMEM)
SMEM = pl.BlockSpec(memory_space=pltpu.SMEM)
MIB = 1024 * 1024


def call(kernel, outs, operands, scratch=(), mib=16):
    return pl.pallas_call(
        kernel,
        out_shape=outs,
        in_specs=[SMEM] + [VMEM] * (len(operands) - 1),
        out_specs=jax.tree.map(lambda unused: VMEM, outs),
        scratch_shapes=list(scratch),
        compiler_params=pltpu.CompilerParams(vmem_limit_bytes=mib * MIB),
    )(*operands)


def body(tokens, w_qkv, w_lr, w_out, w1_init, w2_init, d_out):
    seqs, heads, dps = (lax.axis_size(a) for a in ("seq", "head", "dp"))
    share = seqs * dps // heads
    rows, features = tokens.shape[1:]
    depth, unused, hd = w_qkv.shape
    inner = w1_init.shape[2]
    blocks = seqs * rows // MB
    place = jnp.stack([lax.axis_index(a).astype(jnp.int32) for a in ("seq", "head", "dp")])
    sizes = (seqs, heads, dps, share)

    pairs = []
    for seq in range(seqs):
        for head in range(heads):
            for dp in range(dps):
                k = seq * dps + dp
                target = head * share + k % share
                to = ((target // dps) * heads + k // share) * dps + target % dps
                pairs.append(((seq * heads + head) * dps + dp, to))

    def swapped(array):
        return lax.ppermute(array, ("seq", "head", "dp"), pairs)

    half = depth // 2
    lines = w_lr[:, 0].reshape(seqs * dps, depth // 128, 128)
    line = lax.dynamic_index_in_dim(
        lines, lax.axis_index("seq") * dps + lax.axis_index("dp"), 0, keepdims=False
    )
    line = jnp.pad(line, ((0, EXTRA - depth // 128), (0, 0)))
    outer_w = swapped(jnp.concatenate([w_out, line], axis=0))
    by_kind = w_qkv.transpose(1, 0, 2)
    first_w = swapped(by_kind[:, :half].reshape(3 * half, hd))
    second = by_kind[:, half:].reshape(3 * half, hd)
    second, first_w, outer_w = lax.optimization_barrier((second, first_w, outer_w))
    second_w = swapped(second)
    outer_ws = sum(in_plane(outer_w, 0), [])
    inner_ws = sum(in_plane(first_w, 1), []) + sum(in_plane(second_w, 2), [])

    def summed(arrays):
        return functools.reduce(lambda a, b: a + b, [a.astype(F32) for a in arrays])

    outer_part = call(
        functools.partial(outer_kernel, *sizes),
        (jax.ShapeDtypeStruct((rows + EXTRA, hd), BF16),) * heads,
        (place, tokens[0], d_out[0], *outer_ws),
        [pltpu.VMEM((share, rows, features // share), BF16)] * 2
        + [pltpu.VMEM((heads, rows + EXTRA, hd), F32)],
    )
    outer_all = peers_of(summed(sent_to(outer_part, "head")), "seq")
    later_place, unused = lax.optimization_barrier((place, outer_part[0]))
    inner_part = call(
        functools.partial(inner_projection_kernel, *sizes),
        (jax.ShapeDtypeStruct((rows, 3 * hd), BF16),) * heads,
        (later_place, tokens[0], *inner_ws),
        [
            pltpu.VMEM((share, rows, features // share), BF16),
            pltpu.VMEM((heads, rows, 3 * hd), F32),
        ],
    )
    inner_all = peers_of(summed(sent_to(inner_part, "head")), "seq")

    long = seqs * rows
    scratch = (
        [pltpu.VMEM((long, hd), F32)] * 4
        + [pltpu.VMEM((blocks, 8, 2 * MB), F32)] * 2
        + [pltpu.VMEM((long, 4 * hd), BF16), pltpu.VMEM((blocks, 8, 2 * MB), F32)]
        + [pltpu.VMEM((hd, inner), F32)] * 2
        + [pltpu.VMEM((blocks, hd, inner), BF16)] * 2
        + [pltpu.VMEM((blocks, MB, inner), t) for t in (BF16, F32, F32, F32, BF16, BF16, F32, F32)]
        + [pltpu.VMEM((blocks, MB, hd), t) for t in (BF16, F32, F32, F32, F32, F32, F32, F32)]
        + [pltpu.VMEM((blocks, 8, 2 * MB), F32), pltpu.VMEM((inner, 2 * hd), F32)]
    )
    part = inner // (seqs * dps)
    result, *d_inner = call(
        functools.partial(inner_kernel, seqs, dps),
        (jax.ShapeDtypeStruct((rows + EXTRA, 4 * hd), BF16),)
        + (jax.ShapeDtypeStruct((part, 2 * hd), F32),) * dps,
        (place, *inner_all, *outer_all, w1_init[0], w2_init[0]),
        scratch,
        14 + 2 * blocks,
    )
    got = peers_of(result, "head")
    unused, *d_inner = lax.optimization_barrier((got[1], *d_inner))
    shares = summed(sent_to(d_inner, "dp"))
    out, d_tokens = call(
        functools.partial(output_kernel, *sizes),
        (jax.ShapeDtypeStruct((rows, features), BF16),) * 2,
        (place, *got, *outer_ws, *inner_ws),
        [
            pltpu.VMEM((heads, rows + EXTRA, 4 * hd), BF16),
            pltpu.VMEM((share, rows, features // share), F32),
            pltpu.VMEM((share, rows, features // share), F32),
        ],
    )
    return (out[None], d_tokens[None], shares[:, :hd].transpose(1, 0)[None], shares[:, hd:][None])


def solution(mesh):
    placed = (
        P("dp", "seq", "head"),
        P(("seq", "dp"), None, "head"),
        P(None, "head"),
        P(("seq", "dp"), "head"),
        P("head", None, None),
        P("head", None, None),
        P("dp", "seq", "head"),
    )
    return jax.shard_map(
        body,
        mesh=mesh,
        in_specs=placed,
        out_specs=(
            P("dp", "seq", "head"),
            P("dp", "seq", "head"),
            P("head", None, ("seq", "dp")),
            P("head", ("seq", "dp"), None),
        ),
        check_vma=False,
    )
```

```python
import functools

import jax
import jax.numpy as jnp
from jax import lax
from jax.experimental import pallas as pl
from jax.experimental.pallas import tpu as pltpu
from jax.sharding import PartitionSpec as P

MB = 64
EPSILON = 1e-06
BASE_RATE = 0.1
GELU_SCALE = 0.7978845608028654
GELU_CUBIC = 0.044715
NN = ((1,), (0,))
NT = ((1,), (1,))
TN = ((0,), (0,))
EXTRA = 16
UNROLL_LIMIT = 8
F32 = jnp.float32
BF16 = jnp.bfloat16


def mm(left, right, dims):
    return lax.dot_general(
        left.astype(BF16), right.astype(BF16), (dims, ((), ())), preferred_element_type=F32
    )


def padded(lines):
    return jnp.concatenate([lines, jnp.zeros_like(lines)], axis=1)


def mean(rows):
    return jnp.mean(rows, axis=-1, keepdims=True)


def gelu_parts(v):
    square = v * v
    bend = jnp.tanh(v * (GELU_SCALE + (GELU_SCALE * GELU_CUBIC) * square))
    half = 0.5 + 0.5 * bend
    slope = GELU_SCALE + (3.0 * GELU_SCALE * GELU_CUBIC) * square
    bell = 0.5 - 0.5 * bend * bend
    lean = bell * slope
    second = 2.0 * lean * (1.0 - v * bend * slope) + (6.0 * GELU_SCALE * GELU_CUBIC) * square * bell
    return v * half, half + v * lean, second


def gelu_two(v):
    square = v * v
    bend = jnp.tanh(v * (GELU_SCALE + (GELU_SCALE * GELU_CUBIC) * square))
    half = 0.5 + 0.5 * bend
    slope = GELU_SCALE + (3.0 * GELU_SCALE * GELU_CUBIC) * square
    return v * half, half + v * ((0.5 - 0.5 * bend * bend) * slope)


def mate(index, step, count):
    if count & (count - 1) == 0:
        return index ^ step
    return (index + step) % count


def hop(array, axis, step):
    count = lax.axis_size(axis)
    return lax.ppermute(array, axis, [(mate(i, step, count), i) for i in range(count)])


def peers_of(array, axis):
    return [array] + [hop(array, axis, j) for j in range(1, lax.axis_size(axis))]


def sent_to(arrays, axis):
    count = lax.axis_size(axis)
    back = [arrays[0]]
    for j in range(1, count):
        back.append(lax.ppermute(arrays[j], axis, [(i, mate(i, j, count)) for i in range(count)]))
    return back


def over_seq(near):
    return sum([list(pieces) for pieces in zip(*[peers_of(piece, "seq") for piece in near])], [])


def owner_of(place_ref, seqs, dps, share, j, d):
    seq, dp = place_ref[0], place_ref[2]
    k = mate(seq, j, seqs) * dps + mate(dp, d, dps)
    return k // share, k % share


def rate_line(block, depth):
    rows = block.astype(F32)
    return jnp.concatenate([rows[i : i + 1, :] for i in range(depth // 128)], axis=1)


def outer_kernel(seqs, heads, dps, share, place_ref, tok_ref, dout_ref, *refs):
    w_refs = refs[: seqs * dps]
    out_refs = refs[seqs * dps : seqs * dps + heads]
    tok_s, dout_s, acc = refs[seqs * dps + heads :]
    rows, features = tok_ref.shape
    depth = features // share
    for r in range(share):
        tok_s[r] = tok_ref[:, r * depth : (r + 1) * depth]
        dout_s[r] = dout_ref[:, r * depth : (r + 1) * depth]
    acc[...] = jnp.zeros_like(acc)
    for j in range(seqs):
        for d in range(dps):
            w = w_refs[j * dps + d]
            h, r = owner_of(place_ref, seqs, dps, share, j, d)
            line = rate_line(w[depth:, :], depth)
            logit = mm(jnp.broadcast_to(line, (EXTRA, depth)), tok_s[r], NT)
            back = mm(dout_s[r], w[0:depth, :], NN)
            acc[h] = acc[h] + jnp.concatenate([back, logit], axis=0)
    first_half = lax.broadcasted_iota(jnp.int32, (EXTRA, rows), 0) < EXTRA // 2
    for j in range(heads):
        total = acc[mate(place_ref[1], j, heads)]
        out_refs[j][0:rows, :] = total[0:rows].astype(BF16)
        logit = total[rows:]
        high = logit.astype(BF16).astype(F32)
        out_refs[j][rows:, :] = jnp.where(first_half, high, logit - high).astype(BF16)


def inner_projection_kernel(seqs, heads, dps, share, place_ref, tok_ref, *refs):
    w_refs = refs[: 2 * seqs * dps]
    out_refs = refs[2 * seqs * dps : 2 * seqs * dps + heads]
    tok_s, acc = refs[2 * seqs * dps + heads :]
    rows, features = tok_ref.shape
    depth = features // share
    half = depth // 2
    for r in range(share):
        tok_s[r] = tok_ref[:, r * depth : (r + 1) * depth]
    acc[...] = jnp.zeros_like(acc)
    for part in range(2):
        for j in range(seqs):
            for d in range(dps):
                w = w_refs[(part * seqs + j) * dps + d]
                h, r = owner_of(place_ref, seqs, dps, share, j, d)
                wide = jnp.concatenate([w[c * half : (c + 1) * half, :] for c in range(3)], axis=1)
                acc[h] = acc[h] + mm(tok_s[r][:, part * half : (part + 1) * half], wide, NN)
    for j in range(heads):
        out_refs[j][...] = acc[mate(place_ref[1], j, heads)].astype(BF16)


def inner_kernel(seqs, dps, place_ref, *refs):
    x_refs, y_refs = refs[:seqs], refs[seqs : 2 * seqs]
    w1_ref, w2_ref, res_ref = refs[2 * seqs : 2 * seqs + 3]
    dw_refs = refs[2 * seqs + 3 : 2 * seqs + 3 + dps]
    (
        qs, ks, vs, ds, es, sg, os, lg,
        w1c, w2c, w1b, w2b,
        x2s, g1s, pgs, gfs, xqs, zqs, dx2s, dg1s,
        dys, ns, rs, ss, cs, g2s, dg2s, dks, des, ws,
    ) = refs[2 * seqs + 3 + dps :]
    rows = x_refs[0].shape[0]
    hd = y_refs[0].shape[1]
    width = 4 * hd
    blocks = seqs * rows // MB
    per = rows // MB
    place = place_ref[0]

    for j in range(seqs):
        owner = mate(place, j, seqs)
        at = pl.ds(pl.multiple_of(owner * rows, rows), rows)
        qs[at, :] = x_refs[j][:, 0:hd]
        ks[at, :] = x_refs[j][:, hd : 2 * hd]
        vs[at, :] = x_refs[j][:, 2 * hd : 3 * hd]
        ds[at, :] = y_refs[j][0:rows, :]
        logit = y_refs[j][rows : rows + 8, :] + y_refs[j][rows + 8 : rows + 16, :]
        gate = jax.nn.sigmoid(logit)
        scaled = (BASE_RATE / hd) * gate
        for b in range(per):
            es[owner * per + b] = padded(scaled[:, b * MB : (b + 1) * MB])
            sg[owner * per + b] = padded((scaled * (1.0 - gate))[:, b * MB : (b + 1) * MB])

    w1c[...] = w1_ref[...]
    start = w2_ref[...]
    w2c[...] = (start - mean(start)).T

    at_row = lax.broadcasted_iota(jnp.int32, (MB, MB), 0)
    at_col = lax.broadcasted_iota(jnp.int32, (MB, MB), 1)
    causal = at_col <= at_row
    diagonal = at_col == at_row

    def to_column(line):
        return jnp.sum(jnp.where(diagonal, line, 0.0), axis=1, keepdims=True)

    def to_line(column):
        return jnp.sum(jnp.where(diagonal, column, 0.0), axis=0, keepdims=True)

    def at_block(i):
        if isinstance(i, int):
            return slice(i * MB, (i + 1) * MB)
        return pl.ds(pl.multiple_of(i * MB, MB), MB)

    def forward(i):
        at = at_block(i)
        q, k, v, d_o = qs[at, :], ks[at, :], vs[at, :], ds[at, :]
        line = es[i][0:1, 0:MB]
        e = to_column(line)
        mask = jnp.where(causal, line, 0.0)
        w1 = w1c[...].astype(BF16)
        w2 = w2c[...].astype(BF16)
        w1b[i] = w1
        w2b[i] = w2
        kb, qb = k.astype(BF16), q.astype(BF16)
        gap = v - k
        gap = gap - mean(gap)
        both = mm(jnp.concatenate([kb, qb], axis=0), w1, NN)
        x2, g1, gg1 = gelu_parts(both[:MB])
        x2b = x2.astype(BF16)
        c = mm(x2b, w2, NT)
        var = mean(c * c)
        cross = mean(gap * c)
        s = lax.rsqrt(var + EPSILON)
        n = c * s
        cc = var * s * s - s * cross
        r = n - gap
        g2 = s * (r - n * cc)
        g2b = g2.astype(BF16)
        p = mm(g2b, w2, NN)
        g1f = p * g1
        w1c[...] = w1c[...] - mm(k, e * g1f, TN)
        w2c[...] = w2c[...] - mm(e * g2, x2b, TN)
        g1b = g1f.astype(BF16)
        b1 = mm(qb, kb, NT)
        a1 = (b1 * mask).astype(BF16)
        zq = both[MB:] - mm(a1, g1b, NN)
        xq, gq = gelu_two(zq)
        xqb = xq.astype(BF16)
        b2 = mm(xqb, x2b, NT)
        a2 = (b2 * mask).astype(BF16)
        y = mm(xqb, w2, NT) - mm(a2, g2b, NN)
        sq = lax.rsqrt(mean(y * y) + EPSILON)
        nq = y * sq
        os[at, 3 * hd : 4 * hd] = (q + nq).astype(BF16)
        dy = sq * (d_o - mean(d_o) - nq * mean(d_o * nq))
        dyb = dy.astype(BF16)
        da2 = -mm(dyb, g2b, NT)
        db2 = (da2 * mask).astype(BF16)
        dg2s[i] = -mm(a2, dyb, TN)
        dxq = mm(dyb, w2, NN) + mm(db2, x2b, NN)
        dx2s[i] = mm(db2, xqb, TN)
        dzq = (dxq * gq).astype(BF16)
        da1 = -mm(dzq, g1b, NT)
        db1 = (da1 * mask).astype(BF16)
        dg1s[i] = -mm(a1, dzq, TN)
        dq = d_o + mm(dzq, w1, NT) + mm(db1, kb, NN)
        os[at, 0:hd] = dq.astype(BF16)
        dks[i] = mm(db1, qb, TN)
        de = jnp.sum(jnp.where(causal, da2 * b2 + da1 * b1, 0.0), axis=0, keepdims=True)
        des[i] = padded(jnp.broadcast_to(de, (8, MB)))
        x2s[i] = x2b
        g1s[i] = g1
        pgs[i] = p * gg1
        gfs[i] = g1f
        xqs[i] = xqb
        zqs[i] = dzq
        dys[i] = dyb
        ns[i] = n
        rs[i] = r
        ss[i] = jnp.broadcast_to(s, (MB, hd))
        cs[i] = jnp.broadcast_to(cc, (MB, hd))
        g2s[i] = g2

    def backward(i):
        at = at_block(i)
        q, k = qs[at, :], ks[at, :]
        e = to_column(es[i][0:1, 0:MB])
        w1, w2 = w1b[i], w2b[i]
        d1, d2 = w1c[...].astype(BF16), w2c[...].astype(BF16)
        x2b, g1, g1f, g2 = x2s[i], g1s[i], gfs[i], g2s[i]
        n, s, cc = ns[i], ss[i], cs[i]
        dh1 = -mm(k, d1, NN)
        dh2 = -mm(x2b, d2, NT)
        dg1 = dg1s[i] + e * dh1
        dp = (dg1 * g1).astype(BF16)
        dg2 = dg2s[i] + e * dh2 + mm(dp, w2, NT)
        dt = s * dg2
        mt = mean(dt * n)
        dr = dt - mean(dt) - n * mt
        dn = dr - cc * dt - rs[i] * mt
        du = s * (dn - mean(dn) - n * (mean(dn * n) + mean(dg2 * g2)))
        dub = du.astype(BF16)
        mixed = jnp.concatenate([(-e * g2).astype(BF16), dub], axis=1)
        dx2 = dx2s[i] + mm(mixed, jnp.concatenate([d2, w2], axis=0), NN)
        dz1 = (dg1 * pgs[i] + dx2 * g1).astype(BF16)
        mixed = jnp.concatenate([(-e * g1f).astype(BF16), dz1], axis=1)
        dk = dks[i] + dr + mm(mixed, jnp.concatenate([d1, w1], axis=1), NT)
        w1c[...] = w1c[...] + mm(
            jnp.concatenate([q, k], axis=0), jnp.concatenate([zqs[i], dz1], axis=0), TN
        )
        w2c[...] = w2c[...] + mm(
            jnp.concatenate([dys[i].astype(F32), du, g2], axis=0),
            jnp.concatenate([xqs[i], x2b, dp], axis=0),
            TN,
        )
        extra = jnp.sum(g1f * dh1, axis=1, keepdims=True) + jnp.sum(
            g2 * dh2, axis=1, keepdims=True
        )
        line = (des[i][0:1, 0:MB] + to_line(extra)) * sg[i][0:1, 0:MB]
        lg[i] = padded(jnp.broadcast_to(line, (8, MB)))
        os[at, hd : 2 * hd] = dk.astype(BF16)
        os[at, 2 * hd : 3 * hd] = (-dr).astype(BF16)

    def loop(step, order):
        if blocks <= UNROLL_LIMIT:
            for i in range(blocks):
                step(order(i))
        else:
            lax.fori_loop(0, blocks, lambda i, unused: (step(order(i)), unused)[1], 0)

    loop(forward, lambda i: i)
    w1c[...] = jnp.zeros_like(w1c)
    w2c[...] = jnp.zeros_like(w2c)
    loop(backward, lambda i: blocks - 1 - i)

    res_ref[0:rows, :] = os[pl.ds(pl.multiple_of(place * rows, rows), rows), :]
    res_ref[rows:, :] = jnp.zeros((EXTRA, width), BF16)
    first_row = lax.broadcasted_iota(jnp.int32, (EXTRA, rows), 0) == 0
    lines = jnp.concatenate([lg[place * per + b][0:1, 0:MB] for b in range(per)], axis=1)
    lines = jnp.where(first_row, jnp.broadcast_to(lines, (EXTRA, rows)), 0.0)
    res_ref[rows:, 0:rows] = lines.astype(BF16)

    part = dw_refs[0].shape[0]
    ws[:, 0:hd] = w1c[...].T
    ws[:, hd : 2 * hd] = w2c[...].T
    for d in range(dps):
        first = (place * dps + mate(place_ref[2], d, dps)) * part
        dw_refs[d][...] = ws[pl.ds(pl.multiple_of(first, part), part), :]


def output_kernel(seqs, heads, dps, share, place_ref, *refs):
    got_refs, refs = refs[:heads], refs[heads:]
    o_refs, w_refs = refs[: seqs * dps], refs[seqs * dps : 3 * seqs * dps]
    out_ref, dtok_ref, got, out_s, grad_s = refs[3 * seqs * dps :]
    hd = o_refs[0].shape[1]
    rows, features = out_ref.shape
    depth = features // share
    half = depth // 2
    for j in range(heads):
        got[mate(place_ref[1], j, heads)] = got_refs[j][...]
    out_s[...] = jnp.zeros_like(out_s)
    grad_s[...] = jnp.zeros_like(grad_s)
    for j in range(seqs):
        for d in range(dps):
            o = o_refs[j * dps + d]
            h, r = owner_of(place_ref, seqs, dps, share, j, d)
            out_s[r] = out_s[r] + mm(got[h, 0:rows, 3 * hd :], o[0:depth, :], NT)
            line = rate_line(o[depth:, :], depth)
            logit = got[h, rows:, 0:rows].astype(F32).T
            grad = [mm(logit, jnp.broadcast_to(line, (EXTRA, depth)), NN)]
            mine = got[h, 0:rows, 0 : 3 * hd]
            halves = []
            for part in range(2):
                w = w_refs[(part * seqs + j) * dps + d]
                wide = jnp.concatenate([w[c * half : (c + 1) * half, :] for c in range(3)], axis=1)
                halves.append(mm(mine, wide, NT))
            grad_s[r] = grad_s[r] + grad[0] + jnp.concatenate(halves, axis=1)
    for r in range(share):
        out_ref[:, r * depth : (r + 1) * depth] = out_s[r].astype(BF16)
        dtok_ref[:, r * depth : (r + 1) * depth] = grad_s[r].astype(BF16)


VMEM = pl.BlockSpec(memory_space=pltpu.VMEM)
SMEM = pl.BlockSpec(memory_space=pltpu.SMEM)
MIB = 1024 * 1024


def call(kernel, outs, operands, scratch=(), mib=16):
    return pl.pallas_call(
        kernel,
        out_shape=outs,
        in_specs=[SMEM] + [VMEM] * (len(operands) - 1),
        out_specs=jax.tree.map(lambda unused: VMEM, outs),
        scratch_shapes=list(scratch),
        compiler_params=pltpu.CompilerParams(vmem_limit_bytes=mib * MIB),
    )(*operands)


def body(tokens, w_qkv, w_lr, w_out, w1_init, w2_init, d_out):
    seqs, heads, dps = (lax.axis_size(a) for a in ("seq", "head", "dp"))
    share = seqs * dps // heads
    rows, features = tokens.shape[1:]
    depth, unused, hd = w_qkv.shape
    inner = w1_init.shape[2]
    blocks = seqs * rows // MB
    place = jnp.stack([lax.axis_index(a).astype(jnp.int32) for a in ("seq", "head", "dp")])
    sizes = (seqs, heads, dps, share)
    place, w_out, w_qkv = lax.optimization_barrier((place, w_out, w_qkv))

    pairs = []
    for seq in range(seqs):
        for head in range(heads):
            for dp in range(dps):
                k = seq * dps + dp
                target = head * share + k % share
                to = ((target // dps) * heads + k // share) * dps + target % dps
                pairs.append(((seq * heads + head) * dps + dp, to))

    def swapped(array):
        return lax.ppermute(array, ("seq", "head", "dp"), pairs)

    half = depth // 2
    lines = w_lr[:, 0].reshape(seqs * dps, depth // 128, 128)
    line = lax.dynamic_index_in_dim(
        lines, lax.axis_index("seq") * dps + lax.axis_index("dp"), 0, keepdims=False
    )
    line = jnp.pad(line, ((0, EXTRA - depth // 128), (0, 0)))
    outer_w = swapped(jnp.concatenate([w_out, line], axis=0))
    by_kind = w_qkv.transpose(1, 0, 2)
    first_w = swapped(by_kind[:, :half].reshape(3 * half, hd))
    second = by_kind[:, half:].reshape(3 * half, hd)
    second_w = swapped(second)
    outer_near = peers_of(outer_w, "dp")
    first_near = [first_w, hop(first_w, "dp", 1), hop(first_w, "dp", 2)]
    second_w, *outer_near = lax.optimization_barrier((second_w, *outer_near))
    second_near = [second_w, hop(second_w, "dp", 1), hop(second_w, "dp", 2)]
    outer_ws = over_seq(outer_near)
    def summed(arrays):
        return functools.reduce(lambda a, b: a + b, [a.astype(F32) for a in arrays])

    outer_part = call(
        functools.partial(outer_kernel, *sizes),
        (jax.ShapeDtypeStruct((rows + EXTRA, hd), BF16),) * heads,
        (place, tokens[0], d_out[0], *outer_ws),
        [pltpu.VMEM((share, rows, features // share), BF16)] * 2
        + [pltpu.VMEM((heads, rows + EXTRA, hd), F32)],
    )
    outer_all = peers_of(summed(sent_to(outer_part, "head")), "seq")
    if dps == 4:
        first_near[1], second_near[2], unused = lax.optimization_barrier(
            (first_near[1], second_near[2], outer_part[0])
        )
        first_near.append(hop(first_near[1], "dp", 2))
        second_near.append(hop(second_near[2], "dp", 1))
    else:
        first_near += [hop(first_w, "dp", j) for j in range(3, dps)]
        second_near += [hop(second_w, "dp", j) for j in range(3, dps)]
    inner_ws = over_seq(first_near) + over_seq(second_near)
    inner_part = call(
        functools.partial(inner_projection_kernel, *sizes),
        (jax.ShapeDtypeStruct((rows, 3 * hd), BF16),) * heads,
        (place, tokens[0], *inner_ws),
        [
            pltpu.VMEM((share, rows, features // share), BF16),
            pltpu.VMEM((heads, rows, 3 * hd), F32),
        ],
    )
    inner_all = peers_of(summed(sent_to(inner_part, "head")), "seq")

    long = seqs * rows
    scratch = (
        [pltpu.VMEM((long, hd), F32)] * 4
        + [pltpu.VMEM((blocks, 8, 2 * MB), F32)] * 2
        + [pltpu.VMEM((long, 4 * hd), BF16), pltpu.VMEM((blocks, 8, 2 * MB), F32)]
        + [pltpu.VMEM((hd, inner), F32)] * 2
        + [pltpu.VMEM((blocks, hd, inner), BF16)] * 2
        + [pltpu.VMEM((blocks, MB, inner), t) for t in (BF16, F32, F32, F32, BF16, BF16, F32, F32)]
        + [pltpu.VMEM((blocks, MB, hd), t) for t in (BF16, F32, F32, F32, F32, F32, F32, F32)]
        + [pltpu.VMEM((blocks, 8, 2 * MB), F32), pltpu.VMEM((inner, 2 * hd), F32)]
    )
    part = inner // (seqs * dps)
    result, *d_inner = call(
        functools.partial(inner_kernel, seqs, dps),
        (jax.ShapeDtypeStruct((rows + EXTRA, 4 * hd), BF16),)
        + (jax.ShapeDtypeStruct((part, 2 * hd), F32),) * dps,
        (place, *inner_all, *outer_all, w1_init[0], w2_init[0]),
        scratch,
        14 + 2 * blocks,
    )
    got = peers_of(result, "head")
    unused, *d_inner = lax.optimization_barrier((got[1], *d_inner))
    shares = summed(sent_to(d_inner, "dp"))
    out, d_tokens = call(
        functools.partial(output_kernel, *sizes),
        (jax.ShapeDtypeStruct((rows, features), BF16),) * 2,
        (place, *got, *outer_ws, *inner_ws),
        [
            pltpu.VMEM((heads, rows + EXTRA, 4 * hd), BF16),
            pltpu.VMEM((share, rows, features // share), F32),
            pltpu.VMEM((share, rows, features // share), F32),
        ],
    )
    return (out[None], d_tokens[None], shares[:, :hd].transpose(1, 0)[None], shares[:, hd:][None])


def solution(mesh):
    placed = (
        P("dp", "seq", "head"),
        P(("seq", "dp"), None, "head"),
        P(None, "head"),
        P(("seq", "dp"), "head"),
        P("head", None, None),
        P("head", None, None),
        P("dp", "seq", "head"),
    )
    return jax.shard_map(
        body,
        mesh=mesh,
        in_specs=placed,
        out_specs=(
            P("dp", "seq", "head"),
            P("dp", "seq", "head"),
            P("head", None, ("seq", "dp")),
            P("head", ("seq", "dp"), None),
        ),
        check_vma=False,
    )
```

```python
import functools

import jax
import jax.numpy as jnp
from jax import lax
from jax.experimental import pallas as pl
from jax.experimental.pallas import tpu as pltpu
from jax.sharding import PartitionSpec as P

MB = 64
EPSILON = 1e-06
BASE_RATE = 0.1
GELU_SCALE = 0.7978845608028654
GELU_CUBIC = 0.044715
NN = ((1,), (0,))
NT = ((1,), (1,))
TN = ((0,), (0,))
EXTRA = 16
UNROLL_LIMIT = 8
F32 = jnp.float32
BF16 = jnp.bfloat16


def mm(left, right, dims):
    return lax.dot_general(
        left.astype(BF16), right.astype(BF16), (dims, ((), ())), preferred_element_type=F32
    )


def padded(lines):
    return jnp.concatenate([lines, jnp.zeros_like(lines)], axis=1)


def mean(rows):
    return jnp.mean(rows, axis=-1, keepdims=True)


def gelu_parts(v):
    square = v * v
    bend = jnp.tanh(v * (GELU_SCALE + (GELU_SCALE * GELU_CUBIC) * square))
    half = 0.5 + 0.5 * bend
    slope = GELU_SCALE + (3.0 * GELU_SCALE * GELU_CUBIC) * square
    bell = 0.5 - 0.5 * bend * bend
    lean = bell * slope
    second = 2.0 * lean * (1.0 - v * bend * slope) + (6.0 * GELU_SCALE * GELU_CUBIC) * square * bell
    return v * half, half + v * lean, second


def gelu_two(v):
    square = v * v
    bend = jnp.tanh(v * (GELU_SCALE + (GELU_SCALE * GELU_CUBIC) * square))
    half = 0.5 + 0.5 * bend
    slope = GELU_SCALE + (3.0 * GELU_SCALE * GELU_CUBIC) * square
    return v * half, half + v * ((0.5 - 0.5 * bend * bend) * slope)


def mate(index, step, count):
    if count & (count - 1) == 0:
        return index ^ step
    return (index + step) % count


def hop(array, axis, step):
    count = lax.axis_size(axis)
    return lax.ppermute(array, axis, [(mate(i, step, count), i) for i in range(count)])


def peers_of(array, axis):
    return [array] + [hop(array, axis, j) for j in range(1, lax.axis_size(axis))]


def sent_to(arrays, axis):
    count = lax.axis_size(axis)
    back = [arrays[0]]
    for j in range(1, count):
        back.append(lax.ppermute(arrays[j], axis, [(i, mate(i, j, count)) for i in range(count)]))
    return back


def over_seq(near):
    return sum([list(pieces) for pieces in zip(*[peers_of(piece, "seq") for piece in near])], [])


def owner_of(place_ref, seqs, dps, share, j, d):
    seq, dp = place_ref[0], place_ref[2]
    k = mate(seq, j, seqs) * dps + mate(dp, d, dps)
    return k // share, k % share


def rate_line(block, depth):
    rows = block.astype(F32)
    return jnp.concatenate([rows[i : i + 1, :] for i in range(depth // 128)], axis=1)


def outer_kernel(seqs, heads, dps, share, place_ref, tok_ref, dout_ref, *refs):
    w_refs = refs[: seqs * dps]
    out_refs = refs[seqs * dps : seqs * dps + heads]
    tok_s, dout_s, acc = refs[seqs * dps + heads :]
    rows, features = tok_ref.shape
    depth = features // share
    for r in range(share):
        tok_s[r] = tok_ref[:, r * depth : (r + 1) * depth]
        dout_s[r] = dout_ref[:, r * depth : (r + 1) * depth]
    acc[...] = jnp.zeros_like(acc)
    for j in range(seqs):
        for d in range(dps):
            w = w_refs[j * dps + d]
            h, r = owner_of(place_ref, seqs, dps, share, j, d)
            line = rate_line(w[depth:, :], depth)
            logit = mm(jnp.broadcast_to(line, (EXTRA, depth)), tok_s[r], NT)
            back = mm(dout_s[r], w[0:depth, :], NN)
            acc[h] = acc[h] + jnp.concatenate([back, logit], axis=0)
    first_half = lax.broadcasted_iota(jnp.int32, (EXTRA, rows), 0) < EXTRA // 2
    for j in range(heads):
        total = acc[mate(place_ref[1], j, heads)]
        out_refs[j][0:rows, :] = total[0:rows].astype(BF16)
        logit = total[rows:]
        high = logit.astype(BF16).astype(F32)
        out_refs[j][rows:, :] = jnp.where(first_half, high, logit - high).astype(BF16)


def inner_projection_kernel(seqs, heads, dps, share, place_ref, tok_ref, *refs):
    w_refs = refs[: 2 * seqs * dps]
    out_refs = refs[2 * seqs * dps : 2 * seqs * dps + heads]
    tok_s, acc = refs[2 * seqs * dps + heads :]
    rows, features = tok_ref.shape
    depth = features // share
    half = depth // 2
    for r in range(share):
        tok_s[r] = tok_ref[:, r * depth : (r + 1) * depth]
    acc[...] = jnp.zeros_like(acc)
    for part in range(2):
        for j in range(seqs):
            for d in range(dps):
                w = w_refs[(part * seqs + j) * dps + d]
                h, r = owner_of(place_ref, seqs, dps, share, j, d)
                wide = jnp.concatenate([w[c * half : (c + 1) * half, :] for c in range(3)], axis=1)
                acc[h] = acc[h] + mm(tok_s[r][:, part * half : (part + 1) * half], wide, NN)
    for j in range(heads):
        out_refs[j][...] = acc[mate(place_ref[1], j, heads)].astype(BF16)


def inner_kernel(seqs, dps, place_ref, *refs):
    x_refs, y_refs = refs[:seqs], refs[seqs : 2 * seqs]
    w1_ref, w2_ref, res_ref = refs[2 * seqs : 2 * seqs + 3]
    dw_refs = refs[2 * seqs + 3 : 2 * seqs + 3 + dps]
    (
        qs, ks, vs, ds, es, sg, os, lg,
        w1c, w2c, w1b, w2b,
        x2s, g1s, pgs, gfs, xqs, zqs, dx2s, dg1s,
        dys, ns, rs, ss, cs, g2s, dg2s, dks, des, ws,
    ) = refs[2 * seqs + 3 + dps :]
    rows = x_refs[0].shape[0]
    hd = y_refs[0].shape[1]
    width = 4 * hd
    blocks = seqs * rows // MB
    per = rows // MB
    place = place_ref[0]

    for j in range(seqs):
        owner = mate(place, j, seqs)
        at = pl.ds(pl.multiple_of(owner * rows, rows), rows)
        qs[at, :] = x_refs[j][:, 0:hd]
        ks[at, :] = x_refs[j][:, hd : 2 * hd]
        vs[at, :] = x_refs[j][:, 2 * hd : 3 * hd]
        ds[at, :] = y_refs[j][0:rows, :]
        logit = y_refs[j][rows : rows + 8, :] + y_refs[j][rows + 8 : rows + 16, :]
        gate = jax.nn.sigmoid(logit)
        scaled = (BASE_RATE / hd) * gate
        for b in range(per):
            es[owner * per + b] = padded(scaled[:, b * MB : (b + 1) * MB])
            sg[owner * per + b] = padded((scaled * (1.0 - gate))[:, b * MB : (b + 1) * MB])

    w1c[...] = w1_ref[...]
    start = w2_ref[...]
    w2c[...] = (start - mean(start)).T

    at_row = lax.broadcasted_iota(jnp.int32, (MB, MB), 0)
    at_col = lax.broadcasted_iota(jnp.int32, (MB, MB), 1)
    causal = at_col <= at_row
    diagonal = at_col == at_row

    def to_column(line):
        return jnp.sum(jnp.where(diagonal, line, 0.0), axis=1, keepdims=True)

    def to_line(column):
        return jnp.sum(jnp.where(diagonal, column, 0.0), axis=0, keepdims=True)

    def at_block(i):
        if isinstance(i, int):
            return slice(i * MB, (i + 1) * MB)
        return pl.ds(pl.multiple_of(i * MB, MB), MB)

    def forward(i):
        at = at_block(i)
        q, k, v, d_o = qs[at, :], ks[at, :], vs[at, :], ds[at, :]
        line = es[i][0:1, 0:MB]
        e = to_column(line)
        mask = jnp.where(causal, line, 0.0)
        w1 = w1c[...].astype(BF16)
        w2 = w2c[...].astype(BF16)
        w1b[i] = w1
        w2b[i] = w2
        kb, qb = k.astype(BF16), q.astype(BF16)
        gap = v - k
        gap = gap - mean(gap)
        both = mm(jnp.concatenate([kb, qb], axis=0), w1, NN)
        x2, g1, gg1 = gelu_parts(both[:MB])
        x2b = x2.astype(BF16)
        c = mm(x2b, w2, NT)
        var = mean(c * c)
        cross = mean(gap * c)
        s = lax.rsqrt(var + EPSILON)
        n = c * s
        cc = var * s * s - s * cross
        r = n - gap
        g2 = s * (r - n * cc)
        g2b = g2.astype(BF16)
        p = mm(g2b, w2, NN)
        g1f = p * g1
        w1c[...] = w1c[...] - mm(k, e * g1f, TN)
        w2c[...] = w2c[...] - mm(e * g2, x2b, TN)
        g1b = g1f.astype(BF16)
        b1 = mm(qb, kb, NT)
        a1 = (b1 * mask).astype(BF16)
        zq = both[MB:] - mm(a1, g1b, NN)
        xq, gq = gelu_two(zq)
        xqb = xq.astype(BF16)
        b2 = mm(xqb, x2b, NT)
        a2 = (b2 * mask).astype(BF16)
        y = mm(xqb, w2, NT) - mm(a2, g2b, NN)
        sq = lax.rsqrt(mean(y * y) + EPSILON)
        nq = y * sq
        os[at, 3 * hd : 4 * hd] = (q + nq).astype(BF16)
        dy = sq * (d_o - mean(d_o) - nq * mean(d_o * nq))
        dyb = dy.astype(BF16)
        da2 = -mm(dyb, g2b, NT)
        db2 = (da2 * mask).astype(BF16)
        dg2s[i] = -mm(a2, dyb, TN)
        dxq = mm(dyb, w2, NN) + mm(db2, x2b, NN)
        dx2s[i] = mm(db2, xqb, TN)
        dzq = (dxq * gq).astype(BF16)
        da1 = -mm(dzq, g1b, NT)
        db1 = (da1 * mask).astype(BF16)
        dg1s[i] = -mm(a1, dzq, TN)
        dq = d_o + mm(dzq, w1, NT) + mm(db1, kb, NN)
        os[at, 0:hd] = dq.astype(BF16)
        dks[i] = mm(db1, qb, TN)
        de = jnp.sum(jnp.where(causal, da2 * b2 + da1 * b1, 0.0), axis=0, keepdims=True)
        des[i] = padded(jnp.broadcast_to(de, (8, MB)))
        x2s[i] = x2b
        g1s[i] = g1
        pgs[i] = p * gg1
        gfs[i] = g1f
        xqs[i] = xqb
        zqs[i] = dzq
        dys[i] = dyb
        ns[i] = n
        rs[i] = r
        ss[i] = jnp.broadcast_to(s, (MB, hd))
        cs[i] = jnp.broadcast_to(cc, (MB, hd))
        g2s[i] = g2

    def backward(i):
        at = at_block(i)
        q, k = qs[at, :], ks[at, :]
        e = to_column(es[i][0:1, 0:MB])
        w1, w2 = w1b[i], w2b[i]
        d1, d2 = w1c[...].astype(BF16), w2c[...].astype(BF16)
        x2b, g1, g1f, g2 = x2s[i], g1s[i], gfs[i], g2s[i]
        n, s, cc = ns[i], ss[i], cs[i]
        dh1 = -mm(k, d1, NN)
        dh2 = -mm(x2b, d2, NT)
        dg1 = dg1s[i] + e * dh1
        dp = (dg1 * g1).astype(BF16)
        dg2 = dg2s[i] + e * dh2 + mm(dp, w2, NT)
        dt = s * dg2
        mt = mean(dt * n)
        dr = dt - mean(dt) - n * mt
        dn = dr - cc * dt - rs[i] * mt
        du = s * (dn - mean(dn) - n * (mean(dn * n) + mean(dg2 * g2)))
        dub = du.astype(BF16)
        mixed = jnp.concatenate([(-e * g2).astype(BF16), dub], axis=1)
        dx2 = dx2s[i] + mm(mixed, jnp.concatenate([d2, w2], axis=0), NN)
        dz1 = (dg1 * pgs[i] + dx2 * g1).astype(BF16)
        mixed = jnp.concatenate([(-e * g1f).astype(BF16), dz1], axis=1)
        dk = dks[i] + dr + mm(mixed, jnp.concatenate([d1, w1], axis=1), NT)
        w1c[...] = w1c[...] + mm(
            jnp.concatenate([q, k], axis=0), jnp.concatenate([zqs[i], dz1], axis=0), TN
        )
        w2c[...] = w2c[...] + mm(
            jnp.concatenate([dys[i].astype(F32), du, g2], axis=0),
            jnp.concatenate([xqs[i], x2b, dp], axis=0),
            TN,
        )
        extra = jnp.sum(g1f * dh1, axis=1, keepdims=True) + jnp.sum(
            g2 * dh2, axis=1, keepdims=True
        )
        line = (des[i][0:1, 0:MB] + to_line(extra)) * sg[i][0:1, 0:MB]
        lg[i] = padded(jnp.broadcast_to(line, (8, MB)))
        os[at, hd : 2 * hd] = dk.astype(BF16)
        os[at, 2 * hd : 3 * hd] = (-dr).astype(BF16)

    def loop(step, order):
        if blocks <= UNROLL_LIMIT:
            for i in range(blocks):
                step(order(i))
        else:
            lax.fori_loop(0, blocks, lambda i, unused: (step(order(i)), unused)[1], 0)

    loop(forward, lambda i: i)
    w1c[...] = jnp.zeros_like(w1c)
    w2c[...] = jnp.zeros_like(w2c)
    loop(backward, lambda i: blocks - 1 - i)

    res_ref[0:rows, :] = os[pl.ds(pl.multiple_of(place * rows, rows), rows), :]
    res_ref[rows:, :] = jnp.zeros((EXTRA, width), BF16)
    first_row = lax.broadcasted_iota(jnp.int32, (EXTRA, rows), 0) == 0
    lines = jnp.concatenate([lg[place * per + b][0:1, 0:MB] for b in range(per)], axis=1)
    lines = jnp.where(first_row, jnp.broadcast_to(lines, (EXTRA, rows)), 0.0)
    res_ref[rows:, 0:rows] = lines.astype(BF16)

    part = dw_refs[0].shape[0]
    ws[:, 0:hd] = w1c[...].T
    ws[:, hd : 2 * hd] = w2c[...].T
    for d in range(dps):
        first = (place * dps + mate(place_ref[2], d, dps)) * part
        dw_refs[d][...] = ws[pl.ds(pl.multiple_of(first, part), part), :]


def output_kernel(seqs, heads, dps, share, place_ref, *refs):
    got_refs, refs = refs[:heads], refs[heads:]
    o_refs, w_refs = refs[: seqs * dps], refs[seqs * dps : 3 * seqs * dps]
    out_ref, dtok_ref, got, out_s, grad_s = refs[3 * seqs * dps :]
    hd = o_refs[0].shape[1]
    rows, features = out_ref.shape
    depth = features // share
    half = depth // 2
    for j in range(heads):
        got[mate(place_ref[1], j, heads)] = got_refs[j][...]
    out_s[...] = jnp.zeros_like(out_s)
    grad_s[...] = jnp.zeros_like(grad_s)
    for j in range(seqs):
        for d in range(dps):
            o = o_refs[j * dps + d]
            h, r = owner_of(place_ref, seqs, dps, share, j, d)
            out_s[r] = out_s[r] + mm(got[h, 0:rows, 3 * hd :], o[0:depth, :], NT)
            line = rate_line(o[depth:, :], depth)
            logit = got[h, rows:, 0:rows].astype(F32).T
            grad = [mm(logit, jnp.broadcast_to(line, (EXTRA, depth)), NN)]
            mine = got[h, 0:rows, 0 : 3 * hd]
            halves = []
            for part in range(2):
                w = w_refs[(part * seqs + j) * dps + d]
                wide = jnp.concatenate([w[c * half : (c + 1) * half, :] for c in range(3)], axis=1)
                halves.append(mm(mine, wide, NT))
            grad_s[r] = grad_s[r] + grad[0] + jnp.concatenate(halves, axis=1)
    for r in range(share):
        out_ref[:, r * depth : (r + 1) * depth] = out_s[r].astype(BF16)
        dtok_ref[:, r * depth : (r + 1) * depth] = grad_s[r].astype(BF16)


VMEM = pl.BlockSpec(memory_space=pltpu.VMEM)
SMEM = pl.BlockSpec(memory_space=pltpu.SMEM)
MIB = 1024 * 1024


def call(kernel, outs, operands, scratch=(), mib=16):
    return pl.pallas_call(
        kernel,
        out_shape=outs,
        in_specs=[SMEM] + [VMEM] * (len(operands) - 1),
        out_specs=jax.tree.map(lambda unused: VMEM, outs),
        scratch_shapes=list(scratch),
        compiler_params=pltpu.CompilerParams(vmem_limit_bytes=mib * MIB),
    )(*operands)


def body(tokens, w_qkv, w_lr, w_out, w1_init, w2_init, d_out):
    seqs, heads, dps = (lax.axis_size(a) for a in ("seq", "head", "dp"))
    share = seqs * dps // heads
    rows, features = tokens.shape[1:]
    depth, unused, hd = w_qkv.shape
    inner = w1_init.shape[2]
    blocks = seqs * rows // MB
    place = jnp.stack([lax.axis_index(a).astype(jnp.int32) for a in ("seq", "head", "dp")])
    sizes = (seqs, heads, dps, share)
    place, w_out, w_qkv = lax.optimization_barrier((place, w_out, w_qkv))

    pairs = []
    for seq in range(seqs):
        for head in range(heads):
            for dp in range(dps):
                k = seq * dps + dp
                target = head * share + k % share
                to = ((target // dps) * heads + k // share) * dps + target % dps
                pairs.append(((seq * heads + head) * dps + dp, to))

    def swapped(array):
        return lax.ppermute(array, ("seq", "head", "dp"), pairs)

    half = depth // 2
    lines = w_lr[:, 0].reshape(seqs * dps, depth // 128, 128)
    line = lax.dynamic_index_in_dim(
        lines, lax.axis_index("seq") * dps + lax.axis_index("dp"), 0, keepdims=False
    )
    line = jnp.pad(line, ((0, EXTRA - depth // 128), (0, 0)))
    outer_w = swapped(jnp.concatenate([w_out, line], axis=0))
    by_kind = w_qkv.transpose(1, 0, 2)
    first_w = swapped(by_kind[:, :half].reshape(3 * half, hd))
    second = by_kind[:, half:].reshape(3 * half, hd)
    second_w = swapped(second)
    outer_near = peers_of(outer_w, "dp")
    first_near = [first_w, hop(first_w, "dp", 1), hop(first_w, "dp", 2)]
    second_near = [second_w, hop(second_w, "dp", 1), hop(second_w, "dp", 2)]
    outer_ws = over_seq(outer_near)
    def summed(arrays):
        return functools.reduce(lambda a, b: a + b, [a.astype(F32) for a in arrays])

    outer_part = call(
        functools.partial(outer_kernel, *sizes),
        (jax.ShapeDtypeStruct((rows + EXTRA, hd), BF16),) * heads,
        (place, tokens[0], d_out[0], *outer_ws),
        [pltpu.VMEM((share, rows, features // share), BF16)] * 2
        + [pltpu.VMEM((heads, rows + EXTRA, hd), F32)],
    )
    outer_all = peers_of(summed(sent_to(outer_part, "head")), "seq")
    if dps == 4:
        first_near[1], second_near[2], unused = lax.optimization_barrier(
            (first_near[1], second_near[2], outer_part[0])
        )
        first_near.append(hop(first_near[1], "dp", 2))
        second_near.append(hop(second_near[2], "dp", 1))
    else:
        first_near += [hop(first_w, "dp", j) for j in range(3, dps)]
        second_near += [hop(second_w, "dp", j) for j in range(3, dps)]
    inner_ws = over_seq(first_near) + over_seq(second_near)
    later_place, unused = lax.optimization_barrier((place, outer_all[-1]))
    inner_part = call(
        functools.partial(inner_projection_kernel, *sizes),
        (jax.ShapeDtypeStruct((rows, 3 * hd), BF16),) * heads,
        (later_place, tokens[0], *inner_ws),
        [
            pltpu.VMEM((share, rows, features // share), BF16),
            pltpu.VMEM((heads, rows, 3 * hd), F32),
        ],
    )
    inner_all = peers_of(summed(sent_to(inner_part, "head")), "seq")

    long = seqs * rows
    scratch = (
        [pltpu.VMEM((long, hd), F32)] * 4
        + [pltpu.VMEM((blocks, 8, 2 * MB), F32)] * 2
        + [pltpu.VMEM((long, 4 * hd), BF16), pltpu.VMEM((blocks, 8, 2 * MB), F32)]
        + [pltpu.VMEM((hd, inner), F32)] * 2
        + [pltpu.VMEM((blocks, hd, inner), BF16)] * 2
        + [pltpu.VMEM((blocks, MB, inner), t) for t in (BF16, F32, F32, F32, BF16, BF16, F32, F32)]
        + [pltpu.VMEM((blocks, MB, hd), t) for t in (BF16, F32, F32, F32, F32, F32, F32, F32)]
        + [pltpu.VMEM((blocks, 8, 2 * MB), F32), pltpu.VMEM((inner, 2 * hd), F32)]
    )
    part = inner // (seqs * dps)
    result, *d_inner = call(
        functools.partial(inner_kernel, seqs, dps),
        (jax.ShapeDtypeStruct((rows + EXTRA, 4 * hd), BF16),)
        + (jax.ShapeDtypeStruct((part, 2 * hd), F32),) * dps,
        (place, *inner_all, *outer_all, w1_init[0], w2_init[0]),
        scratch,
        14 + 2 * blocks,
    )
    got = peers_of(result, "head")
    unused, *d_inner = lax.optimization_barrier((got[1], *d_inner))
    shares = summed(sent_to(d_inner, "dp"))
    out, d_tokens = call(
        functools.partial(output_kernel, *sizes),
        (jax.ShapeDtypeStruct((rows, features), BF16),) * 2,
        (place, *got, *outer_ws, *inner_ws),
        [
            pltpu.VMEM((heads, rows + EXTRA, 4 * hd), BF16),
            pltpu.VMEM((share, rows, features // share), F32),
            pltpu.VMEM((share, rows, features // share), F32),
        ],
    )
    return (out[None], d_tokens[None], shares[:, :hd].transpose(1, 0)[None], shares[:, hd:][None])


def solution(mesh):
    placed = (
        P("dp", "seq", "head"),
        P(("seq", "dp"), None, "head"),
        P(None, "head"),
        P(("seq", "dp"), "head"),
        P("head", None, None),
        P("head", None, None),
        P("dp", "seq", "head"),
    )
    return jax.shard_map(
        body,
        mesh=mesh,
        in_specs=placed,
        out_specs=(
            P("dp", "seq", "head"),
            P("dp", "seq", "head"),
            P("head", None, ("seq", "dp")),
            P("head", ("seq", "dp"), None),
        ),
        check_vma=False,
    )
```

```python
import functools

import jax
import jax.numpy as jnp
from jax import lax
from jax.experimental import pallas as pl
from jax.experimental.pallas import tpu as pltpu
from jax.sharding import PartitionSpec as P

MB = 64
EPSILON = 1e-06
BASE_RATE = 0.1
GELU_SCALE = 0.7978845608028654
GELU_CUBIC = 0.044715
NN = ((1,), (0,))
NT = ((1,), (1,))
TN = ((0,), (0,))
EXTRA = 16
UNROLL_LIMIT = 8
F32 = jnp.float32
BF16 = jnp.bfloat16


def mm(left, right, dims):
    return lax.dot_general(
        left.astype(BF16), right.astype(BF16), (dims, ((), ())), preferred_element_type=F32
    )


def padded(lines):
    return jnp.concatenate([lines, jnp.zeros_like(lines)], axis=1)


def mean(rows):
    return jnp.mean(rows, axis=-1, keepdims=True)


def gelu_parts(v):
    square = v * v
    bend = jnp.tanh(v * (GELU_SCALE + (GELU_SCALE * GELU_CUBIC) * square))
    half = 0.5 + 0.5 * bend
    slope = GELU_SCALE + (3.0 * GELU_SCALE * GELU_CUBIC) * square
    bell = 0.5 - 0.5 * bend * bend
    lean = bell * slope
    second = 2.0 * lean * (1.0 - v * bend * slope) + (6.0 * GELU_SCALE * GELU_CUBIC) * square * bell
    return v * half, half + v * lean, second


def gelu_two(v):
    square = v * v
    bend = jnp.tanh(v * (GELU_SCALE + (GELU_SCALE * GELU_CUBIC) * square))
    half = 0.5 + 0.5 * bend
    slope = GELU_SCALE + (3.0 * GELU_SCALE * GELU_CUBIC) * square
    return v * half, half + v * ((0.5 - 0.5 * bend * bend) * slope)


def mate(index, step, count):
    if count & (count - 1) == 0:
        return index ^ step
    return (index + step) % count


def hop(array, axis, step):
    count = lax.axis_size(axis)
    return lax.ppermute(array, axis, [(mate(i, step, count), i) for i in range(count)])


def peers_of(array, axis):
    return [array] + [hop(array, axis, j) for j in range(1, lax.axis_size(axis))]


def sent_to(arrays, axis):
    count = lax.axis_size(axis)
    back = [arrays[0]]
    for j in range(1, count):
        back.append(lax.ppermute(arrays[j], axis, [(i, mate(i, j, count)) for i in range(count)]))
    return back


def over_seq(near):
    return sum([list(pieces) for pieces in zip(*[peers_of(piece, "seq") for piece in near])], [])


def owner_of(place_ref, seqs, dps, share, j, d):
    seq, dp = place_ref[0], place_ref[2]
    k = mate(seq, j, seqs) * dps + mate(dp, d, dps)
    return k // share, k % share


def rate_line(block, depth):
    rows = block.astype(F32)
    return jnp.concatenate([rows[i : i + 1, :] for i in range(depth // 128)], axis=1)


def outer_kernel(seqs, heads, dps, share, place_ref, tok_ref, dout_ref, *refs):
    w_refs = refs[: seqs * dps]
    out_refs = refs[seqs * dps : seqs * dps + heads]
    tok_s, dout_s, acc = refs[seqs * dps + heads :]
    rows, features = tok_ref.shape
    depth = features // share
    for r in range(share):
        tok_s[r] = tok_ref[:, r * depth : (r + 1) * depth]
        dout_s[r] = dout_ref[:, r * depth : (r + 1) * depth]
    acc[...] = jnp.zeros_like(acc)
    for j in range(seqs):
        for d in range(dps):
            w = w_refs[j * dps + d]
            h, r = owner_of(place_ref, seqs, dps, share, j, d)
            line = rate_line(w[depth:, :], depth)
            logit = mm(jnp.broadcast_to(line, (EXTRA, depth)), tok_s[r], NT)
            back = mm(dout_s[r], w[0:depth, :], NN)
            acc[h] = acc[h] + jnp.concatenate([back, logit], axis=0)
    first_half = lax.broadcasted_iota(jnp.int32, (EXTRA, rows), 0) < EXTRA // 2
    for j in range(heads):
        total = acc[mate(place_ref[1], j, heads)]
        out_refs[j][0:rows, :] = total[0:rows].astype(BF16)
        logit = total[rows:]
        high = logit.astype(BF16).astype(F32)
        out_refs[j][rows:, :] = jnp.where(first_half, high, logit - high).astype(BF16)


def inner_projection_kernel(seqs, heads, dps, share, place_ref, tok_ref, *refs):
    w_refs = refs[: 2 * seqs * dps]
    out_refs = refs[2 * seqs * dps : 2 * seqs * dps + heads]
    tok_s, acc = refs[2 * seqs * dps + heads :]
    rows, features = tok_ref.shape
    depth = features // share
    half = depth // 2
    for r in range(share):
        tok_s[r] = tok_ref[:, r * depth : (r + 1) * depth]
    acc[...] = jnp.zeros_like(acc)
    for part in range(2):
        for j in range(seqs):
            for d in range(dps):
                w = w_refs[(part * seqs + j) * dps + d]
                h, r = owner_of(place_ref, seqs, dps, share, j, d)
                wide = jnp.concatenate([w[c * half : (c + 1) * half, :] for c in range(3)], axis=1)
                acc[h] = acc[h] + mm(tok_s[r][:, part * half : (part + 1) * half], wide, NN)
    for j in range(heads):
        out_refs[j][...] = acc[mate(place_ref[1], j, heads)].astype(BF16)


def inner_kernel(seqs, dps, place_ref, *refs):
    x_refs, y_refs = refs[:seqs], refs[seqs : 2 * seqs]
    w1_ref, w2_ref, res_ref = refs[2 * seqs : 2 * seqs + 3]
    dw_refs = refs[2 * seqs + 3 : 2 * seqs + 3 + dps]
    (
        qs, ks, vs, ds, es, sg, os, lg,
        w1c, w2c, w1b, w2b,
        x2s, g1s, pgs, gfs, xqs, zqs, dx2s, dg1s,
        dys, ns, rs, ss, cs, g2s, dg2s, dks, des, ws,
    ) = refs[2 * seqs + 3 + dps :]
    rows = x_refs[0].shape[0]
    hd = y_refs[0].shape[1]
    width = 4 * hd
    blocks = seqs * rows // MB
    per = rows // MB
    place = place_ref[0]

    for j in range(seqs):
        owner = mate(place, j, seqs)
        at = pl.ds(pl.multiple_of(owner * rows, rows), rows)
        qs[at, :] = x_refs[j][:, 0:hd]
        ks[at, :] = x_refs[j][:, hd : 2 * hd]
        vs[at, :] = x_refs[j][:, 2 * hd : 3 * hd]
        ds[at, :] = y_refs[j][0:rows, :]
        logit = y_refs[j][rows : rows + 8, :] + y_refs[j][rows + 8 : rows + 16, :]
        gate = jax.nn.sigmoid(logit)
        scaled = (BASE_RATE / hd) * gate
        for b in range(per):
            es[owner * per + b] = padded(scaled[:, b * MB : (b + 1) * MB])
            sg[owner * per + b] = padded((scaled * (1.0 - gate))[:, b * MB : (b + 1) * MB])

    w1c[...] = w1_ref[...]
    start = w2_ref[...]
    w2c[...] = (start - mean(start)).T

    at_row = lax.broadcasted_iota(jnp.int32, (MB, MB), 0)
    at_col = lax.broadcasted_iota(jnp.int32, (MB, MB), 1)
    causal = at_col <= at_row
    diagonal = at_col == at_row

    def to_column(line):
        return jnp.sum(jnp.where(diagonal, line, 0.0), axis=1, keepdims=True)

    def to_line(column):
        return jnp.sum(jnp.where(diagonal, column, 0.0), axis=0, keepdims=True)

    def at_block(i):
        if isinstance(i, int):
            return slice(i * MB, (i + 1) * MB)
        return pl.ds(pl.multiple_of(i * MB, MB), MB)

    def forward(i):
        at = at_block(i)
        q, k, v, d_o = qs[at, :], ks[at, :], vs[at, :], ds[at, :]
        line = es[i][0:1, 0:MB]
        e = to_column(line)
        mask = jnp.where(causal, line, 0.0)
        w1 = w1c[...].astype(BF16)
        w2 = w2c[...].astype(BF16)
        w1b[i] = w1
        w2b[i] = w2
        kb, qb = k.astype(BF16), q.astype(BF16)
        gap = v - k
        gap = gap - mean(gap)
        both = mm(jnp.concatenate([kb, qb], axis=0), w1, NN)
        x2, g1, gg1 = gelu_parts(both[:MB])
        x2b = x2.astype(BF16)
        c = mm(x2b, w2, NT)
        var = mean(c * c)
        cross = mean(gap * c)
        s = lax.rsqrt(var + EPSILON)
        n = c * s
        cc = var * s * s - s * cross
        r = n - gap
        g2 = s * (r - n * cc)
        g2b = g2.astype(BF16)
        p = mm(g2b, w2, NN)
        g1f = p * g1
        w1c[...] = w1c[...] - mm(k, e * g1f, TN)
        w2c[...] = w2c[...] - mm(e * g2, x2b, TN)
        g1b = g1f.astype(BF16)
        b1 = mm(qb, kb, NT)
        a1 = (b1 * mask).astype(BF16)
        zq = both[MB:] - mm(a1, g1b, NN)
        xq, gq = gelu_two(zq)
        xqb = xq.astype(BF16)
        b2 = mm(xqb, x2b, NT)
        a2 = (b2 * mask).astype(BF16)
        y = mm(xqb, w2, NT) - mm(a2, g2b, NN)
        sq = lax.rsqrt(mean(y * y) + EPSILON)
        nq = y * sq
        os[at, 3 * hd : 4 * hd] = (q + nq).astype(BF16)
        dy = sq * (d_o - mean(d_o) - nq * mean(d_o * nq))
        dyb = dy.astype(BF16)
        da2 = -mm(dyb, g2b, NT)
        db2 = (da2 * mask).astype(BF16)
        dg2s[i] = -mm(a2, dyb, TN)
        dxq = mm(dyb, w2, NN) + mm(db2, x2b, NN)
        dx2s[i] = mm(db2, xqb, TN)
        dzq = (dxq * gq).astype(BF16)
        da1 = -mm(dzq, g1b, NT)
        db1 = (da1 * mask).astype(BF16)
        dg1s[i] = -mm(a1, dzq, TN)
        dq = d_o + mm(dzq, w1, NT) + mm(db1, kb, NN)
        os[at, 0:hd] = dq.astype(BF16)
        dks[i] = mm(db1, qb, TN)
        de = jnp.sum(jnp.where(causal, da2 * b2 + da1 * b1, 0.0), axis=0, keepdims=True)
        des[i] = padded(jnp.broadcast_to(de, (8, MB)))
        x2s[i] = x2b
        g1s[i] = g1
        pgs[i] = p * gg1
        gfs[i] = g1f
        xqs[i] = xqb
        zqs[i] = dzq
        dys[i] = dyb
        ns[i] = n
        rs[i] = r
        ss[i] = jnp.broadcast_to(s, (MB, hd))
        cs[i] = jnp.broadcast_to(cc, (MB, hd))
        g2s[i] = g2

    def backward(i):
        at = at_block(i)
        q, k = qs[at, :], ks[at, :]
        e = to_column(es[i][0:1, 0:MB])
        w1, w2 = w1b[i], w2b[i]
        d1, d2 = w1c[...].astype(BF16), w2c[...].astype(BF16)
        x2b, g1, g1f, g2 = x2s[i], g1s[i], gfs[i], g2s[i]
        n, s, cc = ns[i], ss[i], cs[i]
        dh1 = -mm(k, d1, NN)
        dh2 = -mm(x2b, d2, NT)
        dg1 = dg1s[i] + e * dh1
        dp = (dg1 * g1).astype(BF16)
        dg2 = dg2s[i] + e * dh2 + mm(dp, w2, NT)
        dt = s * dg2
        mt = mean(dt * n)
        dr = dt - mean(dt) - n * mt
        dn = dr - cc * dt - rs[i] * mt
        du = s * (dn - mean(dn) - n * (mean(dn * n) + mean(dg2 * g2)))
        dub = du.astype(BF16)
        mixed = jnp.concatenate([(-e * g2).astype(BF16), dub], axis=1)
        dx2 = dx2s[i] + mm(mixed, jnp.concatenate([d2, w2], axis=0), NN)
        dz1 = (dg1 * pgs[i] + dx2 * g1).astype(BF16)
        mixed = jnp.concatenate([(-e * g1f).astype(BF16), dz1], axis=1)
        dk = dks[i] + dr + mm(mixed, jnp.concatenate([d1, w1], axis=1), NT)
        w1c[...] = w1c[...] + mm(
            jnp.concatenate([q, k], axis=0), jnp.concatenate([zqs[i], dz1], axis=0), TN
        )
        w2c[...] = w2c[...] + mm(
            jnp.concatenate([dys[i].astype(F32), du, g2], axis=0),
            jnp.concatenate([xqs[i], x2b, dp], axis=0),
            TN,
        )
        extra = jnp.sum(g1f * dh1, axis=1, keepdims=True) + jnp.sum(
            g2 * dh2, axis=1, keepdims=True
        )
        line = (des[i][0:1, 0:MB] + to_line(extra)) * sg[i][0:1, 0:MB]
        lg[i] = padded(jnp.broadcast_to(line, (8, MB)))
        os[at, hd : 2 * hd] = dk.astype(BF16)
        os[at, 2 * hd : 3 * hd] = (-dr).astype(BF16)

    def loop(step, order):
        if blocks <= UNROLL_LIMIT:
            for i in range(blocks):
                step(order(i))
        else:
            lax.fori_loop(0, blocks, lambda i, unused: (step(order(i)), unused)[1], 0)

    loop(forward, lambda i: i)
    w1c[...] = jnp.zeros_like(w1c)
    w2c[...] = jnp.zeros_like(w2c)
    loop(backward, lambda i: blocks - 1 - i)

    res_ref[0:rows, :] = os[pl.ds(pl.multiple_of(place * rows, rows), rows), :]
    res_ref[rows:, :] = jnp.zeros((EXTRA, width), BF16)
    first_row = lax.broadcasted_iota(jnp.int32, (EXTRA, rows), 0) == 0
    lines = jnp.concatenate([lg[place * per + b][0:1, 0:MB] for b in range(per)], axis=1)
    lines = jnp.where(first_row, jnp.broadcast_to(lines, (EXTRA, rows)), 0.0)
    res_ref[rows:, 0:rows] = lines.astype(BF16)

    part = dw_refs[0].shape[0]
    ws[:, 0:hd] = w1c[...].T
    ws[:, hd : 2 * hd] = w2c[...].T
    for d in range(dps):
        first = (place * dps + mate(place_ref[2], d, dps)) * part
        dw_refs[d][...] = ws[pl.ds(pl.multiple_of(first, part), part), :]


def output_kernel(seqs, heads, dps, share, place_ref, *refs):
    got_refs, refs = refs[:heads], refs[heads:]
    o_refs, w_refs = refs[: seqs * dps], refs[seqs * dps : 3 * seqs * dps]
    out_ref, dtok_ref, got, out_s, grad_s = refs[3 * seqs * dps :]
    hd = o_refs[0].shape[1]
    rows, features = out_ref.shape
    depth = features // share
    half = depth // 2
    for j in range(heads):
        got[mate(place_ref[1], j, heads)] = got_refs[j][...]
    out_s[...] = jnp.zeros_like(out_s)
    grad_s[...] = jnp.zeros_like(grad_s)
    for j in range(seqs):
        for d in range(dps):
            o = o_refs[j * dps + d]
            h, r = owner_of(place_ref, seqs, dps, share, j, d)
            out_s[r] = out_s[r] + mm(got[h, 0:rows, 3 * hd :], o[0:depth, :], NT)
            line = rate_line(o[depth:, :], depth)
            logit = got[h, rows:, 0:rows].astype(F32).T
            grad = [mm(logit, jnp.broadcast_to(line, (EXTRA, depth)), NN)]
            mine = got[h, 0:rows, 0 : 3 * hd]
            halves = []
            for part in range(2):
                w = w_refs[(part * seqs + j) * dps + d]
                wide = jnp.concatenate([w[c * half : (c + 1) * half, :] for c in range(3)], axis=1)
                halves.append(mm(mine, wide, NT))
            grad_s[r] = grad_s[r] + grad[0] + jnp.concatenate(halves, axis=1)
    for r in range(share):
        out_ref[:, r * depth : (r + 1) * depth] = out_s[r].astype(BF16)
        dtok_ref[:, r * depth : (r + 1) * depth] = grad_s[r].astype(BF16)


VMEM = pl.BlockSpec(memory_space=pltpu.VMEM)
SMEM = pl.BlockSpec(memory_space=pltpu.SMEM)
MIB = 1024 * 1024


def call(kernel, outs, operands, scratch=(), mib=16):
    return pl.pallas_call(
        kernel,
        out_shape=outs,
        in_specs=[SMEM] + [VMEM] * (len(operands) - 1),
        out_specs=jax.tree.map(lambda unused: VMEM, outs),
        scratch_shapes=list(scratch),
        compiler_params=pltpu.CompilerParams(vmem_limit_bytes=mib * MIB),
    )(*operands)


def body(tokens, w_qkv, w_lr, w_out, w1_init, w2_init, d_out):
    seqs, heads, dps = (lax.axis_size(a) for a in ("seq", "head", "dp"))
    share = seqs * dps // heads
    rows, features = tokens.shape[1:]
    depth, unused, hd = w_qkv.shape
    inner = w1_init.shape[2]
    blocks = seqs * rows // MB
    place = jnp.stack([lax.axis_index(a).astype(jnp.int32) for a in ("seq", "head", "dp")])
    sizes = (seqs, heads, dps, share)
    place, w_out, w_qkv = lax.optimization_barrier((place, w_out, w_qkv))

    pairs = []
    for seq in range(seqs):
        for head in range(heads):
            for dp in range(dps):
                k = seq * dps + dp
                target = head * share + k % share
                to = ((target // dps) * heads + k // share) * dps + target % dps
                pairs.append(((seq * heads + head) * dps + dp, to))

    def swapped(array):
        return lax.ppermute(array, ("seq", "head", "dp"), pairs)

    half = depth // 2
    lines = w_lr[:, 0].reshape(seqs * dps, depth // 128, 128)
    line = lax.dynamic_index_in_dim(
        lines, lax.axis_index("seq") * dps + lax.axis_index("dp"), 0, keepdims=False
    )
    line = jnp.pad(line, ((0, EXTRA - depth // 128), (0, 0)))
    by_kind = w_qkv.transpose(1, 0, 2)
    first, second, outer = lax.optimization_barrier(
        (
            by_kind[:, :half].reshape(3 * half, hd),
            by_kind[:, half:].reshape(3 * half, hd),
            jnp.concatenate([w_out, line], axis=0),
        )
    )
    first_w, second_w, outer_w = swapped(first), swapped(second), swapped(outer)
    first_near = [first_w, hop(first_w, "dp", 1), hop(first_w, "dp", 2)]
    outer_w, unused = lax.optimization_barrier((outer_w, second_w))
    outer_near = peers_of(outer_w, "dp")
    second_near = [second_w, hop(second_w, "dp", 1), hop(second_w, "dp", 2)]
    outer_ws = over_seq(outer_near)
    def summed(arrays):
        return functools.reduce(lambda a, b: a + b, [a.astype(F32) for a in arrays])

    outer_part = call(
        functools.partial(outer_kernel, *sizes),
        (jax.ShapeDtypeStruct((rows + EXTRA, hd), BF16),) * heads,
        (place, tokens[0], d_out[0], *outer_ws),
        [pltpu.VMEM((share, rows, features // share), BF16)] * 2
        + [pltpu.VMEM((heads, rows + EXTRA, hd), F32)],
    )
    outer_all = peers_of(summed(sent_to(outer_part, "head")), "seq")
    if dps == 4:
        first_near[1], second_near[2], unused = lax.optimization_barrier(
            (first_near[1], second_near[2], outer_part[0])
        )
        first_near.append(hop(first_near[1], "dp", 2))
        second_near.append(hop(second_near[2], "dp", 1))
    else:
        first_near += [hop(first_w, "dp", j) for j in range(3, dps)]
        second_near += [hop(second_w, "dp", j) for j in range(3, dps)]
    inner_ws = over_seq(first_near) + over_seq(second_near)
    later_place, unused = lax.optimization_barrier((place, outer_all[-1]))
    inner_part = call(
        functools.partial(inner_projection_kernel, *sizes),
        (jax.ShapeDtypeStruct((rows, 3 * hd), BF16),) * heads,
        (later_place, tokens[0], *inner_ws),
        [
            pltpu.VMEM((share, rows, features // share), BF16),
            pltpu.VMEM((heads, rows, 3 * hd), F32),
        ],
    )
    inner_all = peers_of(summed(sent_to(inner_part, "head")), "seq")

    long = seqs * rows
    scratch = (
        [pltpu.VMEM((long, hd), F32)] * 4
        + [pltpu.VMEM((blocks, 8, 2 * MB), F32)] * 2
        + [pltpu.VMEM((long, 4 * hd), BF16), pltpu.VMEM((blocks, 8, 2 * MB), F32)]
        + [pltpu.VMEM((hd, inner), F32)] * 2
        + [pltpu.VMEM((blocks, hd, inner), BF16)] * 2
        + [pltpu.VMEM((blocks, MB, inner), t) for t in (BF16, F32, F32, F32, BF16, BF16, F32, F32)]
        + [pltpu.VMEM((blocks, MB, hd), t) for t in (BF16, F32, F32, F32, F32, F32, F32, F32)]
        + [pltpu.VMEM((blocks, 8, 2 * MB), F32), pltpu.VMEM((inner, 2 * hd), F32)]
    )
    part = inner // (seqs * dps)
    result, *d_inner = call(
        functools.partial(inner_kernel, seqs, dps),
        (jax.ShapeDtypeStruct((rows + EXTRA, 4 * hd), BF16),)
        + (jax.ShapeDtypeStruct((part, 2 * hd), F32),) * dps,
        (place, *inner_all, *outer_all, w1_init[0], w2_init[0]),
        scratch,
        14 + 2 * blocks,
    )
    got = peers_of(result, "head")
    unused, *d_inner = lax.optimization_barrier((got[1], *d_inner))
    shares = summed(sent_to(d_inner, "dp"))
    out, d_tokens = call(
        functools.partial(output_kernel, *sizes),
        (jax.ShapeDtypeStruct((rows, features), BF16),) * 2,
        (place, *got, *outer_ws, *inner_ws),
        [
            pltpu.VMEM((heads, rows + EXTRA, 4 * hd), BF16),
            pltpu.VMEM((share, rows, features // share), F32),
            pltpu.VMEM((share, rows, features // share), F32),
        ],
    )
    return (out[None], d_tokens[None], shares[:, :hd].transpose(1, 0)[None], shares[:, hd:][None])


def solution(mesh):
    placed = (
        P("dp", "seq", "head"),
        P(("seq", "dp"), None, "head"),
        P(None, "head"),
        P(("seq", "dp"), "head"),
        P("head", None, None),
        P("head", None, None),
        P("dp", "seq", "head"),
    )
    return jax.shard_map(
        body,
        mesh=mesh,
        in_specs=placed,
        out_specs=(
            P("dp", "seq", "head"),
            P("dp", "seq", "head"),
            P("head", None, ("seq", "dp")),
            P("head", ("seq", "dp"), None),
        ),
        check_vma=False,
    )
```

```python
import functools

import jax
import jax.numpy as jnp
from jax import lax
from jax.experimental import pallas as pl
from jax.experimental.pallas import tpu as pltpu
from jax.sharding import PartitionSpec as P

MB = 64
EPSILON = 1e-06
BASE_RATE = 0.1
GELU_SCALE = 0.7978845608028654
GELU_CUBIC = 0.044715
NN = ((1,), (0,))
NT = ((1,), (1,))
TN = ((0,), (0,))
EXTRA = 16
UNROLL_LIMIT = 8
F32 = jnp.float32
BF16 = jnp.bfloat16


def mm(left, right, dims):
    return lax.dot_general(
        left.astype(BF16), right.astype(BF16), (dims, ((), ())), preferred_element_type=F32
    )


def padded(lines):
    return jnp.concatenate([lines, jnp.zeros_like(lines)], axis=1)


def mean(rows):
    return jnp.mean(rows, axis=-1, keepdims=True)


def gelu_parts(v):
    square = v * v
    bend = jnp.tanh(v * (GELU_SCALE + (GELU_SCALE * GELU_CUBIC) * square))
    half = 0.5 + 0.5 * bend
    slope = GELU_SCALE + (3.0 * GELU_SCALE * GELU_CUBIC) * square
    bell = 0.5 - 0.5 * bend * bend
    lean = bell * slope
    second = 2.0 * lean * (1.0 - v * bend * slope) + (6.0 * GELU_SCALE * GELU_CUBIC) * square * bell
    return v * half, half + v * lean, second


def gelu_two(v):
    square = v * v
    bend = jnp.tanh(v * (GELU_SCALE + (GELU_SCALE * GELU_CUBIC) * square))
    half = 0.5 + 0.5 * bend
    slope = GELU_SCALE + (3.0 * GELU_SCALE * GELU_CUBIC) * square
    return v * half, half + v * ((0.5 - 0.5 * bend * bend) * slope)


def mate(index, step, count):
    if count & (count - 1) == 0:
        return index ^ step
    return (index + step) % count


def hop(array, axis, step):
    count = lax.axis_size(axis)
    return lax.ppermute(array, axis, [(mate(i, step, count), i) for i in range(count)])


def peers_of(array, axis):
    return [array] + [hop(array, axis, j) for j in range(1, lax.axis_size(axis))]


def sent_to(arrays, axis):
    count = lax.axis_size(axis)
    back = [arrays[0]]
    for j in range(1, count):
        back.append(lax.ppermute(arrays[j], axis, [(i, mate(i, j, count)) for i in range(count)]))
    return back


def over_seq(near):
    return sum([list(pieces) for pieces in zip(*[peers_of(piece, "seq") for piece in near])], [])


def owner_of(place_ref, seqs, dps, share, j, d):
    seq, dp = place_ref[0], place_ref[2]
    k = mate(seq, j, seqs) * dps + mate(dp, d, dps)
    return k // share, k % share


def rate_line(block, depth):
    rows = block.astype(F32)
    return jnp.concatenate([rows[i : i + 1, :] for i in range(depth // 128)], axis=1)


def outer_kernel(seqs, heads, dps, share, place_ref, tok_ref, dout_ref, *refs):
    w_refs = refs[: seqs * dps]
    out_refs = refs[seqs * dps : seqs * dps + heads]
    tok_s, dout_s, acc = refs[seqs * dps + heads :]
    rows, features = tok_ref.shape
    depth = features // share
    for r in range(share):
        tok_s[r] = tok_ref[:, r * depth : (r + 1) * depth]
        dout_s[r] = dout_ref[:, r * depth : (r + 1) * depth]
    acc[...] = jnp.zeros_like(acc)
    for j in range(seqs):
        for d in range(dps):
            w = w_refs[j * dps + d]
            h, r = owner_of(place_ref, seqs, dps, share, j, d)
            line = rate_line(w[depth:, :], depth)
            logit = mm(jnp.broadcast_to(line, (EXTRA, depth)), tok_s[r], NT)
            back = mm(dout_s[r], w[0:depth, :], NN)
            acc[h] = acc[h] + jnp.concatenate([back, logit], axis=0)
    first_half = lax.broadcasted_iota(jnp.int32, (EXTRA, rows), 0) < EXTRA // 2
    for j in range(heads):
        total = acc[mate(place_ref[1], j, heads)]
        out_refs[j][0:rows, :] = total[0:rows].astype(BF16)
        logit = total[rows:]
        high = logit.astype(BF16).astype(F32)
        out_refs[j][rows:, :] = jnp.where(first_half, high, logit - high).astype(BF16)


def inner_projection_kernel(seqs, heads, dps, share, place_ref, tok_ref, *refs):
    w_refs = refs[: 2 * seqs * dps]
    out_refs = refs[2 * seqs * dps : 2 * seqs * dps + heads]
    tok_s, acc = refs[2 * seqs * dps + heads :]
    rows, features = tok_ref.shape
    depth = features // share
    half = depth // 2
    for r in range(share):
        tok_s[r] = tok_ref[:, r * depth : (r + 1) * depth]
    acc[...] = jnp.zeros_like(acc)
    for part in range(2):
        for j in range(seqs):
            for d in range(dps):
                w = w_refs[(part * seqs + j) * dps + d]
                h, r = owner_of(place_ref, seqs, dps, share, j, d)
                wide = jnp.concatenate([w[c * half : (c + 1) * half, :] for c in range(3)], axis=1)
                acc[h] = acc[h] + mm(tok_s[r][:, part * half : (part + 1) * half], wide, NN)
    for j in range(heads):
        out_refs[j][...] = acc[mate(place_ref[1], j, heads)].astype(BF16)


def inner_kernel(seqs, dps, place_ref, *refs):
    x_refs, y_refs = refs[:seqs], refs[seqs : 2 * seqs]
    w1_ref, w2_ref, res_ref = refs[2 * seqs : 2 * seqs + 3]
    dw_refs = refs[2 * seqs + 3 : 2 * seqs + 3 + dps]
    (
        qs, ks, vs, ds, es, sg, os, lg,
        w1c, w2c, w1b, w2b,
        x2s, g1s, pgs, gfs, xqs, zqs, dx2s, dg1s,
        dys, ns, rs, ss, cs, g2s, dg2s, dks, des, ws,
    ) = refs[2 * seqs + 3 + dps :]
    rows = x_refs[0].shape[0]
    hd = y_refs[0].shape[1]
    width = 4 * hd
    blocks = seqs * rows // MB
    per = rows // MB
    place = place_ref[0]

    for j in range(seqs):
        owner = mate(place, j, seqs)
        at = pl.ds(pl.multiple_of(owner * rows, rows), rows)
        qs[at, :] = x_refs[j][:, 0:hd]
        ks[at, :] = x_refs[j][:, hd : 2 * hd]
        vs[at, :] = x_refs[j][:, 2 * hd : 3 * hd]
        ds[at, :] = y_refs[j][0:rows, :]
        logit = y_refs[j][rows : rows + 8, :] + y_refs[j][rows + 8 : rows + 16, :]
        gate = jax.nn.sigmoid(logit)
        scaled = (BASE_RATE / hd) * gate
        for b in range(per):
            es[owner * per + b] = padded(scaled[:, b * MB : (b + 1) * MB])
            sg[owner * per + b] = padded((scaled * (1.0 - gate))[:, b * MB : (b + 1) * MB])

    w1c[...] = w1_ref[...]
    start = w2_ref[...]
    w2c[...] = (start - mean(start)).T

    at_row = lax.broadcasted_iota(jnp.int32, (MB, MB), 0)
    at_col = lax.broadcasted_iota(jnp.int32, (MB, MB), 1)
    causal = at_col <= at_row
    diagonal = at_col == at_row

    def to_column(line):
        return jnp.sum(jnp.where(diagonal, line, 0.0), axis=1, keepdims=True)

    def to_line(column):
        return jnp.sum(jnp.where(diagonal, column, 0.0), axis=0, keepdims=True)

    def at_block(i):
        if isinstance(i, int):
            return slice(i * MB, (i + 1) * MB)
        return pl.ds(pl.multiple_of(i * MB, MB), MB)

    def forward(i):
        at = at_block(i)
        q, k, v, d_o = qs[at, :], ks[at, :], vs[at, :], ds[at, :]
        line = es[i][0:1, 0:MB]
        e = to_column(line)
        mask = jnp.where(causal, line, 0.0)
        w1 = w1c[...].astype(BF16)
        w2 = w2c[...].astype(BF16)
        w1b[i] = w1
        w2b[i] = w2
        kb, qb = k.astype(BF16), q.astype(BF16)
        gap = v - k
        gap = gap - mean(gap)
        both = mm(jnp.concatenate([kb, qb], axis=0), w1, NN)
        x2, g1, gg1 = gelu_parts(both[:MB])
        x2b = x2.astype(BF16)
        c = mm(x2b, w2, NT)
        var = mean(c * c)
        cross = mean(gap * c)
        s = lax.rsqrt(var + EPSILON)
        n = c * s
        cc = var * s * s - s * cross
        r = n - gap
        g2 = s * (r - n * cc)
        g2b = g2.astype(BF16)
        p = mm(g2b, w2, NN)
        g1f = p * g1
        w1c[...] = w1c[...] - mm(k, e * g1f, TN)
        w2c[...] = w2c[...] - mm(e * g2, x2b, TN)
        g1b = g1f.astype(BF16)
        b1 = mm(qb, kb, NT)
        a1 = (b1 * mask).astype(BF16)
        zq = both[MB:] - mm(a1, g1b, NN)
        xq, gq = gelu_two(zq)
        xqb = xq.astype(BF16)
        b2 = mm(xqb, x2b, NT)
        a2 = (b2 * mask).astype(BF16)
        y = mm(xqb, w2, NT) - mm(a2, g2b, NN)
        sq = lax.rsqrt(mean(y * y) + EPSILON)
        nq = y * sq
        os[at, 3 * hd : 4 * hd] = (q + nq).astype(BF16)
        dy = sq * (d_o - mean(d_o) - nq * mean(d_o * nq))
        dyb = dy.astype(BF16)
        da2 = -mm(dyb, g2b, NT)
        db2 = (da2 * mask).astype(BF16)
        dg2s[i] = -mm(a2, dyb, TN)
        dxq = mm(dyb, w2, NN) + mm(db2, x2b, NN)
        dx2s[i] = mm(db2, xqb, TN)
        dzq = (dxq * gq).astype(BF16)
        da1 = -mm(dzq, g1b, NT)
        db1 = (da1 * mask).astype(BF16)
        dg1s[i] = -mm(a1, dzq, TN)
        dq = d_o + mm(dzq, w1, NT) + mm(db1, kb, NN)
        os[at, 0:hd] = dq.astype(BF16)
        dks[i] = mm(db1, qb, TN)
        de = jnp.sum(jnp.where(causal, da2 * b2 + da1 * b1, 0.0), axis=0, keepdims=True)
        des[i] = padded(jnp.broadcast_to(de, (8, MB)))
        x2s[i] = x2b
        g1s[i] = g1
        pgs[i] = p * gg1
        gfs[i] = g1f
        xqs[i] = xqb
        zqs[i] = dzq
        dys[i] = dyb
        ns[i] = n
        rs[i] = r
        ss[i] = jnp.broadcast_to(s, (MB, hd))
        cs[i] = jnp.broadcast_to(cc, (MB, hd))
        g2s[i] = g2

    def backward(i):
        at = at_block(i)
        q, k = qs[at, :], ks[at, :]
        e = to_column(es[i][0:1, 0:MB])
        w1, w2 = w1b[i], w2b[i]
        d1, d2 = w1c[...].astype(BF16), w2c[...].astype(BF16)
        x2b, g1, g1f, g2 = x2s[i], g1s[i], gfs[i], g2s[i]
        n, s, cc = ns[i], ss[i], cs[i]
        dh1 = -mm(k, d1, NN)
        dh2 = -mm(x2b, d2, NT)
        dg1 = dg1s[i] + e * dh1
        dp = (dg1 * g1).astype(BF16)
        dg2 = dg2s[i] + e * dh2 + mm(dp, w2, NT)
        dt = s * dg2
        mt = mean(dt * n)
        dr = dt - mean(dt) - n * mt
        dn = dr - cc * dt - rs[i] * mt
        du = s * (dn - mean(dn) - n * (mean(dn * n) + mean(dg2 * g2)))
        dub = du.astype(BF16)
        mixed = jnp.concatenate([(-e * g2).astype(BF16), dub], axis=1)
        dx2 = dx2s[i] + mm(mixed, jnp.concatenate([d2, w2], axis=0), NN)
        dz1 = (dg1 * pgs[i] + dx2 * g1).astype(BF16)
        mixed = jnp.concatenate([(-e * g1f).astype(BF16), dz1], axis=1)
        dk = dks[i] + dr + mm(mixed, jnp.concatenate([d1, w1], axis=1), NT)
        w1c[...] = w1c[...] + mm(
            jnp.concatenate([q, k], axis=0), jnp.concatenate([zqs[i], dz1], axis=0), TN
        )
        w2c[...] = w2c[...] + mm(
            jnp.concatenate([dys[i].astype(F32), du, g2], axis=0),
            jnp.concatenate([xqs[i], x2b, dp], axis=0),
            TN,
        )
        extra = jnp.sum(g1f * dh1, axis=1, keepdims=True) + jnp.sum(
            g2 * dh2, axis=1, keepdims=True
        )
        line = (des[i][0:1, 0:MB] + to_line(extra)) * sg[i][0:1, 0:MB]
        lg[i] = padded(jnp.broadcast_to(line, (8, MB)))
        os[at, hd : 2 * hd] = dk.astype(BF16)
        os[at, 2 * hd : 3 * hd] = (-dr).astype(BF16)

    def loop(step, order):
        if blocks <= UNROLL_LIMIT:
            for i in range(blocks):
                step(order(i))
        else:
            lax.fori_loop(0, blocks, lambda i, unused: (step(order(i)), unused)[1], 0)

    loop(forward, lambda i: i)
    w1c[...] = jnp.zeros_like(w1c)
    w2c[...] = jnp.zeros_like(w2c)
    loop(backward, lambda i: blocks - 1 - i)

    res_ref[0:rows, :] = os[pl.ds(pl.multiple_of(place * rows, rows), rows), :]
    res_ref[rows:, :] = jnp.zeros((EXTRA, width), BF16)
    first_row = lax.broadcasted_iota(jnp.int32, (EXTRA, rows), 0) == 0
    lines = jnp.concatenate([lg[place * per + b][0:1, 0:MB] for b in range(per)], axis=1)
    lines = jnp.where(first_row, jnp.broadcast_to(lines, (EXTRA, rows)), 0.0)
    res_ref[rows:, 0:rows] = lines.astype(BF16)

    part = dw_refs[0].shape[0]
    ws[:, 0:hd] = w1c[...].T
    ws[:, hd : 2 * hd] = w2c[...].T
    for d in range(dps):
        first = (place * dps + mate(place_ref[2], d, dps)) * part
        dw_refs[d][...] = ws[pl.ds(pl.multiple_of(first, part), part), :]


def output_kernel(seqs, heads, dps, share, place_ref, *refs):
    got_refs, refs = refs[:heads], refs[heads:]
    o_refs, w_refs = refs[: seqs * dps], refs[seqs * dps : 3 * seqs * dps]
    out_ref, dtok_ref, got, out_s, grad_s = refs[3 * seqs * dps :]
    hd = o_refs[0].shape[1]
    rows, features = out_ref.shape
    depth = features // share
    half = depth // 2
    for j in range(heads):
        got[mate(place_ref[1], j, heads)] = got_refs[j][...]
    out_s[...] = jnp.zeros_like(out_s)
    grad_s[...] = jnp.zeros_like(grad_s)
    for j in range(seqs):
        for d in range(dps):
            o = o_refs[j * dps + d]
            h, r = owner_of(place_ref, seqs, dps, share, j, d)
            out_s[r] = out_s[r] + mm(got[h, 0:rows, 3 * hd :], o[0:depth, :], NT)
            line = rate_line(o[depth:, :], depth)
            logit = got[h, rows:, 0:rows].astype(F32).T
            grad = [mm(logit, jnp.broadcast_to(line, (EXTRA, depth)), NN)]
            mine = got[h, 0:rows, 0 : 3 * hd]
            halves = []
            for part in range(2):
                w = w_refs[(part * seqs + j) * dps + d]
                wide = jnp.concatenate([w[c * half : (c + 1) * half, :] for c in range(3)], axis=1)
                halves.append(mm(mine, wide, NT))
            grad_s[r] = grad_s[r] + grad[0] + jnp.concatenate(halves, axis=1)
    for r in range(share):
        out_ref[:, r * depth : (r + 1) * depth] = out_s[r].astype(BF16)
        dtok_ref[:, r * depth : (r + 1) * depth] = grad_s[r].astype(BF16)


VMEM = pl.BlockSpec(memory_space=pltpu.VMEM)
SMEM = pl.BlockSpec(memory_space=pltpu.SMEM)
MIB = 1024 * 1024


def call(kernel, outs, operands, scratch=(), mib=16):
    return pl.pallas_call(
        kernel,
        out_shape=outs,
        in_specs=[SMEM] + [VMEM] * (len(operands) - 1),
        out_specs=jax.tree.map(lambda unused: VMEM, outs),
        scratch_shapes=list(scratch),
        compiler_params=pltpu.CompilerParams(vmem_limit_bytes=mib * MIB),
    )(*operands)


def body(tokens, w_qkv, w_lr, w_out, w1_init, w2_init, d_out):
    seqs, heads, dps = (lax.axis_size(a) for a in ("seq", "head", "dp"))
    share = seqs * dps // heads
    rows, features = tokens.shape[1:]
    depth, unused, hd = w_qkv.shape
    inner = w1_init.shape[2]
    blocks = seqs * rows // MB
    place = jnp.stack([lax.axis_index(a).astype(jnp.int32) for a in ("seq", "head", "dp")])
    sizes = (seqs, heads, dps, share)
    place, w_out, w_qkv = lax.optimization_barrier((place, w_out, w_qkv))

    pairs = []
    for seq in range(seqs):
        for head in range(heads):
            for dp in range(dps):
                k = seq * dps + dp
                target = head * share + k % share
                to = ((target // dps) * heads + k // share) * dps + target % dps
                pairs.append(((seq * heads + head) * dps + dp, to))

    def swapped(array):
        return lax.ppermute(array, ("seq", "head", "dp"), pairs)

    half = depth // 2
    lines = w_lr[:, 0].reshape(seqs * dps, depth // 128, 128)
    line = lax.dynamic_index_in_dim(
        lines, lax.axis_index("seq") * dps + lax.axis_index("dp"), 0, keepdims=False
    )
    line = jnp.pad(line, ((0, EXTRA - depth // 128), (0, 0)))
    by_kind = w_qkv.transpose(1, 0, 2)
    first, second, outer = lax.optimization_barrier(
        (
            by_kind[:, :half].reshape(3 * half, hd),
            by_kind[:, half:].reshape(3 * half, hd),
            jnp.concatenate([w_out, line], axis=0),
        )
    )
    first_w, second_w, outer_w = swapped(first), swapped(second), swapped(outer)
    outer_w, first_w, second_w = lax.optimization_barrier((outer_w, first_w, second_w))
    first_near = [first_w, hop(first_w, "dp", 1), hop(first_w, "dp", 2)]
    outer_near = peers_of(outer_w, "dp")
    second_near = [second_w, hop(second_w, "dp", 1), hop(second_w, "dp", 2)]
    outer_ws = over_seq(outer_near)
    def summed(arrays):
        return functools.reduce(lambda a, b: a + b, [a.astype(F32) for a in arrays])

    outer_part = call(
        functools.partial(outer_kernel, *sizes),
        (jax.ShapeDtypeStruct((rows + EXTRA, hd), BF16),) * heads,
        (place, tokens[0], d_out[0], *outer_ws),
        [pltpu.VMEM((share, rows, features // share), BF16)] * 2
        + [pltpu.VMEM((heads, rows + EXTRA, hd), F32)],
    )
    outer_all = peers_of(summed(sent_to(outer_part, "head")), "seq")
    if dps == 4:
        first_near[1], second_near[2], unused = lax.optimization_barrier(
            (first_near[1], second_near[2], outer_part[0])
        )
        first_near.append(hop(first_near[1], "dp", 2))
        second_near.append(hop(second_near[2], "dp", 1))
    else:
        first_near += [hop(first_w, "dp", j) for j in range(3, dps)]
        second_near += [hop(second_w, "dp", j) for j in range(3, dps)]
    inner_ws = over_seq(first_near) + over_seq(second_near)
    later_place, unused = lax.optimization_barrier((place, outer_all[-1]))
    inner_part = call(
        functools.partial(inner_projection_kernel, *sizes),
        (jax.ShapeDtypeStruct((rows, 3 * hd), BF16),) * heads,
        (later_place, tokens[0], *inner_ws),
        [
            pltpu.VMEM((share, rows, features // share), BF16),
            pltpu.VMEM((heads, rows, 3 * hd), F32),
        ],
    )
    inner_all = peers_of(summed(sent_to(inner_part, "head")), "seq")

    long = seqs * rows
    scratch = (
        [pltpu.VMEM((long, hd), F32)] * 4
        + [pltpu.VMEM((blocks, 8, 2 * MB), F32)] * 2
        + [pltpu.VMEM((long, 4 * hd), BF16), pltpu.VMEM((blocks, 8, 2 * MB), F32)]
        + [pltpu.VMEM((hd, inner), F32)] * 2
        + [pltpu.VMEM((blocks, hd, inner), BF16)] * 2
        + [pltpu.VMEM((blocks, MB, inner), t) for t in (BF16, F32, F32, F32, BF16, BF16, F32, F32)]
        + [pltpu.VMEM((blocks, MB, hd), t) for t in (BF16, F32, F32, F32, F32, F32, F32, F32)]
        + [pltpu.VMEM((blocks, 8, 2 * MB), F32), pltpu.VMEM((inner, 2 * hd), F32)]
    )
    part = inner // (seqs * dps)
    result, *d_inner = call(
        functools.partial(inner_kernel, seqs, dps),
        (jax.ShapeDtypeStruct((rows + EXTRA, 4 * hd), BF16),)
        + (jax.ShapeDtypeStruct((part, 2 * hd), F32),) * dps,
        (place, *inner_all, *outer_all, w1_init[0], w2_init[0]),
        scratch,
        14 + 2 * blocks,
    )
    got = peers_of(result, "head")
    unused, *d_inner = lax.optimization_barrier((got[1], *d_inner))
    shares = summed(sent_to(d_inner, "dp"))
    out, d_tokens = call(
        functools.partial(output_kernel, *sizes),
        (jax.ShapeDtypeStruct((rows, features), BF16),) * 2,
        (place, *got, *outer_ws, *inner_ws),
        [
            pltpu.VMEM((heads, rows + EXTRA, 4 * hd), BF16),
            pltpu.VMEM((share, rows, features // share), F32),
            pltpu.VMEM((share, rows, features // share), F32),
        ],
    )
    return (out[None], d_tokens[None], shares[:, :hd].transpose(1, 0)[None], shares[:, hd:][None])


def solution(mesh):
    placed = (
        P("dp", "seq", "head"),
        P(("seq", "dp"), None, "head"),
        P(None, "head"),
        P(("seq", "dp"), "head"),
        P("head", None, None),
        P("head", None, None),
        P("dp", "seq", "head"),
    )
    return jax.shard_map(
        body,
        mesh=mesh,
        in_specs=placed,
        out_specs=(
            P("dp", "seq", "head"),
            P("dp", "seq", "head"),
            P("head", None, ("seq", "dp")),
            P("head", ("seq", "dp"), None),
        ),
        check_vma=False,
    )
```

```python
import functools

import jax
import jax.numpy as jnp
from jax import lax
from jax.experimental import pallas as pl
from jax.experimental.pallas import tpu as pltpu
from jax.sharding import PartitionSpec as P

MB = 64
EPSILON = 1e-06
BASE_RATE = 0.1
GELU_SCALE = 0.7978845608028654
GELU_CUBIC = 0.044715
NN = ((1,), (0,))
NT = ((1,), (1,))
TN = ((0,), (0,))
EXTRA = 16
UNROLL_LIMIT = 8
F32 = jnp.float32
BF16 = jnp.bfloat16


def mm(left, right, dims):
    return lax.dot_general(
        left.astype(BF16), right.astype(BF16), (dims, ((), ())), preferred_element_type=F32
    )


def padded(lines):
    return jnp.concatenate([lines, jnp.zeros_like(lines)], axis=1)


def mean(rows):
    return jnp.mean(rows, axis=-1, keepdims=True)


def gelu_parts(v):
    square = v * v
    bend = jnp.tanh(v * (GELU_SCALE + (GELU_SCALE * GELU_CUBIC) * square))
    half = 0.5 + 0.5 * bend
    slope = GELU_SCALE + (3.0 * GELU_SCALE * GELU_CUBIC) * square
    bell = 0.5 - 0.5 * bend * bend
    lean = bell * slope
    second = 2.0 * lean * (1.0 - v * bend * slope) + (6.0 * GELU_SCALE * GELU_CUBIC) * square * bell
    return v * half, half + v * lean, second


def gelu_two(v):
    square = v * v
    bend = jnp.tanh(v * (GELU_SCALE + (GELU_SCALE * GELU_CUBIC) * square))
    half = 0.5 + 0.5 * bend
    slope = GELU_SCALE + (3.0 * GELU_SCALE * GELU_CUBIC) * square
    return v * half, half + v * ((0.5 - 0.5 * bend * bend) * slope)


def mate(index, step, count):
    if count & (count - 1) == 0:
        return index ^ step
    return (index + step) % count


def hop(array, axis, step):
    count = lax.axis_size(axis)
    return lax.ppermute(array, axis, [(mate(i, step, count), i) for i in range(count)])


def peers_of(array, axis):
    return [array] + [hop(array, axis, j) for j in range(1, lax.axis_size(axis))]


def sent_to(arrays, axis):
    count = lax.axis_size(axis)
    back = [arrays[0]]
    for j in range(1, count):
        back.append(lax.ppermute(arrays[j], axis, [(i, mate(i, j, count)) for i in range(count)]))
    return back


def over_seq(near):
    return sum([list(pieces) for pieces in zip(*[peers_of(piece, "seq") for piece in near])], [])


def owner_of(place_ref, seqs, dps, share, j, d):
    seq, dp = place_ref[0], place_ref[2]
    k = mate(seq, j, seqs) * dps + mate(dp, d, dps)
    return k // share, k % share


def rate_line(block, depth):
    rows = block.astype(F32)
    return jnp.concatenate([rows[i : i + 1, :] for i in range(depth // 128)], axis=1)


def outer_kernel(seqs, heads, dps, share, place_ref, tok_ref, dout_ref, *refs):
    w_refs = refs[: seqs * dps]
    out_refs = refs[seqs * dps : seqs * dps + heads]
    tok_s, dout_s, acc = refs[seqs * dps + heads :]
    rows, features = tok_ref.shape
    depth = features // share
    for r in range(share):
        tok_s[r] = tok_ref[:, r * depth : (r + 1) * depth]
        dout_s[r] = dout_ref[:, r * depth : (r + 1) * depth]
    acc[...] = jnp.zeros_like(acc)
    for j in range(seqs):
        for d in range(dps):
            w = w_refs[j * dps + d]
            h, r = owner_of(place_ref, seqs, dps, share, j, d)
            line = rate_line(w[depth:, :], depth)
            logit = mm(jnp.broadcast_to(line, (EXTRA, depth)), tok_s[r], NT)
            back = mm(dout_s[r], w[0:depth, :], NN)
            acc[h] = acc[h] + jnp.concatenate([back, logit], axis=0)
    first_half = lax.broadcasted_iota(jnp.int32, (EXTRA, rows), 0) < EXTRA // 2
    for j in range(heads):
        total = acc[mate(place_ref[1], j, heads)]
        out_refs[j][0:rows, :] = total[0:rows].astype(BF16)
        logit = total[rows:]
        high = logit.astype(BF16).astype(F32)
        out_refs[j][rows:, :] = jnp.where(first_half, high, logit - high).astype(BF16)


def inner_projection_kernel(seqs, heads, dps, share, place_ref, tok_ref, *refs):
    w_refs = refs[: 2 * seqs * dps]
    out_refs = refs[2 * seqs * dps : 2 * seqs * dps + heads]
    tok_s, acc = refs[2 * seqs * dps + heads :]
    rows, features = tok_ref.shape
    depth = features // share
    half = depth // 2
    for r in range(share):
        tok_s[r] = tok_ref[:, r * depth : (r + 1) * depth]
    acc[...] = jnp.zeros_like(acc)
    for part in range(2):
        for j in range(seqs):
            for d in range(dps):
                w = w_refs[(part * seqs + j) * dps + d]
                h, r = owner_of(place_ref, seqs, dps, share, j, d)
                wide = jnp.concatenate([w[c * half : (c + 1) * half, :] for c in range(3)], axis=1)
                acc[h] = acc[h] + mm(tok_s[r][:, part * half : (part + 1) * half], wide, NN)
    for j in range(heads):
        out_refs[j][...] = acc[mate(place_ref[1], j, heads)].astype(BF16)


def inner_kernel(seqs, dps, place_ref, *refs):
    x_refs, y_refs = refs[:seqs], refs[seqs : 2 * seqs]
    w1_ref, w2_ref, res_ref = refs[2 * seqs : 2 * seqs + 3]
    dw_refs = refs[2 * seqs + 3 : 2 * seqs + 3 + dps]
    (
        qs, ks, vs, ds, es, sg, os, lg,
        w1c, w2c, w1b, w2b,
        x2s, g1s, pgs, gfs, xqs, zqs, dx2s, dg1s,
        dys, ns, rs, ss, cs, g2s, dg2s, dks, des, ws,
    ) = refs[2 * seqs + 3 + dps :]
    rows = x_refs[0].shape[0]
    hd = y_refs[0].shape[1]
    width = 4 * hd
    blocks = seqs * rows // MB
    per = rows // MB
    place = place_ref[0]

    for j in range(seqs):
        owner = mate(place, j, seqs)
        at = pl.ds(pl.multiple_of(owner * rows, rows), rows)
        qs[at, :] = x_refs[j][:, 0:hd]
        ks[at, :] = x_refs[j][:, hd : 2 * hd]
        vs[at, :] = x_refs[j][:, 2 * hd : 3 * hd]
        ds[at, :] = y_refs[j][0:rows, :]
        logit = y_refs[j][rows : rows + 8, :] + y_refs[j][rows + 8 : rows + 16, :]
        gate = jax.nn.sigmoid(logit)
        scaled = (BASE_RATE / hd) * gate
        for b in range(per):
            es[owner * per + b] = padded(scaled[:, b * MB : (b + 1) * MB])
            sg[owner * per + b] = padded((scaled * (1.0 - gate))[:, b * MB : (b + 1) * MB])

    w1c[...] = w1_ref[...]
    start = w2_ref[...]
    w2c[...] = (start - mean(start)).T

    at_row = lax.broadcasted_iota(jnp.int32, (MB, MB), 0)
    at_col = lax.broadcasted_iota(jnp.int32, (MB, MB), 1)
    causal = at_col <= at_row
    diagonal = at_col == at_row

    def to_column(line):
        return jnp.sum(jnp.where(diagonal, line, 0.0), axis=1, keepdims=True)

    def to_line(column):
        return jnp.sum(jnp.where(diagonal, column, 0.0), axis=0, keepdims=True)

    def at_block(i):
        if isinstance(i, int):
            return slice(i * MB, (i + 1) * MB)
        return pl.ds(pl.multiple_of(i * MB, MB), MB)

    def forward(i):
        at = at_block(i)
        q, k, v, d_o = qs[at, :], ks[at, :], vs[at, :], ds[at, :]
        line = es[i][0:1, 0:MB]
        e = to_column(line)
        mask = jnp.where(causal, line, 0.0)
        w1 = w1c[...].astype(BF16)
        w2 = w2c[...].astype(BF16)
        w1b[i] = w1
        w2b[i] = w2
        kb, qb = k.astype(BF16), q.astype(BF16)
        gap = v - k
        gap = gap - mean(gap)
        both = mm(jnp.concatenate([kb, qb], axis=0), w1, NN)
        x2, g1, gg1 = gelu_parts(both[:MB])
        x2b = x2.astype(BF16)
        c = mm(x2b, w2, NT)
        var = mean(c * c)
        cross = mean(gap * c)
        s = lax.rsqrt(var + EPSILON)
        n = c * s
        cc = var * s * s - s * cross
        r = n - gap
        g2 = s * (r - n * cc)
        g2b = g2.astype(BF16)
        p = mm(g2b, w2, NN)
        g1f = p * g1
        w1c[...] = w1c[...] - mm(k, e * g1f, TN)
        w2c[...] = w2c[...] - mm(e * g2, x2b, TN)
        g1b = g1f.astype(BF16)
        b1 = mm(qb, kb, NT)
        a1 = (b1 * mask).astype(BF16)
        zq = both[MB:] - mm(a1, g1b, NN)
        xq, gq = gelu_two(zq)
        xqb = xq.astype(BF16)
        b2 = mm(xqb, x2b, NT)
        a2 = (b2 * mask).astype(BF16)
        y = mm(xqb, w2, NT) - mm(a2, g2b, NN)
        sq = lax.rsqrt(mean(y * y) + EPSILON)
        nq = y * sq
        os[at, 3 * hd : 4 * hd] = (q + nq).astype(BF16)
        dy = sq * (d_o - mean(d_o) - nq * mean(d_o * nq))
        dyb = dy.astype(BF16)
        da2 = -mm(dyb, g2b, NT)
        db2 = (da2 * mask).astype(BF16)
        dg2s[i] = -mm(a2, dyb, TN)
        dxq = mm(dyb, w2, NN) + mm(db2, x2b, NN)
        dx2s[i] = mm(db2, xqb, TN)
        dzq = (dxq * gq).astype(BF16)
        da1 = -mm(dzq, g1b, NT)
        db1 = (da1 * mask).astype(BF16)
        dg1s[i] = -mm(a1, dzq, TN)
        dq = d_o + mm(dzq, w1, NT) + mm(db1, kb, NN)
        os[at, 0:hd] = dq.astype(BF16)
        dks[i] = mm(db1, qb, TN)
        de = jnp.sum(jnp.where(causal, da2 * b2 + da1 * b1, 0.0), axis=0, keepdims=True)
        des[i] = padded(jnp.broadcast_to(de, (8, MB)))
        x2s[i] = x2b
        g1s[i] = g1
        pgs[i] = p * gg1
        gfs[i] = g1f
        xqs[i] = xqb
        zqs[i] = dzq
        dys[i] = dyb
        ns[i] = n
        rs[i] = r
        ss[i] = jnp.broadcast_to(s, (MB, hd))
        cs[i] = jnp.broadcast_to(cc, (MB, hd))
        g2s[i] = g2

    def backward(i):
        at = at_block(i)
        q, k = qs[at, :], ks[at, :]
        e = to_column(es[i][0:1, 0:MB])
        w1, w2 = w1b[i], w2b[i]
        d1, d2 = w1c[...].astype(BF16), w2c[...].astype(BF16)
        x2b, g1, g1f, g2 = x2s[i], g1s[i], gfs[i], g2s[i]
        n, s, cc = ns[i], ss[i], cs[i]
        dh1 = -mm(k, d1, NN)
        dh2 = -mm(x2b, d2, NT)
        dg1 = dg1s[i] + e * dh1
        dp = (dg1 * g1).astype(BF16)
        dg2 = dg2s[i] + e * dh2 + mm(dp, w2, NT)
        dt = s * dg2
        mt = mean(dt * n)
        dr = dt - mean(dt) - n * mt
        dn = dr - cc * dt - rs[i] * mt
        du = s * (dn - mean(dn) - n * (mean(dn * n) + mean(dg2 * g2)))
        dub = du.astype(BF16)
        mixed = jnp.concatenate([(-e * g2).astype(BF16), dub], axis=1)
        dx2 = dx2s[i] + mm(mixed, jnp.concatenate([d2, w2], axis=0), NN)
        dz1 = (dg1 * pgs[i] + dx2 * g1).astype(BF16)
        mixed = jnp.concatenate([(-e * g1f).astype(BF16), dz1], axis=1)
        dk = dks[i] + dr + mm(mixed, jnp.concatenate([d1, w1], axis=1), NT)
        w1c[...] = w1c[...] + mm(
            jnp.concatenate([q, k], axis=0), jnp.concatenate([zqs[i], dz1], axis=0), TN
        )
        w2c[...] = w2c[...] + mm(
            jnp.concatenate([dys[i].astype(F32), du, g2], axis=0),
            jnp.concatenate([xqs[i], x2b, dp], axis=0),
            TN,
        )
        extra = jnp.sum(g1f * dh1, axis=1, keepdims=True) + jnp.sum(
            g2 * dh2, axis=1, keepdims=True
        )
        line = (des[i][0:1, 0:MB] + to_line(extra)) * sg[i][0:1, 0:MB]
        lg[i] = padded(jnp.broadcast_to(line, (8, MB)))
        os[at, hd : 2 * hd] = dk.astype(BF16)
        os[at, 2 * hd : 3 * hd] = (-dr).astype(BF16)

    def loop(step, order):
        if blocks <= UNROLL_LIMIT:
            for i in range(blocks):
                step(order(i))
        else:
            lax.fori_loop(0, blocks, lambda i, unused: (step(order(i)), unused)[1], 0)

    loop(forward, lambda i: i)
    w1c[...] = jnp.zeros_like(w1c)
    w2c[...] = jnp.zeros_like(w2c)
    loop(backward, lambda i: blocks - 1 - i)

    res_ref[0:rows, :] = os[pl.ds(pl.multiple_of(place * rows, rows), rows), :]
    res_ref[rows:, :] = jnp.zeros((EXTRA, width), BF16)
    first_row = lax.broadcasted_iota(jnp.int32, (EXTRA, rows), 0) == 0
    lines = jnp.concatenate([lg[place * per + b][0:1, 0:MB] for b in range(per)], axis=1)
    lines = jnp.where(first_row, jnp.broadcast_to(lines, (EXTRA, rows)), 0.0)
    res_ref[rows:, 0:rows] = lines.astype(BF16)

    part = dw_refs[0].shape[0]
    ws[:, 0:hd] = w1c[...].T
    ws[:, hd : 2 * hd] = w2c[...].T
    for d in range(dps):
        first = (place * dps + mate(place_ref[2], d, dps)) * part
        dw_refs[d][...] = ws[pl.ds(pl.multiple_of(first, part), part), :]


def output_kernel(seqs, heads, dps, share, place_ref, *refs):
    got_refs, refs = refs[:heads], refs[heads:]
    o_refs, w_refs = refs[: seqs * dps], refs[seqs * dps : 3 * seqs * dps]
    out_ref, dtok_ref, got, out_s, grad_s = refs[3 * seqs * dps :]
    hd = o_refs[0].shape[1]
    rows, features = out_ref.shape
    depth = features // share
    half = depth // 2
    for j in range(heads):
        got[mate(place_ref[1], j, heads)] = got_refs[j][...]
    out_s[...] = jnp.zeros_like(out_s)
    grad_s[...] = jnp.zeros_like(grad_s)
    for j in range(seqs):
        for d in range(dps):
            o = o_refs[j * dps + d]
            h, r = owner_of(place_ref, seqs, dps, share, j, d)
            out_s[r] = out_s[r] + mm(got[h, 0:rows, 3 * hd :], o[0:depth, :], NT)
            line = rate_line(o[depth:, :], depth)
            logit = got[h, rows:, 0:rows].astype(F32).T
            grad = [mm(logit, jnp.broadcast_to(line, (EXTRA, depth)), NN)]
            mine = got[h, 0:rows, 0 : 3 * hd]
            halves = []
            for part in range(2):
                w = w_refs[(part * seqs + j) * dps + d]
                wide = jnp.concatenate([w[c * half : (c + 1) * half, :] for c in range(3)], axis=1)
                halves.append(mm(mine, wide, NT))
            grad_s[r] = grad_s[r] + grad[0] + jnp.concatenate(halves, axis=1)
    for r in range(share):
        out_ref[:, r * depth : (r + 1) * depth] = out_s[r].astype(BF16)
        dtok_ref[:, r * depth : (r + 1) * depth] = grad_s[r].astype(BF16)


VMEM = pl.BlockSpec(memory_space=pltpu.VMEM)
SMEM = pl.BlockSpec(memory_space=pltpu.SMEM)
MIB = 1024 * 1024


def call(kernel, outs, operands, scratch=(), mib=16):
    return pl.pallas_call(
        kernel,
        out_shape=outs,
        in_specs=[SMEM] + [VMEM] * (len(operands) - 1),
        out_specs=jax.tree.map(lambda unused: VMEM, outs),
        scratch_shapes=list(scratch),
        compiler_params=pltpu.CompilerParams(vmem_limit_bytes=mib * MIB),
    )(*operands)


def body(tokens, w_qkv, w_lr, w_out, w1_init, w2_init, d_out):
    seqs, heads, dps = (lax.axis_size(a) for a in ("seq", "head", "dp"))
    share = seqs * dps // heads
    rows, features = tokens.shape[1:]
    depth, unused, hd = w_qkv.shape
    inner = w1_init.shape[2]
    blocks = seqs * rows // MB
    place = jnp.stack([lax.axis_index(a).astype(jnp.int32) for a in ("seq", "head", "dp")])
    sizes = (seqs, heads, dps, share)
    place, w_out, w_qkv = lax.optimization_barrier((place, w_out, w_qkv))

    pairs = []
    for seq in range(seqs):
        for head in range(heads):
            for dp in range(dps):
                k = seq * dps + dp
                target = head * share + k % share
                to = ((target // dps) * heads + k // share) * dps + target % dps
                pairs.append(((seq * heads + head) * dps + dp, to))

    def swapped(array):
        return lax.ppermute(array, ("seq", "head", "dp"), pairs)

    half = depth // 2
    lines = w_lr[:, 0].reshape(seqs * dps, depth // 128, 128)
    line = lax.dynamic_index_in_dim(
        lines, lax.axis_index("seq") * dps + lax.axis_index("dp"), 0, keepdims=False
    )
    line = jnp.pad(line, ((0, EXTRA - depth // 128), (0, 0)))
    by_kind = w_qkv.transpose(1, 0, 2)
    first, second, outer = lax.optimization_barrier(
        (
            by_kind[:, :half].reshape(3 * half, hd),
            by_kind[:, half:].reshape(3 * half, hd),
            jnp.concatenate([w_out, line], axis=0),
        )
    )
    first_w, second_w, outer_w = swapped(first), swapped(second), swapped(outer)
    outer_w, first_w, second_w = lax.optimization_barrier((outer_w, first_w, second_w))
    first_near = [first_w, hop(first_w, "dp", 1), hop(first_w, "dp", 2)]
    second_near = [second_w, hop(second_w, "dp", 1), hop(second_w, "dp", 2)]
    outer_w, first_near[1], second_near[2] = lax.optimization_barrier(
        (outer_w, first_near[1], second_near[2])
    )
    outer_near = peers_of(outer_w, "dp")
    outer_ws = over_seq(outer_near)
    def summed(arrays):
        return functools.reduce(lambda a, b: a + b, [a.astype(F32) for a in arrays])

    outer_part = call(
        functools.partial(outer_kernel, *sizes),
        (jax.ShapeDtypeStruct((rows + EXTRA, hd), BF16),) * heads,
        (place, tokens[0], d_out[0], *outer_ws),
        [pltpu.VMEM((share, rows, features // share), BF16)] * 2
        + [pltpu.VMEM((heads, rows + EXTRA, hd), F32)],
    )
    outer_all = peers_of(summed(sent_to(outer_part, "head")), "seq")
    if dps == 4:
        first_near.append(hop(first_near[1], "dp", 2))
        second_near.append(hop(second_near[2], "dp", 1))
    else:
        first_near += [hop(first_w, "dp", j) for j in range(3, dps)]
        second_near += [hop(second_w, "dp", j) for j in range(3, dps)]
    inner_ws = over_seq(first_near) + over_seq(second_near)
    later_place, unused = lax.optimization_barrier((place, outer_part[0]))
    inner_part = call(
        functools.partial(inner_projection_kernel, *sizes),
        (jax.ShapeDtypeStruct((rows, 3 * hd), BF16),) * heads,
        (later_place, tokens[0], *inner_ws),
        [
            pltpu.VMEM((share, rows, features // share), BF16),
            pltpu.VMEM((heads, rows, 3 * hd), F32),
        ],
    )
    inner_all = peers_of(summed(sent_to(inner_part, "head")), "seq")

    long = seqs * rows
    scratch = (
        [pltpu.VMEM((long, hd), F32)] * 4
        + [pltpu.VMEM((blocks, 8, 2 * MB), F32)] * 2
        + [pltpu.VMEM((long, 4 * hd), BF16), pltpu.VMEM((blocks, 8, 2 * MB), F32)]
        + [pltpu.VMEM((hd, inner), F32)] * 2
        + [pltpu.VMEM((blocks, hd, inner), BF16)] * 2
        + [pltpu.VMEM((blocks, MB, inner), t) for t in (BF16, F32, F32, F32, BF16, BF16, F32, F32)]
        + [pltpu.VMEM((blocks, MB, hd), t) for t in (BF16, F32, F32, F32, F32, F32, F32, F32)]
        + [pltpu.VMEM((blocks, 8, 2 * MB), F32), pltpu.VMEM((inner, 2 * hd), F32)]
    )
    part = inner // (seqs * dps)
    result, *d_inner = call(
        functools.partial(inner_kernel, seqs, dps),
        (jax.ShapeDtypeStruct((rows + EXTRA, 4 * hd), BF16),)
        + (jax.ShapeDtypeStruct((part, 2 * hd), F32),) * dps,
        (place, *inner_all, *outer_all, w1_init[0], w2_init[0]),
        scratch,
        14 + 2 * blocks,
    )
    got = peers_of(result, "head")
    unused, *d_inner = lax.optimization_barrier((got[1], *d_inner))
    shares = summed(sent_to(d_inner, "dp"))
    out, d_tokens = call(
        functools.partial(output_kernel, *sizes),
        (jax.ShapeDtypeStruct((rows, features), BF16),) * 2,
        (place, *got, *outer_ws, *inner_ws),
        [
            pltpu.VMEM((heads, rows + EXTRA, 4 * hd), BF16),
            pltpu.VMEM((share, rows, features // share), F32),
            pltpu.VMEM((share, rows, features // share), F32),
        ],
    )
    return (out[None], d_tokens[None], shares[:, :hd].transpose(1, 0)[None], shares[:, hd:][None])


def solution(mesh):
    placed = (
        P("dp", "seq", "head"),
        P(("seq", "dp"), None, "head"),
        P(None, "head"),
        P(("seq", "dp"), "head"),
        P("head", None, None),
        P("head", None, None),
        P("dp", "seq", "head"),
    )
    return jax.shard_map(
        body,
        mesh=mesh,
        in_specs=placed,
        out_specs=(
            P("dp", "seq", "head"),
            P("dp", "seq", "head"),
            P("head", None, ("seq", "dp")),
            P("head", ("seq", "dp"), None),
        ),
        check_vma=False,
    )
```

```python
import functools

import jax
import jax.numpy as jnp
from jax import lax
from jax.experimental import pallas as pl
from jax.experimental.pallas import tpu as pltpu
from jax.sharding import PartitionSpec as P

MB = 64
EPSILON = 1e-06
BASE_RATE = 0.1
GELU_SCALE = 0.7978845608028654
GELU_CUBIC = 0.044715
NN = ((1,), (0,))
NT = ((1,), (1,))
TN = ((0,), (0,))
EXTRA = 16
UNROLL_LIMIT = 8
F32 = jnp.float32
BF16 = jnp.bfloat16


def mm(left, right, dims):
    return lax.dot_general(
        left.astype(BF16), right.astype(BF16), (dims, ((), ())), preferred_element_type=F32
    )


def padded(lines):
    return jnp.concatenate([lines, jnp.zeros_like(lines)], axis=1)


def mean(rows):
    return jnp.mean(rows, axis=-1, keepdims=True)


def gelu_parts(v):
    square = v * v
    bend = jnp.tanh(v * (GELU_SCALE + (GELU_SCALE * GELU_CUBIC) * square))
    half = 0.5 + 0.5 * bend
    slope = GELU_SCALE + (3.0 * GELU_SCALE * GELU_CUBIC) * square
    bell = 0.5 - 0.5 * bend * bend
    lean = bell * slope
    second = 2.0 * lean * (1.0 - v * bend * slope) + (6.0 * GELU_SCALE * GELU_CUBIC) * square * bell
    return v * half, half + v * lean, second


def gelu_two(v):
    square = v * v
    bend = jnp.tanh(v * (GELU_SCALE + (GELU_SCALE * GELU_CUBIC) * square))
    half = 0.5 + 0.5 * bend
    slope = GELU_SCALE + (3.0 * GELU_SCALE * GELU_CUBIC) * square
    return v * half, half + v * ((0.5 - 0.5 * bend * bend) * slope)


def mate(index, step, count):
    if count & (count - 1) == 0:
        return index ^ step
    return (index + step) % count


def hop(array, axis, step):
    count = lax.axis_size(axis)
    return lax.ppermute(array, axis, [(mate(i, step, count), i) for i in range(count)])


def peers_of(array, axis):
    return [array] + [hop(array, axis, j) for j in range(1, lax.axis_size(axis))]


def sent_to(arrays, axis):
    count = lax.axis_size(axis)
    back = [arrays[0]]
    for j in range(1, count):
        back.append(lax.ppermute(arrays[j], axis, [(i, mate(i, j, count)) for i in range(count)]))
    return back


def over_seq(near):
    return sum([list(pieces) for pieces in zip(*[peers_of(piece, "seq") for piece in near])], [])


def owner_of(place_ref, seqs, dps, share, j, d):
    seq, dp = place_ref[0], place_ref[2]
    k = mate(seq, j, seqs) * dps + mate(dp, d, dps)
    return k // share, k % share


def rate_line(block, depth):
    rows = block.astype(F32)
    return jnp.concatenate([rows[i : i + 1, :] for i in range(depth // 128)], axis=1)


def outer_kernel(seqs, heads, dps, share, place_ref, tok_ref, dout_ref, *refs):
    w_refs = refs[: seqs * dps]
    out_refs = refs[seqs * dps : seqs * dps + heads]
    tok_s, dout_s, acc = refs[seqs * dps + heads :]
    rows, features = tok_ref.shape
    depth = features // share
    for r in range(share):
        tok_s[r] = tok_ref[:, r * depth : (r + 1) * depth]
        dout_s[r] = dout_ref[:, r * depth : (r + 1) * depth]
    acc[...] = jnp.zeros_like(acc)
    for j in range(seqs):
        for d in range(dps):
            w = w_refs[j * dps + d]
            h, r = owner_of(place_ref, seqs, dps, share, j, d)
            line = rate_line(w[depth:, :], depth)
            logit = mm(jnp.broadcast_to(line, (EXTRA, depth)), tok_s[r], NT)
            back = mm(dout_s[r], w[0:depth, :], NN)
            acc[h] = acc[h] + jnp.concatenate([back, logit], axis=0)
    first_half = lax.broadcasted_iota(jnp.int32, (EXTRA, rows), 0) < EXTRA // 2
    for j in range(heads):
        total = acc[mate(place_ref[1], j, heads)]
        out_refs[j][0:rows, :] = total[0:rows].astype(BF16)
        logit = total[rows:]
        high = logit.astype(BF16).astype(F32)
        out_refs[j][rows:, :] = jnp.where(first_half, high, logit - high).astype(BF16)


def inner_projection_kernel(seqs, heads, dps, share, place_ref, tok_ref, *refs):
    w_refs = refs[: 2 * seqs * dps]
    out_refs = refs[2 * seqs * dps : 2 * seqs * dps + heads]
    tok_s, acc = refs[2 * seqs * dps + heads :]
    rows, features = tok_ref.shape
    depth = features // share
    half = depth // 2
    for r in range(share):
        tok_s[r] = tok_ref[:, r * depth : (r + 1) * depth]
    acc[...] = jnp.zeros_like(acc)
    for part in range(2):
        for j in range(seqs):
            for d in range(dps):
                w = w_refs[(part * seqs + j) * dps + d]
                h, r = owner_of(place_ref, seqs, dps, share, j, d)
                wide = jnp.concatenate([w[c * half : (c + 1) * half, :] for c in range(3)], axis=1)
                acc[h] = acc[h] + mm(tok_s[r][:, part * half : (part + 1) * half], wide, NN)
    for j in range(heads):
        out_refs[j][...] = acc[mate(place_ref[1], j, heads)].astype(BF16)


def inner_kernel(seqs, dps, place_ref, *refs):
    x_refs, y_refs = refs[:seqs], refs[seqs : 2 * seqs]
    w1_ref, w2_ref, res_ref = refs[2 * seqs : 2 * seqs + 3]
    dw_refs = refs[2 * seqs + 3 : 2 * seqs + 3 + dps]
    (
        qs, ks, vs, ds, es, sg, os, lg,
        w1c, w2c, w1b, w2b,
        x2s, g1s, pgs, gfs, xqs, zqs, dx2s, dg1s,
        dys, ns, rs, ss, cs, g2s, dg2s, dks, des, ws,
    ) = refs[2 * seqs + 3 + dps :]
    rows = x_refs[0].shape[0]
    hd = y_refs[0].shape[1]
    width = 4 * hd
    blocks = seqs * rows // MB
    per = rows // MB
    place = place_ref[0]

    for j in range(seqs):
        owner = mate(place, j, seqs)
        at = pl.ds(pl.multiple_of(owner * rows, rows), rows)
        qs[at, :] = x_refs[j][:, 0:hd]
        ks[at, :] = x_refs[j][:, hd : 2 * hd]
        vs[at, :] = x_refs[j][:, 2 * hd : 3 * hd]
        ds[at, :] = y_refs[j][0:rows, :]
        logit = y_refs[j][rows : rows + 8, :] + y_refs[j][rows + 8 : rows + 16, :]
        gate = jax.nn.sigmoid(logit)
        scaled = (BASE_RATE / hd) * gate
        for b in range(per):
            es[owner * per + b] = padded(scaled[:, b * MB : (b + 1) * MB])
            sg[owner * per + b] = padded((scaled * (1.0 - gate))[:, b * MB : (b + 1) * MB])

    w1c[...] = w1_ref[...]
    start = w2_ref[...]
    w2c[...] = (start - mean(start)).T

    at_row = lax.broadcasted_iota(jnp.int32, (MB, MB), 0)
    at_col = lax.broadcasted_iota(jnp.int32, (MB, MB), 1)
    causal = at_col <= at_row
    diagonal = at_col == at_row

    def to_column(line):
        return jnp.sum(jnp.where(diagonal, line, 0.0), axis=1, keepdims=True)

    def to_line(column):
        return jnp.sum(jnp.where(diagonal, column, 0.0), axis=0, keepdims=True)

    def at_block(i):
        if isinstance(i, int):
            return slice(i * MB, (i + 1) * MB)
        return pl.ds(pl.multiple_of(i * MB, MB), MB)

    def forward(i):
        at = at_block(i)
        q, k, v, d_o = qs[at, :], ks[at, :], vs[at, :], ds[at, :]
        line = es[i][0:1, 0:MB]
        e = to_column(line)
        mask = jnp.where(causal, line, 0.0)
        w1 = w1c[...].astype(BF16)
        w2 = w2c[...].astype(BF16)
        w1b[i] = w1
        w2b[i] = w2
        kb, qb = k.astype(BF16), q.astype(BF16)
        gap = v - k
        gap = gap - mean(gap)
        both = mm(jnp.concatenate([kb, qb], axis=0), w1, NN)
        x2, g1, gg1 = gelu_parts(both[:MB])
        x2b = x2.astype(BF16)
        c = mm(x2b, w2, NT)
        var = mean(c * c)
        cross = mean(gap * c)
        s = lax.rsqrt(var + EPSILON)
        n = c * s
        cc = var * s * s - s * cross
        r = n - gap
        g2 = s * (r - n * cc)
        g2b = g2.astype(BF16)
        p = mm(g2b, w2, NN)
        g1f = p * g1
        w1c[...] = w1c[...] - mm(k, e * g1f, TN)
        w2c[...] = w2c[...] - mm(e * g2, x2b, TN)
        g1b = g1f.astype(BF16)
        b1 = mm(qb, kb, NT)
        a1 = (b1 * mask).astype(BF16)
        zq = both[MB:] - mm(a1, g1b, NN)
        xq, gq = gelu_two(zq)
        xqb = xq.astype(BF16)
        b2 = mm(xqb, x2b, NT)
        a2 = (b2 * mask).astype(BF16)
        y = mm(xqb, w2, NT) - mm(a2, g2b, NN)
        sq = lax.rsqrt(mean(y * y) + EPSILON)
        nq = y * sq
        os[at, 3 * hd : 4 * hd] = (q + nq).astype(BF16)
        dy = sq * (d_o - mean(d_o) - nq * mean(d_o * nq))
        dyb = dy.astype(BF16)
        da2 = -mm(dyb, g2b, NT)
        db2 = (da2 * mask).astype(BF16)
        dg2s[i] = -mm(a2, dyb, TN)
        dxq = mm(dyb, w2, NN) + mm(db2, x2b, NN)
        dx2s[i] = mm(db2, xqb, TN)
        dzq = (dxq * gq).astype(BF16)
        da1 = -mm(dzq, g1b, NT)
        db1 = (da1 * mask).astype(BF16)
        dg1s[i] = -mm(a1, dzq, TN)
        dq = d_o + mm(dzq, w1, NT) + mm(db1, kb, NN)
        os[at, 0:hd] = dq.astype(BF16)
        dks[i] = mm(db1, qb, TN)
        de = jnp.sum(jnp.where(causal, da2 * b2 + da1 * b1, 0.0), axis=0, keepdims=True)
        des[i] = padded(jnp.broadcast_to(de, (8, MB)))
        x2s[i] = x2b
        g1s[i] = g1
        pgs[i] = p * gg1
        gfs[i] = g1f
        xqs[i] = xqb
        zqs[i] = dzq
        dys[i] = dyb
        ns[i] = n
        rs[i] = r
        ss[i] = jnp.broadcast_to(s, (MB, hd))
        cs[i] = jnp.broadcast_to(cc, (MB, hd))
        g2s[i] = g2

    def backward(i):
        at = at_block(i)
        q, k = qs[at, :], ks[at, :]
        e = to_column(es[i][0:1, 0:MB])
        w1, w2 = w1b[i], w2b[i]
        d1, d2 = w1c[...].astype(BF16), w2c[...].astype(BF16)
        x2b, g1, g1f, g2 = x2s[i], g1s[i], gfs[i], g2s[i]
        n, s, cc = ns[i], ss[i], cs[i]
        dh1 = -mm(k, d1, NN)
        dh2 = -mm(x2b, d2, NT)
        dg1 = dg1s[i] + e * dh1
        dp = (dg1 * g1).astype(BF16)
        dg2 = dg2s[i] + e * dh2 + mm(dp, w2, NT)
        dt = s * dg2
        mt = mean(dt * n)
        dr = dt - mean(dt) - n * mt
        dn = dr - cc * dt - rs[i] * mt
        du = s * (dn - mean(dn) - n * (mean(dn * n) + mean(dg2 * g2)))
        dub = du.astype(BF16)
        mixed = jnp.concatenate([(-e * g2).astype(BF16), dub], axis=1)
        dx2 = dx2s[i] + mm(mixed, jnp.concatenate([d2, w2], axis=0), NN)
        dz1 = (dg1 * pgs[i] + dx2 * g1).astype(BF16)
        mixed = jnp.concatenate([(-e * g1f).astype(BF16), dz1], axis=1)
        dk = dks[i] + dr + mm(mixed, jnp.concatenate([d1, w1], axis=1), NT)
        w1c[...] = w1c[...] + mm(
            jnp.concatenate([q, k], axis=0), jnp.concatenate([zqs[i], dz1], axis=0), TN
        )
        w2c[...] = w2c[...] + mm(
            jnp.concatenate([dys[i].astype(F32), du, g2], axis=0),
            jnp.concatenate([xqs[i], x2b, dp], axis=0),
            TN,
        )
        extra = jnp.sum(g1f * dh1, axis=1, keepdims=True) + jnp.sum(
            g2 * dh2, axis=1, keepdims=True
        )
        line = (des[i][0:1, 0:MB] + to_line(extra)) * sg[i][0:1, 0:MB]
        lg[i] = padded(jnp.broadcast_to(line, (8, MB)))
        os[at, hd : 2 * hd] = dk.astype(BF16)
        os[at, 2 * hd : 3 * hd] = (-dr).astype(BF16)

    def loop(step, order):
        if blocks <= UNROLL_LIMIT:
            for i in range(blocks):
                step(order(i))
        else:
            lax.fori_loop(0, blocks, lambda i, unused: (step(order(i)), unused)[1], 0)

    loop(forward, lambda i: i)
    w1c[...] = jnp.zeros_like(w1c)
    w2c[...] = jnp.zeros_like(w2c)
    loop(backward, lambda i: blocks - 1 - i)

    res_ref[0:rows, :] = os[pl.ds(pl.multiple_of(place * rows, rows), rows), :]
    res_ref[rows:, :] = jnp.zeros((EXTRA, width), BF16)
    first_row = lax.broadcasted_iota(jnp.int32, (EXTRA, rows), 0) == 0
    lines = jnp.concatenate([lg[place * per + b][0:1, 0:MB] for b in range(per)], axis=1)
    lines = jnp.where(first_row, jnp.broadcast_to(lines, (EXTRA, rows)), 0.0)
    res_ref[rows:, 0:rows] = lines.astype(BF16)

    part = dw_refs[0].shape[0]
    ws[:, 0:hd] = w1c[...].T
    ws[:, hd : 2 * hd] = w2c[...].T
    for d in range(dps):
        first = (place * dps + mate(place_ref[2], d, dps)) * part
        dw_refs[d][...] = ws[pl.ds(pl.multiple_of(first, part), part), :]


def output_kernel(seqs, heads, dps, share, place_ref, *refs):
    got_refs, refs = refs[:heads], refs[heads:]
    o_refs, w_refs = refs[: seqs * dps], refs[seqs * dps : 3 * seqs * dps]
    out_ref, dtok_ref, got, out_s, grad_s = refs[3 * seqs * dps :]
    hd = o_refs[0].shape[1]
    rows, features = out_ref.shape
    depth = features // share
    half = depth // 2
    for j in range(heads):
        got[mate(place_ref[1], j, heads)] = got_refs[j][...]
    out_s[...] = jnp.zeros_like(out_s)
    grad_s[...] = jnp.zeros_like(grad_s)
    for j in range(seqs):
        for d in range(dps):
            o = o_refs[j * dps + d]
            h, r = owner_of(place_ref, seqs, dps, share, j, d)
            out_s[r] = out_s[r] + mm(got[h, 0:rows, 3 * hd :], o[0:depth, :], NT)
            line = rate_line(o[depth:, :], depth)
            logit = got[h, rows:, 0:rows].astype(F32).T
            grad = [mm(logit, jnp.broadcast_to(line, (EXTRA, depth)), NN)]
            mine = got[h, 0:rows, 0 : 3 * hd]
            halves = []
            for part in range(2):
                w = w_refs[(part * seqs + j) * dps + d]
                wide = jnp.concatenate([w[c * half : (c + 1) * half, :] for c in range(3)], axis=1)
                halves.append(mm(mine, wide, NT))
            grad_s[r] = grad_s[r] + grad[0] + jnp.concatenate(halves, axis=1)
    for r in range(share):
        out_ref[:, r * depth : (r + 1) * depth] = out_s[r].astype(BF16)
        dtok_ref[:, r * depth : (r + 1) * depth] = grad_s[r].astype(BF16)


VMEM = pl.BlockSpec(memory_space=pltpu.VMEM)
SMEM = pl.BlockSpec(memory_space=pltpu.SMEM)
MIB = 1024 * 1024


def call(kernel, outs, operands, scratch=(), mib=16):
    return pl.pallas_call(
        kernel,
        out_shape=outs,
        in_specs=[SMEM] + [VMEM] * (len(operands) - 1),
        out_specs=jax.tree.map(lambda unused: VMEM, outs),
        scratch_shapes=list(scratch),
        compiler_params=pltpu.CompilerParams(vmem_limit_bytes=mib * MIB),
    )(*operands)


def body(tokens, w_qkv, w_lr, w_out, w1_init, w2_init, d_out):
    seqs, heads, dps = (lax.axis_size(a) for a in ("seq", "head", "dp"))
    share = seqs * dps // heads
    rows, features = tokens.shape[1:]
    depth, unused, hd = w_qkv.shape
    inner = w1_init.shape[2]
    blocks = seqs * rows // MB
    place = jnp.stack([lax.axis_index(a).astype(jnp.int32) for a in ("seq", "head", "dp")])
    sizes = (seqs, heads, dps, share)
    place, w_out, w_qkv = lax.optimization_barrier((place, w_out, w_qkv))

    pairs = []
    for seq in range(seqs):
        for head in range(heads):
            for dp in range(dps):
                k = seq * dps + dp
                target = head * share + k % share
                to = ((target // dps) * heads + k // share) * dps + target % dps
                pairs.append(((seq * heads + head) * dps + dp, to))

    def swapped(array):
        return lax.ppermute(array, ("seq", "head", "dp"), pairs)

    half = depth // 2
    lines = w_lr[:, 0].reshape(seqs * dps, depth // 128, 128)
    line = lax.dynamic_index_in_dim(
        lines, lax.axis_index("seq") * dps + lax.axis_index("dp"), 0, keepdims=False
    )
    line = jnp.pad(line, ((0, EXTRA - depth // 128), (0, 0)))
    by_kind = w_qkv.transpose(1, 0, 2)
    first, second, outer = lax.optimization_barrier(
        (
            by_kind[:, :half].reshape(3 * half, hd),
            by_kind[:, half:].reshape(3 * half, hd),
            jnp.concatenate([w_out, line], axis=0),
        )
    )
    outer_w, first_w, second_w = swapped(outer), swapped(first), swapped(second)
    outer_near = peers_of(outer_w, "dp")
    first_near = [first_w, hop(first_w, "dp", 1), hop(first_w, "dp", 2)]
    second_near = [second_w, hop(second_w, "dp", 1), hop(second_w, "dp", 2)]
    outer_ws = over_seq(outer_near)
    def summed(arrays):
        return functools.reduce(lambda a, b: a + b, [a.astype(F32) for a in arrays])

    outer_part = call(
        functools.partial(outer_kernel, *sizes),
        (jax.ShapeDtypeStruct((rows + EXTRA, hd), BF16),) * heads,
        (place, tokens[0], d_out[0], *outer_ws),
        [pltpu.VMEM((share, rows, features // share), BF16)] * 2
        + [pltpu.VMEM((heads, rows + EXTRA, hd), F32)],
    )
    outer_all = peers_of(summed(sent_to(outer_part, "head")), "seq")
    if dps == 4:
        first_near.append(hop(first_near[1], "dp", 2))
        second_near.append(hop(second_near[2], "dp", 1))
    else:
        first_near += [hop(first_w, "dp", j) for j in range(3, dps)]
        second_near += [hop(second_w, "dp", j) for j in range(3, dps)]
    inner_ws = over_seq(first_near) + over_seq(second_near)
    later_place, unused = lax.optimization_barrier((place, outer_all[-1]))
    inner_part = call(
        functools.partial(inner_projection_kernel, *sizes),
        (jax.ShapeDtypeStruct((rows, 3 * hd), BF16),) * heads,
        (later_place, tokens[0], *inner_ws),
        [
            pltpu.VMEM((share, rows, features // share), BF16),
            pltpu.VMEM((heads, rows, 3 * hd), F32),
        ],
    )
    inner_all = peers_of(summed(sent_to(inner_part, "head")), "seq")

    long = seqs * rows
    scratch = (
        [pltpu.VMEM((long, hd), F32)] * 4
        + [pltpu.VMEM((blocks, 8, 2 * MB), F32)] * 2
        + [pltpu.VMEM((long, 4 * hd), BF16), pltpu.VMEM((blocks, 8, 2 * MB), F32)]
        + [pltpu.VMEM((hd, inner), F32)] * 2
        + [pltpu.VMEM((blocks, hd, inner), BF16)] * 2
        + [pltpu.VMEM((blocks, MB, inner), t) for t in (BF16, F32, F32, F32, BF16, BF16, F32, F32)]
        + [pltpu.VMEM((blocks, MB, hd), t) for t in (BF16, F32, F32, F32, F32, F32, F32, F32)]
        + [pltpu.VMEM((blocks, 8, 2 * MB), F32), pltpu.VMEM((inner, 2 * hd), F32)]
    )
    part = inner // (seqs * dps)
    result, *d_inner = call(
        functools.partial(inner_kernel, seqs, dps),
        (jax.ShapeDtypeStruct((rows + EXTRA, 4 * hd), BF16),)
        + (jax.ShapeDtypeStruct((part, 2 * hd), F32),) * dps,
        (place, *inner_all, *outer_all, w1_init[0], w2_init[0]),
        scratch,
        14 + 2 * blocks,
    )
    got = peers_of(result, "head")
    unused, *d_inner = lax.optimization_barrier((got[1], *d_inner))
    shares = summed(sent_to(d_inner, "dp"))
    out, d_tokens = call(
        functools.partial(output_kernel, *sizes),
        (jax.ShapeDtypeStruct((rows, features), BF16),) * 2,
        (place, *got, *outer_ws, *inner_ws),
        [
            pltpu.VMEM((heads, rows + EXTRA, 4 * hd), BF16),
            pltpu.VMEM((share, rows, features // share), F32),
            pltpu.VMEM((share, rows, features // share), F32),
        ],
    )
    return (out[None], d_tokens[None], shares[:, :hd].transpose(1, 0)[None], shares[:, hd:][None])


def solution(mesh):
    placed = (
        P("dp", "seq", "head"),
        P(("seq", "dp"), None, "head"),
        P(None, "head"),
        P(("seq", "dp"), "head"),
        P("head", None, None),
        P("head", None, None),
        P("dp", "seq", "head"),
    )
    return jax.shard_map(
        body,
        mesh=mesh,
        in_specs=placed,
        out_specs=(
            P("dp", "seq", "head"),
            P("dp", "seq", "head"),
            P("head", None, ("seq", "dp")),
            P("head", ("seq", "dp"), None),
        ),
        check_vma=False,
    )
```

```python
import functools

import jax
import jax.numpy as jnp
from jax import lax
from jax.experimental import pallas as pl
from jax.experimental.pallas import tpu as pltpu
from jax.sharding import PartitionSpec as P

MB = 64
EPSILON = 1e-06
BASE_RATE = 0.1
GELU_SCALE = 0.7978845608028654
GELU_CUBIC = 0.044715
NN = ((1,), (0,))
NT = ((1,), (1,))
TN = ((0,), (0,))
EXTRA = 16
UNROLL_LIMIT = 8
F32 = jnp.float32
BF16 = jnp.bfloat16


def mm(left, right, dims):
    return lax.dot_general(
        left.astype(BF16), right.astype(BF16), (dims, ((), ())), preferred_element_type=F32
    )


def padded(lines):
    return jnp.concatenate([lines, jnp.zeros_like(lines)], axis=1)


def mean(rows):
    return jnp.mean(rows, axis=-1, keepdims=True)


def gelu_parts(v):
    square = v * v
    bend = jnp.tanh(v * (GELU_SCALE + (GELU_SCALE * GELU_CUBIC) * square))
    half = 0.5 + 0.5 * bend
    slope = GELU_SCALE + (3.0 * GELU_SCALE * GELU_CUBIC) * square
    bell = 0.5 - 0.5 * bend * bend
    lean = bell * slope
    second = 2.0 * lean * (1.0 - v * bend * slope) + (6.0 * GELU_SCALE * GELU_CUBIC) * square * bell
    return v * half, half + v * lean, second


def gelu_two(v):
    square = v * v
    bend = jnp.tanh(v * (GELU_SCALE + (GELU_SCALE * GELU_CUBIC) * square))
    half = 0.5 + 0.5 * bend
    slope = GELU_SCALE + (3.0 * GELU_SCALE * GELU_CUBIC) * square
    return v * half, half + v * ((0.5 - 0.5 * bend * bend) * slope)


def mate(index, step, count):
    if count & (count - 1) == 0:
        return index ^ step
    return (index + step) % count


def hop(array, axis, step):
    count = lax.axis_size(axis)
    return lax.ppermute(array, axis, [(mate(i, step, count), i) for i in range(count)])


def peers_of(array, axis):
    return [array] + [hop(array, axis, j) for j in range(1, lax.axis_size(axis))]


def sent_to(arrays, axis):
    count = lax.axis_size(axis)
    back = [arrays[0]]
    for j in range(1, count):
        back.append(lax.ppermute(arrays[j], axis, [(i, mate(i, j, count)) for i in range(count)]))
    return back


def over_seq(near):
    return sum([list(pieces) for pieces in zip(*[peers_of(piece, "seq") for piece in near])], [])


def owner_of(place_ref, seqs, dps, share, j, d):
    seq, dp = place_ref[0], place_ref[2]
    k = mate(seq, j, seqs) * dps + mate(dp, d, dps)
    return k // share, k % share


def rate_line(block, depth):
    rows = block.astype(F32)
    return jnp.concatenate([rows[i : i + 1, :] for i in range(depth // 128)], axis=1)


def outer_kernel(seqs, heads, dps, share, place_ref, tok_ref, dout_ref, *refs):
    w_refs = refs[: seqs * dps]
    out_refs = refs[seqs * dps : seqs * dps + heads]
    tok_s, dout_s, acc = refs[seqs * dps + heads :]
    rows, features = tok_ref.shape
    depth = features // share
    for r in range(share):
        tok_s[r] = tok_ref[:, r * depth : (r + 1) * depth]
        dout_s[r] = dout_ref[:, r * depth : (r + 1) * depth]
    acc[...] = jnp.zeros_like(acc)
    for j in range(seqs):
        for d in range(dps):
            w = w_refs[j * dps + d]
            h, r = owner_of(place_ref, seqs, dps, share, j, d)
            line = rate_line(w[depth:, :], depth)
            logit = mm(jnp.broadcast_to(line, (EXTRA, depth)), tok_s[r], NT)
            back = mm(dout_s[r], w[0:depth, :], NN)
            acc[h] = acc[h] + jnp.concatenate([back, logit], axis=0)
    first_half = lax.broadcasted_iota(jnp.int32, (EXTRA, rows), 0) < EXTRA // 2
    for j in range(heads):
        total = acc[mate(place_ref[1], j, heads)]
        out_refs[j][0:rows, :] = total[0:rows].astype(BF16)
        logit = total[rows:]
        high = logit.astype(BF16).astype(F32)
        out_refs[j][rows:, :] = jnp.where(first_half, high, logit - high).astype(BF16)


def inner_projection_kernel(seqs, heads, dps, share, place_ref, tok_ref, *refs):
    w_refs = refs[: 2 * seqs * dps]
    out_refs = refs[2 * seqs * dps : 2 * seqs * dps + heads]
    tok_s, acc = refs[2 * seqs * dps + heads :]
    rows, features = tok_ref.shape
    depth = features // share
    half = depth // 2
    for r in range(share):
        tok_s[r] = tok_ref[:, r * depth : (r + 1) * depth]
    acc[...] = jnp.zeros_like(acc)
    for part in range(2):
        for j in range(seqs):
            for d in range(dps):
                w = w_refs[(part * seqs + j) * dps + d]
                h, r = owner_of(place_ref, seqs, dps, share, j, d)
                wide = jnp.concatenate([w[c * half : (c + 1) * half, :] for c in range(3)], axis=1)
                acc[h] = acc[h] + mm(tok_s[r][:, part * half : (part + 1) * half], wide, NN)
    for j in range(heads):
        out_refs[j][...] = acc[mate(place_ref[1], j, heads)].astype(BF16)


def inner_kernel(seqs, dps, place_ref, *refs):
    x_refs, y_refs = refs[:seqs], refs[seqs : 2 * seqs]
    w1_ref, w2_ref, res_ref = refs[2 * seqs : 2 * seqs + 3]
    dw_refs = refs[2 * seqs + 3 : 2 * seqs + 3 + dps]
    (
        qs, ks, vs, ds, es, sg, os, lg,
        w1c, w2c, w1b, w2b,
        x2s, g1s, pgs, gfs, xqs, zqs, dx2s, dg1s,
        dys, ns, rs, ss, cs, g2s, dg2s, dks, des, ws,
    ) = refs[2 * seqs + 3 + dps :]
    rows = x_refs[0].shape[0]
    hd = y_refs[0].shape[1]
    width = 4 * hd
    blocks = seqs * rows // MB
    per = rows // MB
    place = place_ref[0]

    for j in range(seqs):
        owner = mate(place, j, seqs)
        at = pl.ds(pl.multiple_of(owner * rows, rows), rows)
        qs[at, :] = x_refs[j][:, 0:hd]
        ks[at, :] = x_refs[j][:, hd : 2 * hd]
        vs[at, :] = x_refs[j][:, 2 * hd : 3 * hd]
        ds[at, :] = y_refs[j][0:rows, :]
        logit = y_refs[j][rows : rows + 8, :] + y_refs[j][rows + 8 : rows + 16, :]
        gate = jax.nn.sigmoid(logit)
        scaled = (BASE_RATE / hd) * gate
        for b in range(per):
            es[owner * per + b] = padded(scaled[:, b * MB : (b + 1) * MB])
            sg[owner * per + b] = padded((scaled * (1.0 - gate))[:, b * MB : (b + 1) * MB])

    w1c[...] = w1_ref[...]
    start = w2_ref[...]
    w2c[...] = (start - mean(start)).T

    at_row = lax.broadcasted_iota(jnp.int32, (MB, MB), 0)
    at_col = lax.broadcasted_iota(jnp.int32, (MB, MB), 1)
    causal = at_col <= at_row
    diagonal = at_col == at_row

    def to_column(line):
        return jnp.sum(jnp.where(diagonal, line, 0.0), axis=1, keepdims=True)

    def to_line(column):
        return jnp.sum(jnp.where(diagonal, column, 0.0), axis=0, keepdims=True)

    def at_block(i):
        if isinstance(i, int):
            return slice(i * MB, (i + 1) * MB)
        return pl.ds(pl.multiple_of(i * MB, MB), MB)

    def forward(i):
        at = at_block(i)
        q, k, v, d_o = qs[at, :], ks[at, :], vs[at, :], ds[at, :]
        line = es[i][0:1, 0:MB]
        e = to_column(line)
        mask = jnp.where(causal, line, 0.0)
        w1 = w1c[...].astype(BF16)
        w2 = w2c[...].astype(BF16)
        w1b[i] = w1
        w2b[i] = w2
        kb, qb = k.astype(BF16), q.astype(BF16)
        gap = v - k
        gap = gap - mean(gap)
        both = mm(jnp.concatenate([kb, qb], axis=0), w1, NN)
        x2, g1, gg1 = gelu_parts(both[:MB])
        x2b = x2.astype(BF16)
        c = mm(x2b, w2, NT)
        var = mean(c * c)
        cross = mean(gap * c)
        s = lax.rsqrt(var + EPSILON)
        n = c * s
        cc = var * s * s - s * cross
        r = n - gap
        g2 = s * (r - n * cc)
        g2b = g2.astype(BF16)
        p = mm(g2b, w2, NN)
        g1f = p * g1
        w1c[...] = w1c[...] - mm(k, e * g1f, TN)
        w2c[...] = w2c[...] - mm(e * g2, x2b, TN)
        g1b = g1f.astype(BF16)
        b1 = mm(qb, kb, NT)
        a1 = (b1 * mask).astype(BF16)
        zq = both[MB:] - mm(a1, g1b, NN)
        xq, gq = gelu_two(zq)
        xqb = xq.astype(BF16)
        b2 = mm(xqb, x2b, NT)
        a2 = (b2 * mask).astype(BF16)
        y = mm(xqb, w2, NT) - mm(a2, g2b, NN)
        sq = lax.rsqrt(mean(y * y) + EPSILON)
        nq = y * sq
        os[at, 3 * hd : 4 * hd] = (q + nq).astype(BF16)
        dy = sq * (d_o - mean(d_o) - nq * mean(d_o * nq))
        dyb = dy.astype(BF16)
        da2 = -mm(dyb, g2b, NT)
        db2 = (da2 * mask).astype(BF16)
        dg2s[i] = -mm(a2, dyb, TN)
        dxq = mm(dyb, w2, NN) + mm(db2, x2b, NN)
        dx2s[i] = mm(db2, xqb, TN)
        dzq = (dxq * gq).astype(BF16)
        da1 = -mm(dzq, g1b, NT)
        db1 = (da1 * mask).astype(BF16)
        dg1s[i] = -mm(a1, dzq, TN)
        dq = d_o + mm(dzq, w1, NT) + mm(db1, kb, NN)
        os[at, 0:hd] = dq.astype(BF16)
        dks[i] = mm(db1, qb, TN)
        de = jnp.sum(jnp.where(causal, da2 * b2 + da1 * b1, 0.0), axis=0, keepdims=True)
        des[i] = padded(jnp.broadcast_to(de, (8, MB)))
        x2s[i] = x2b
        g1s[i] = g1
        pgs[i] = p * gg1
        gfs[i] = g1f
        xqs[i] = xqb
        zqs[i] = dzq
        dys[i] = dyb
        ns[i] = n
        rs[i] = r
        ss[i] = jnp.broadcast_to(s, (MB, hd))
        cs[i] = jnp.broadcast_to(cc, (MB, hd))
        g2s[i] = g2

    def backward(i):
        at = at_block(i)
        q, k = qs[at, :], ks[at, :]
        e = to_column(es[i][0:1, 0:MB])
        w1, w2 = w1b[i], w2b[i]
        d1, d2 = w1c[...].astype(BF16), w2c[...].astype(BF16)
        x2b, g1, g1f, g2 = x2s[i], g1s[i], gfs[i], g2s[i]
        n, s, cc = ns[i], ss[i], cs[i]
        dh1 = -mm(k, d1, NN)
        dh2 = -mm(x2b, d2, NT)
        dg1 = dg1s[i] + e * dh1
        dp = (dg1 * g1).astype(BF16)
        dg2 = dg2s[i] + e * dh2 + mm(dp, w2, NT)
        dt = s * dg2
        mt = mean(dt * n)
        dr = dt - mean(dt) - n * mt
        dn = dr - cc * dt - rs[i] * mt
        du = s * (dn - mean(dn) - n * (mean(dn * n) + mean(dg2 * g2)))
        dub = du.astype(BF16)
        mixed = jnp.concatenate([(-e * g2).astype(BF16), dub], axis=1)
        dx2 = dx2s[i] + mm(mixed, jnp.concatenate([d2, w2], axis=0), NN)
        dz1 = (dg1 * pgs[i] + dx2 * g1).astype(BF16)
        mixed = jnp.concatenate([(-e * g1f).astype(BF16), dz1], axis=1)
        dk = dks[i] + dr + mm(mixed, jnp.concatenate([d1, w1], axis=1), NT)
        w1c[...] = w1c[...] + mm(
            jnp.concatenate([q, k], axis=0), jnp.concatenate([zqs[i], dz1], axis=0), TN
        )
        w2c[...] = w2c[...] + mm(
            jnp.concatenate([dys[i].astype(F32), du, g2], axis=0),
            jnp.concatenate([xqs[i], x2b, dp], axis=0),
            TN,
        )
        extra = jnp.sum(g1f * dh1, axis=1, keepdims=True) + jnp.sum(
            g2 * dh2, axis=1, keepdims=True
        )
        line = (des[i][0:1, 0:MB] + to_line(extra)) * sg[i][0:1, 0:MB]
        lg[i] = padded(jnp.broadcast_to(line, (8, MB)))
        os[at, hd : 2 * hd] = dk.astype(BF16)
        os[at, 2 * hd : 3 * hd] = (-dr).astype(BF16)

    def loop(step, order):
        if blocks <= UNROLL_LIMIT:
            for i in range(blocks):
                step(order(i))
        else:
            lax.fori_loop(0, blocks, lambda i, unused: (step(order(i)), unused)[1], 0)

    loop(forward, lambda i: i)
    w1c[...] = jnp.zeros_like(w1c)
    w2c[...] = jnp.zeros_like(w2c)
    loop(backward, lambda i: blocks - 1 - i)

    res_ref[0:rows, :] = os[pl.ds(pl.multiple_of(place * rows, rows), rows), :]
    res_ref[rows:, :] = jnp.zeros((EXTRA, width), BF16)
    first_row = lax.broadcasted_iota(jnp.int32, (EXTRA, rows), 0) == 0
    lines = jnp.concatenate([lg[place * per + b][0:1, 0:MB] for b in range(per)], axis=1)
    lines = jnp.where(first_row, jnp.broadcast_to(lines, (EXTRA, rows)), 0.0)
    res_ref[rows:, 0:rows] = lines.astype(BF16)

    part = dw_refs[0].shape[0]
    ws[:, 0:hd] = w1c[...].T
    ws[:, hd : 2 * hd] = w2c[...].T
    for d in range(dps):
        first = (place * dps + mate(place_ref[2], d, dps)) * part
        dw_refs[d][...] = ws[pl.ds(pl.multiple_of(first, part), part), :]


def output_kernel(seqs, heads, dps, share, place_ref, *refs):
    got_refs, refs = refs[:heads], refs[heads:]
    o_refs, w_refs = refs[: seqs * dps], refs[seqs * dps : 3 * seqs * dps]
    out_ref, dtok_ref, got, out_s, grad_s = refs[3 * seqs * dps :]
    hd = o_refs[0].shape[1]
    rows, features = out_ref.shape
    depth = features // share
    half = depth // 2
    for j in range(heads):
        got[mate(place_ref[1], j, heads)] = got_refs[j][...]
    out_s[...] = jnp.zeros_like(out_s)
    grad_s[...] = jnp.zeros_like(grad_s)
    for j in range(seqs):
        for d in range(dps):
            o = o_refs[j * dps + d]
            h, r = owner_of(place_ref, seqs, dps, share, j, d)
            out_s[r] = out_s[r] + mm(got[h, 0:rows, 3 * hd :], o[0:depth, :], NT)
            line = rate_line(o[depth:, :], depth)
            logit = got[h, rows:, 0:rows].astype(F32).T
            grad = [mm(logit, jnp.broadcast_to(line, (EXTRA, depth)), NN)]
            mine = got[h, 0:rows, 0 : 3 * hd]
            halves = []
            for part in range(2):
                w = w_refs[(part * seqs + j) * dps + d]
                wide = jnp.concatenate([w[c * half : (c + 1) * half, :] for c in range(3)], axis=1)
                halves.append(mm(mine, wide, NT))
            grad_s[r] = grad_s[r] + grad[0] + jnp.concatenate(halves, axis=1)
    for r in range(share):
        out_ref[:, r * depth : (r + 1) * depth] = out_s[r].astype(BF16)
        dtok_ref[:, r * depth : (r + 1) * depth] = grad_s[r].astype(BF16)


VMEM = pl.BlockSpec(memory_space=pltpu.VMEM)
SMEM = pl.BlockSpec(memory_space=pltpu.SMEM)
MIB = 1024 * 1024


def call(kernel, outs, operands, scratch=(), mib=16):
    return pl.pallas_call(
        kernel,
        out_shape=outs,
        in_specs=[SMEM] + [VMEM] * (len(operands) - 1),
        out_specs=jax.tree.map(lambda unused: VMEM, outs),
        scratch_shapes=list(scratch),
        compiler_params=pltpu.CompilerParams(vmem_limit_bytes=mib * MIB),
    )(*operands)


def body(tokens, w_qkv, w_lr, w_out, w1_init, w2_init, d_out):
    seqs, heads, dps = (lax.axis_size(a) for a in ("seq", "head", "dp"))
    share = seqs * dps // heads
    rows, features = tokens.shape[1:]
    depth, unused, hd = w_qkv.shape
    inner = w1_init.shape[2]
    blocks = seqs * rows // MB
    place = jnp.stack([lax.axis_index(a).astype(jnp.int32) for a in ("seq", "head", "dp")])
    sizes = (seqs, heads, dps, share)
    place, w_out, w_qkv = lax.optimization_barrier((place, w_out, w_qkv))

    pairs = []
    for seq in range(seqs):
        for head in range(heads):
            for dp in range(dps):
                k = seq * dps + dp
                target = head * share + k % share
                to = ((target // dps) * heads + k // share) * dps + target % dps
                pairs.append(((seq * heads + head) * dps + dp, to))

    def swapped(array):
        return lax.ppermute(array, ("seq", "head", "dp"), pairs)

    half = depth // 2
    lines = w_lr[:, 0].reshape(seqs * dps, depth // 128, 128)
    line = lax.dynamic_index_in_dim(
        lines, lax.axis_index("seq") * dps + lax.axis_index("dp"), 0, keepdims=False
    )
    line = jnp.pad(line, ((0, EXTRA - depth // 128), (0, 0)))
    by_kind = w_qkv.transpose(1, 0, 2)
    first, second, outer = lax.optimization_barrier(
        (
            by_kind[:, :half].reshape(3 * half, hd),
            by_kind[:, half:].reshape(3 * half, hd),
            jnp.concatenate([w_out, line], axis=0),
        )
    )
    outer_w, first_w, second_w = swapped(outer), swapped(first), swapped(second)
    outer_w, first_w = lax.optimization_barrier((outer_w, first_w))
    outer_near = peers_of(outer_w, "dp")
    first_near = [first_w, hop(first_w, "dp", 1), hop(first_w, "dp", 2)]
    second_near = [second_w, hop(second_w, "dp", 1), hop(second_w, "dp", 2)]
    outer_ws = over_seq(outer_near)
    def summed(arrays):
        return functools.reduce(lambda a, b: a + b, [a.astype(F32) for a in arrays])

    outer_part = call(
        functools.partial(outer_kernel, *sizes),
        (jax.ShapeDtypeStruct((rows + EXTRA, hd), BF16),) * heads,
        (place, tokens[0], d_out[0], *outer_ws),
        [pltpu.VMEM((share, rows, features // share), BF16)] * 2
        + [pltpu.VMEM((heads, rows + EXTRA, hd), F32)],
    )
    outer_all = peers_of(summed(sent_to(outer_part, "head")), "seq")
    if dps == 4:
        first_near.append(hop(first_near[1], "dp", 2))
        second_near.append(hop(second_near[2], "dp", 1))
    else:
        first_near += [hop(first_w, "dp", j) for j in range(3, dps)]
        second_near += [hop(second_w, "dp", j) for j in range(3, dps)]
    inner_ws = over_seq(first_near) + over_seq(second_near)
    later_place, unused = lax.optimization_barrier((place, outer_all[-1]))
    inner_part = call(
        functools.partial(inner_projection_kernel, *sizes),
        (jax.ShapeDtypeStruct((rows, 3 * hd), BF16),) * heads,
        (later_place, tokens[0], *inner_ws),
        [
            pltpu.VMEM((share, rows, features // share), BF16),
            pltpu.VMEM((heads, rows, 3 * hd), F32),
        ],
    )
    inner_all = peers_of(summed(sent_to(inner_part, "head")), "seq")

    long = seqs * rows
    scratch = (
        [pltpu.VMEM((long, hd), F32)] * 4
        + [pltpu.VMEM((blocks, 8, 2 * MB), F32)] * 2
        + [pltpu.VMEM((long, 4 * hd), BF16), pltpu.VMEM((blocks, 8, 2 * MB), F32)]
        + [pltpu.VMEM((hd, inner), F32)] * 2
        + [pltpu.VMEM((blocks, hd, inner), BF16)] * 2
        + [pltpu.VMEM((blocks, MB, inner), t) for t in (BF16, F32, F32, F32, BF16, BF16, F32, F32)]
        + [pltpu.VMEM((blocks, MB, hd), t) for t in (BF16, F32, F32, F32, F32, F32, F32, F32)]
        + [pltpu.VMEM((blocks, 8, 2 * MB), F32), pltpu.VMEM((inner, 2 * hd), F32)]
    )
    part = inner // (seqs * dps)
    result, *d_inner = call(
        functools.partial(inner_kernel, seqs, dps),
        (jax.ShapeDtypeStruct((rows + EXTRA, 4 * hd), BF16),)
        + (jax.ShapeDtypeStruct((part, 2 * hd), F32),) * dps,
        (place, *inner_all, *outer_all, w1_init[0], w2_init[0]),
        scratch,
        14 + 2 * blocks,
    )
    got = peers_of(result, "head")
    unused, *d_inner = lax.optimization_barrier((got[1], *d_inner))
    shares = summed(sent_to(d_inner, "dp"))
    out, d_tokens = call(
        functools.partial(output_kernel, *sizes),
        (jax.ShapeDtypeStruct((rows, features), BF16),) * 2,
        (place, *got, *outer_ws, *inner_ws),
        [
            pltpu.VMEM((heads, rows + EXTRA, 4 * hd), BF16),
            pltpu.VMEM((share, rows, features // share), F32),
            pltpu.VMEM((share, rows, features // share), F32),
        ],
    )
    return (out[None], d_tokens[None], shares[:, :hd].transpose(1, 0)[None], shares[:, hd:][None])


def solution(mesh):
    placed = (
        P("dp", "seq", "head"),
        P(("seq", "dp"), None, "head"),
        P(None, "head"),
        P(("seq", "dp"), "head"),
        P("head", None, None),
        P("head", None, None),
        P("dp", "seq", "head"),
    )
    return jax.shard_map(
        body,
        mesh=mesh,
        in_specs=placed,
        out_specs=(
            P("dp", "seq", "head"),
            P("dp", "seq", "head"),
            P("head", None, ("seq", "dp")),
            P("head", ("seq", "dp"), None),
        ),
        check_vma=False,
    )
```

```python
import functools

import jax
import jax.numpy as jnp
from jax import lax
from jax.experimental import pallas as pl
from jax.experimental.pallas import tpu as pltpu
from jax.sharding import PartitionSpec as P

MB = 64
EPSILON = 1e-06
BASE_RATE = 0.1
GELU_SCALE = 0.7978845608028654
GELU_CUBIC = 0.044715
NN = ((1,), (0,))
NT = ((1,), (1,))
TN = ((0,), (0,))
EXTRA = 16
UNROLL_LIMIT = 8
F32 = jnp.float32
BF16 = jnp.bfloat16


def mm(left, right, dims):
    return lax.dot_general(
        left.astype(BF16), right.astype(BF16), (dims, ((), ())), preferred_element_type=F32
    )


def padded(lines):
    return jnp.concatenate([lines, jnp.zeros_like(lines)], axis=1)


def mean(rows):
    return jnp.mean(rows, axis=-1, keepdims=True)


def gelu_parts(v):
    square = v * v
    bend = jnp.tanh(v * (GELU_SCALE + (GELU_SCALE * GELU_CUBIC) * square))
    half = 0.5 + 0.5 * bend
    slope = GELU_SCALE + (3.0 * GELU_SCALE * GELU_CUBIC) * square
    bell = 0.5 - 0.5 * bend * bend
    lean = bell * slope
    second = 2.0 * lean * (1.0 - v * bend * slope) + (6.0 * GELU_SCALE * GELU_CUBIC) * square * bell
    return v * half, half + v * lean, second


def gelu_two(v):
    square = v * v
    bend = jnp.tanh(v * (GELU_SCALE + (GELU_SCALE * GELU_CUBIC) * square))
    half = 0.5 + 0.5 * bend
    slope = GELU_SCALE + (3.0 * GELU_SCALE * GELU_CUBIC) * square
    return v * half, half + v * ((0.5 - 0.5 * bend * bend) * slope)


def mate(index, step, count):
    if count & (count - 1) == 0:
        return index ^ step
    return (index + step) % count


def hop(array, axis, step):
    count = lax.axis_size(axis)
    return lax.ppermute(array, axis, [(mate(i, step, count), i) for i in range(count)])


def peers_of(array, axis):
    return [array] + [hop(array, axis, j) for j in range(1, lax.axis_size(axis))]


def sent_to(arrays, axis):
    count = lax.axis_size(axis)
    back = [arrays[0]]
    for j in range(1, count):
        back.append(lax.ppermute(arrays[j], axis, [(i, mate(i, j, count)) for i in range(count)]))
    return back


def over_seq(near):
    return sum([list(pieces) for pieces in zip(*[peers_of(piece, "seq") for piece in near])], [])


def owner_of(place_ref, seqs, dps, share, j, d):
    seq, dp = place_ref[0], place_ref[2]
    k = mate(seq, j, seqs) * dps + mate(dp, d, dps)
    return k // share, k % share


def rate_line(block, depth):
    rows = block.astype(F32)
    return jnp.concatenate([rows[i : i + 1, :] for i in range(depth // 128)], axis=1)


def outer_kernel(seqs, heads, dps, share, place_ref, tok_ref, dout_ref, *refs):
    w_refs = refs[: seqs * dps]
    out_refs = refs[seqs * dps : seqs * dps + heads]
    tok_s, dout_s, acc = refs[seqs * dps + heads :]
    rows, features = tok_ref.shape
    depth = features // share
    for r in range(share):
        tok_s[r] = tok_ref[:, r * depth : (r + 1) * depth]
        dout_s[r] = dout_ref[:, r * depth : (r + 1) * depth]
    acc[...] = jnp.zeros_like(acc)
    for j in range(seqs):
        for d in range(dps):
            w = w_refs[j * dps + d]
            h, r = owner_of(place_ref, seqs, dps, share, j, d)
            line = rate_line(w[depth:, :], depth)
            logit = mm(jnp.broadcast_to(line, (EXTRA, depth)), tok_s[r], NT)
            back = mm(dout_s[r], w[0:depth, :], NN)
            acc[h] = acc[h] + jnp.concatenate([back, logit], axis=0)
    first_half = lax.broadcasted_iota(jnp.int32, (EXTRA, rows), 0) < EXTRA // 2
    for j in range(heads):
        total = acc[mate(place_ref[1], j, heads)]
        out_refs[j][0:rows, :] = total[0:rows].astype(BF16)
        logit = total[rows:]
        high = logit.astype(BF16).astype(F32)
        out_refs[j][rows:, :] = jnp.where(first_half, high, logit - high).astype(BF16)


def inner_projection_kernel(seqs, heads, dps, share, place_ref, tok_ref, *refs):
    w_refs = refs[: 2 * seqs * dps]
    out_refs = refs[2 * seqs * dps : 2 * seqs * dps + heads]
    tok_s, acc = refs[2 * seqs * dps + heads :]
    rows, features = tok_ref.shape
    depth = features // share
    half = depth // 2
    for r in range(share):
        tok_s[r] = tok_ref[:, r * depth : (r + 1) * depth]
    acc[...] = jnp.zeros_like(acc)
    for part in range(2):
        for j in range(seqs):
            for d in range(dps):
                w = w_refs[(part * seqs + j) * dps + d]
                h, r = owner_of(place_ref, seqs, dps, share, j, d)
                wide = jnp.concatenate([w[c * half : (c + 1) * half, :] for c in range(3)], axis=1)
                acc[h] = acc[h] + mm(tok_s[r][:, part * half : (part + 1) * half], wide, NN)
    for j in range(heads):
        out_refs[j][...] = acc[mate(place_ref[1], j, heads)].astype(BF16)


def inner_kernel(seqs, dps, place_ref, *refs):
    x_refs, y_refs = refs[:seqs], refs[seqs : 2 * seqs]
    w1_ref, w2_ref, res_ref = refs[2 * seqs : 2 * seqs + 3]
    dw_refs = refs[2 * seqs + 3 : 2 * seqs + 3 + dps]
    (
        qs, ks, vs, ds, es, sg, os, lg,
        w1c, w2c, w1b, w2b,
        x2s, g1s, pgs, gfs, xqs, zqs, dx2s, dg1s,
        dys, ns, rs, ss, cs, g2s, dg2s, dks, des, ws,
    ) = refs[2 * seqs + 3 + dps :]
    rows = x_refs[0].shape[0]
    hd = y_refs[0].shape[1]
    width = 4 * hd
    blocks = seqs * rows // MB
    per = rows // MB
    place = place_ref[0]

    for j in range(seqs):
        owner = mate(place, j, seqs)
        at = pl.ds(pl.multiple_of(owner * rows, rows), rows)
        qs[at, :] = x_refs[j][:, 0:hd]
        ks[at, :] = x_refs[j][:, hd : 2 * hd]
        vs[at, :] = x_refs[j][:, 2 * hd : 3 * hd]
        ds[at, :] = y_refs[j][0:rows, :]
        logit = y_refs[j][rows : rows + 8, :] + y_refs[j][rows + 8 : rows + 16, :]
        gate = jax.nn.sigmoid(logit)
        scaled = (BASE_RATE / hd) * gate
        for b in range(per):
            es[owner * per + b] = padded(scaled[:, b * MB : (b + 1) * MB])
            sg[owner * per + b] = padded((scaled * (1.0 - gate))[:, b * MB : (b + 1) * MB])

    w1c[...] = w1_ref[...]
    start = w2_ref[...]
    w2c[...] = (start - mean(start)).T

    at_row = lax.broadcasted_iota(jnp.int32, (MB, MB), 0)
    at_col = lax.broadcasted_iota(jnp.int32, (MB, MB), 1)
    causal = at_col <= at_row
    diagonal = at_col == at_row

    def to_column(line):
        return jnp.sum(jnp.where(diagonal, line, 0.0), axis=1, keepdims=True)

    def to_line(column):
        return jnp.sum(jnp.where(diagonal, column, 0.0), axis=0, keepdims=True)

    def at_block(i):
        if isinstance(i, int):
            return slice(i * MB, (i + 1) * MB)
        return pl.ds(pl.multiple_of(i * MB, MB), MB)

    def is_last(i):
        return isinstance(i, int) and i == blocks - 1

    def forward(i):
        at = at_block(i)
        q, k, v, d_o = qs[at, :], ks[at, :], vs[at, :], ds[at, :]
        line = es[i][0:1, 0:MB]
        e = to_column(line)
        mask = jnp.where(causal, line, 0.0)
        w1 = w1c[...].astype(BF16)
        w2 = w2c[...].astype(BF16)
        w1b[i] = w1
        w2b[i] = w2
        kb, qb = k.astype(BF16), q.astype(BF16)
        gap = v - k
        gap = gap - mean(gap)
        both = mm(jnp.concatenate([kb, qb], axis=0), w1, NN)
        x2, g1, gg1 = gelu_parts(both[:MB])
        x2b = x2.astype(BF16)
        c = mm(x2b, w2, NT)
        var = mean(c * c)
        cross = mean(gap * c)
        s = lax.rsqrt(var + EPSILON)
        n = c * s
        cc = var * s * s - s * cross
        r = n - gap
        g2 = s * (r - n * cc)
        g2b = g2.astype(BF16)
        p = mm(g2b, w2, NN)
        g1f = p * g1
        if not is_last(i):
            w1c[...] = w1c[...] - mm(k, e * g1f, TN)
            w2c[...] = w2c[...] - mm(e * g2, x2b, TN)
        g1b = g1f.astype(BF16)
        b1 = mm(qb, kb, NT)
        a1 = (b1 * mask).astype(BF16)
        zq = both[MB:] - mm(a1, g1b, NN)
        xq, gq = gelu_two(zq)
        xqb = xq.astype(BF16)
        b2 = mm(xqb, x2b, NT)
        a2 = (b2 * mask).astype(BF16)
        y = mm(xqb, w2, NT) - mm(a2, g2b, NN)
        sq = lax.rsqrt(mean(y * y) + EPSILON)
        nq = y * sq
        os[at, 3 * hd : 4 * hd] = (q + nq).astype(BF16)
        dy = sq * (d_o - mean(d_o) - nq * mean(d_o * nq))
        dyb = dy.astype(BF16)
        da2 = -mm(dyb, g2b, NT)
        db2 = (da2 * mask).astype(BF16)
        dg2s[i] = -mm(a2, dyb, TN)
        dxq = mm(dyb, w2, NN) + mm(db2, x2b, NN)
        dx2s[i] = mm(db2, xqb, TN)
        dzq = (dxq * gq).astype(BF16)
        da1 = -mm(dzq, g1b, NT)
        db1 = (da1 * mask).astype(BF16)
        dg1s[i] = -mm(a1, dzq, TN)
        dq = d_o + mm(dzq, w1, NT) + mm(db1, kb, NN)
        os[at, 0:hd] = dq.astype(BF16)
        dks[i] = mm(db1, qb, TN)
        de = jnp.sum(jnp.where(causal, da2 * b2 + da1 * b1, 0.0), axis=0, keepdims=True)
        des[i] = padded(jnp.broadcast_to(de, (8, MB)))
        x2s[i] = x2b
        g1s[i] = g1
        pgs[i] = p * gg1
        gfs[i] = g1f
        xqs[i] = xqb
        zqs[i] = dzq
        dys[i] = dyb
        ns[i] = n
        rs[i] = r
        ss[i] = jnp.broadcast_to(s, (MB, hd))
        cs[i] = jnp.broadcast_to(cc, (MB, hd))
        g2s[i] = g2

    def backward(i):
        at = at_block(i)
        q, k = qs[at, :], ks[at, :]
        e = to_column(es[i][0:1, 0:MB])
        w1, w2 = w1b[i], w2b[i]
        d1, d2 = w1c[...].astype(BF16), w2c[...].astype(BF16)
        x2b, g1, g1f, g2 = x2s[i], g1s[i], gfs[i], g2s[i]
        n, s, cc = ns[i], ss[i], cs[i]
        last = is_last(i)
        dh1 = jnp.zeros_like(g1f) if last else -mm(k, d1, NN)
        dh2 = jnp.zeros_like(g2) if last else -mm(x2b, d2, NT)
        dg1 = dg1s[i] + e * dh1
        dp = (dg1 * g1).astype(BF16)
        dg2 = dg2s[i] + e * dh2 + mm(dp, w2, NT)
        dt = s * dg2
        mt = mean(dt * n)
        dr = dt - mean(dt) - n * mt
        dn = dr - cc * dt - rs[i] * mt
        du = s * (dn - mean(dn) - n * (mean(dn * n) + mean(dg2 * g2)))
        dub = du.astype(BF16)
        if last:
            dx2 = dx2s[i] + mm(dub, w2, NN)
        else:
            mixed = jnp.concatenate([(-e * g2).astype(BF16), dub], axis=1)
            dx2 = dx2s[i] + mm(mixed, jnp.concatenate([d2, w2], axis=0), NN)
        dz1 = (dg1 * pgs[i] + dx2 * g1).astype(BF16)
        if last:
            dk = dks[i] + dr + mm(dz1, w1, NT)
        else:
            mixed = jnp.concatenate([(-e * g1f).astype(BF16), dz1], axis=1)
            dk = dks[i] + dr + mm(mixed, jnp.concatenate([d1, w1], axis=1), NT)
        w1c[...] = w1c[...] + mm(
            jnp.concatenate([q, k], axis=0), jnp.concatenate([zqs[i], dz1], axis=0), TN
        )
        w2c[...] = w2c[...] + mm(
            jnp.concatenate([dys[i].astype(F32), du, g2], axis=0),
            jnp.concatenate([xqs[i], x2b, dp], axis=0),
            TN,
        )
        extra = jnp.sum(g1f * dh1, axis=1, keepdims=True) + jnp.sum(
            g2 * dh2, axis=1, keepdims=True
        )
        line = (des[i][0:1, 0:MB] + to_line(extra)) * sg[i][0:1, 0:MB]
        lg[i] = padded(jnp.broadcast_to(line, (8, MB)))
        os[at, hd : 2 * hd] = dk.astype(BF16)
        os[at, 2 * hd : 3 * hd] = (-dr).astype(BF16)

    def loop(step, order):
        if blocks <= UNROLL_LIMIT:
            for i in range(blocks):
                step(order(i))
        else:
            lax.fori_loop(0, blocks, lambda i, unused: (step(order(i)), unused)[1], 0)

    loop(forward, lambda i: i)
    w1c[...] = jnp.zeros_like(w1c)
    w2c[...] = jnp.zeros_like(w2c)
    loop(backward, lambda i: blocks - 1 - i)

    res_ref[0:rows, :] = os[pl.ds(pl.multiple_of(place * rows, rows), rows), :]
    res_ref[rows:, :] = jnp.zeros((EXTRA, width), BF16)
    first_row = lax.broadcasted_iota(jnp.int32, (EXTRA, rows), 0) == 0
    lines = jnp.concatenate([lg[place * per + b][0:1, 0:MB] for b in range(per)], axis=1)
    lines = jnp.where(first_row, jnp.broadcast_to(lines, (EXTRA, rows)), 0.0)
    res_ref[rows:, 0:rows] = lines.astype(BF16)

    part = dw_refs[0].shape[0]
    ws[:, 0:hd] = w1c[...].T
    ws[:, hd : 2 * hd] = w2c[...].T
    for d in range(dps):
        first = (place * dps + mate(place_ref[2], d, dps)) * part
        dw_refs[d][...] = ws[pl.ds(pl.multiple_of(first, part), part), :]


def output_kernel(seqs, heads, dps, share, place_ref, *refs):
    got_refs, refs = refs[:heads], refs[heads:]
    o_refs, w_refs = refs[: seqs * dps], refs[seqs * dps : 3 * seqs * dps]
    out_ref, dtok_ref, got, out_s, grad_s = refs[3 * seqs * dps :]
    hd = o_refs[0].shape[1]
    rows, features = out_ref.shape
    depth = features // share
    half = depth // 2
    for j in range(heads):
        got[mate(place_ref[1], j, heads)] = got_refs[j][...]
    out_s[...] = jnp.zeros_like(out_s)
    grad_s[...] = jnp.zeros_like(grad_s)
    for j in range(seqs):
        for d in range(dps):
            o = o_refs[j * dps + d]
            h, r = owner_of(place_ref, seqs, dps, share, j, d)
            out_s[r] = out_s[r] + mm(got[h, 0:rows, 3 * hd :], o[0:depth, :], NT)
            line = rate_line(o[depth:, :], depth)
            logit = got[h, rows:, 0:rows].astype(F32).T
            grad = [mm(logit, jnp.broadcast_to(line, (EXTRA, depth)), NN)]
            mine = got[h, 0:rows, 0 : 3 * hd]
            halves = []
            for part in range(2):
                w = w_refs[(part * seqs + j) * dps + d]
                wide = jnp.concatenate([w[c * half : (c + 1) * half, :] for c in range(3)], axis=1)
                halves.append(mm(mine, wide, NT))
            grad_s[r] = grad_s[r] + grad[0] + jnp.concatenate(halves, axis=1)
    for r in range(share):
        out_ref[:, r * depth : (r + 1) * depth] = out_s[r].astype(BF16)
        dtok_ref[:, r * depth : (r + 1) * depth] = grad_s[r].astype(BF16)


VMEM = pl.BlockSpec(memory_space=pltpu.VMEM)
SMEM = pl.BlockSpec(memory_space=pltpu.SMEM)
MIB = 1024 * 1024


def call(kernel, outs, operands, scratch=(), mib=16):
    return pl.pallas_call(
        kernel,
        out_shape=outs,
        in_specs=[SMEM] + [VMEM] * (len(operands) - 1),
        out_specs=jax.tree.map(lambda unused: VMEM, outs),
        scratch_shapes=list(scratch),
        compiler_params=pltpu.CompilerParams(vmem_limit_bytes=mib * MIB),
    )(*operands)


def body(tokens, w_qkv, w_lr, w_out, w1_init, w2_init, d_out):
    seqs, heads, dps = (lax.axis_size(a) for a in ("seq", "head", "dp"))
    share = seqs * dps // heads
    rows, features = tokens.shape[1:]
    depth, unused, hd = w_qkv.shape
    inner = w1_init.shape[2]
    blocks = seqs * rows // MB
    place = jnp.stack([lax.axis_index(a).astype(jnp.int32) for a in ("seq", "head", "dp")])
    sizes = (seqs, heads, dps, share)
    place, w_out, w_qkv = lax.optimization_barrier((place, w_out, w_qkv))

    pairs = []
    for seq in range(seqs):
        for head in range(heads):
            for dp in range(dps):
                k = seq * dps + dp
                target = head * share + k % share
                to = ((target // dps) * heads + k // share) * dps + target % dps
                pairs.append(((seq * heads + head) * dps + dp, to))

    def swapped(array):
        return lax.ppermute(array, ("seq", "head", "dp"), pairs)

    half = depth // 2
    lines = w_lr[:, 0].reshape(seqs * dps, depth // 128, 128)
    line = lax.dynamic_index_in_dim(
        lines, lax.axis_index("seq") * dps + lax.axis_index("dp"), 0, keepdims=False
    )
    line = jnp.pad(line, ((0, EXTRA - depth // 128), (0, 0)))
    by_kind = w_qkv.transpose(1, 0, 2)
    first, second, outer = lax.optimization_barrier(
        (
            by_kind[:, :half].reshape(3 * half, hd),
            by_kind[:, half:].reshape(3 * half, hd),
            jnp.concatenate([w_out, line], axis=0),
        )
    )
    outer_w, first_w, second_w = swapped(outer), swapped(first), swapped(second)
    outer_near = peers_of(outer_w, "dp")
    first_near = [first_w, hop(first_w, "dp", 1), hop(first_w, "dp", 2)]
    second_near = [second_w, hop(second_w, "dp", 1), hop(second_w, "dp", 2)]
    outer_ws = over_seq(outer_near)
    def summed(arrays):
        return functools.reduce(lambda a, b: a + b, [a.astype(F32) for a in arrays])

    outer_part = call(
        functools.partial(outer_kernel, *sizes),
        (jax.ShapeDtypeStruct((rows + EXTRA, hd), BF16),) * heads,
        (place, tokens[0], d_out[0], *outer_ws),
        [pltpu.VMEM((share, rows, features // share), BF16)] * 2
        + [pltpu.VMEM((heads, rows + EXTRA, hd), F32)],
    )
    outer_all = peers_of(summed(sent_to(outer_part, "head")), "seq")
    if dps == 4:
        first_near.append(hop(first_near[1], "dp", 2))
        second_near.append(hop(second_near[2], "dp", 1))
    else:
        first_near += [hop(first_w, "dp", j) for j in range(3, dps)]
        second_near += [hop(second_w, "dp", j) for j in range(3, dps)]
    inner_ws = over_seq(first_near) + over_seq(second_near)
    later_place, unused = lax.optimization_barrier((place, outer_all[-1]))
    inner_part = call(
        functools.partial(inner_projection_kernel, *sizes),
        (jax.ShapeDtypeStruct((rows, 3 * hd), BF16),) * heads,
        (later_place, tokens[0], *inner_ws),
        [
            pltpu.VMEM((share, rows, features // share), BF16),
            pltpu.VMEM((heads, rows, 3 * hd), F32),
        ],
    )
    inner_all = peers_of(summed(sent_to(inner_part, "head")), "seq")

    long = seqs * rows
    scratch = (
        [pltpu.VMEM((long, hd), F32)] * 4
        + [pltpu.VMEM((blocks, 8, 2 * MB), F32)] * 2
        + [pltpu.VMEM((long, 4 * hd), BF16), pltpu.VMEM((blocks, 8, 2 * MB), F32)]
        + [pltpu.VMEM((hd, inner), F32)] * 2
        + [pltpu.VMEM((blocks, hd, inner), BF16)] * 2
        + [pltpu.VMEM((blocks, MB, inner), t) for t in (BF16, F32, F32, F32, BF16, BF16, F32, F32)]
        + [pltpu.VMEM((blocks, MB, hd), t) for t in (BF16, F32, F32, F32, F32, F32, F32, F32)]
        + [pltpu.VMEM((blocks, 8, 2 * MB), F32), pltpu.VMEM((inner, 2 * hd), F32)]
    )
    part = inner // (seqs * dps)
    result, *d_inner = call(
        functools.partial(inner_kernel, seqs, dps),
        (jax.ShapeDtypeStruct((rows + EXTRA, 4 * hd), BF16),)
        + (jax.ShapeDtypeStruct((part, 2 * hd), F32),) * dps,
        (place, *inner_all, *outer_all, w1_init[0], w2_init[0]),
        scratch,
        14 + 2 * blocks,
    )
    got = peers_of(result, "head")
    unused, *d_inner = lax.optimization_barrier((got[1], *d_inner))
    shares = summed(sent_to(d_inner, "dp"))
    out, d_tokens = call(
        functools.partial(output_kernel, *sizes),
        (jax.ShapeDtypeStruct((rows, features), BF16),) * 2,
        (place, *got, *outer_ws, *inner_ws),
        [
            pltpu.VMEM((heads, rows + EXTRA, 4 * hd), BF16),
            pltpu.VMEM((share, rows, features // share), F32),
            pltpu.VMEM((share, rows, features // share), F32),
        ],
    )
    return (out[None], d_tokens[None], shares[:, :hd].transpose(1, 0)[None], shares[:, hd:][None])


def solution(mesh):
    placed = (
        P("dp", "seq", "head"),
        P(("seq", "dp"), None, "head"),
        P(None, "head"),
        P(("seq", "dp"), "head"),
        P("head", None, None),
        P("head", None, None),
        P("dp", "seq", "head"),
    )
    return jax.shard_map(
        body,
        mesh=mesh,
        in_specs=placed,
        out_specs=(
            P("dp", "seq", "head"),
            P("dp", "seq", "head"),
            P("head", None, ("seq", "dp")),
            P("head", ("seq", "dp"), None),
        ),
        check_vma=False,
    )
```
